32 devices in a mesh: dp: 8 (over z, x), row: 2 (over y), col: 2 (over core).
Axes of the slice: x: 2, y: 2, z: 4, core: 2. Of those that a mesh axis runs over, the one named last changes fastest.
Arguments:
- inputs: bfloat16 [4096, 2048], P('dp', ('col', 'row')), may hold values from -6 to 6
- norm_gain: bfloat16 [2048], P(('col', 'row')), may hold values from 0.5 to 1.5
- norm_shift: bfloat16 [2048], P(('col', 'row')), may hold values from -3 to 3
- qkv_weight: bfloat16 [2048, 6144], P('col', 'row'), may hold values from -0.125 to 0.125
- qkv_bias: bfloat16 [6144], P(('row', 'col')), may hold values from -3 to 3
- up_weight: bfloat16 [2048, 8192], P('col', 'row')
- up_bias: bfloat16 [8192], P(('row', 'col')), may hold values from -3 to 3
- dense_weight: bfloat16 [2048, 2048], P('row', 'col'), may hold values from -0.75 to 0.75
- down_weight: bfloat16 [8192, 2048], P('row', 'col'), may hold values from -0.0625 to 0.0625
- out_bias: bfloat16 [2048], P(('col', 'row')), may hold values from -3 to 3
- cotangent: bfloat16 [4096, 2048], P('dp', ('col', 'row')), may hold values from -6 to 6
- seq_lengths: int32 [32], replicated, may hold values from 1 to 512, as said below
- seq_owner: int32 [32], replicated, may hold values from 0 to 7, as said below
Outputs:
- outputs: bfloat16 [4096, 2048], P('dp', ('col', 'row'))
- grad_inputs: float32 [4096, 2048], P('dp', ('col', 'row'))
- grad_norm_gain: float32 [2048], P(('col', 'row'))
- grad_norm_shift: float32 [2048], P(('col', 'row'))
- grad_qkv_weight: float32 [2048, 6144], P(('col', 'dp'), 'row')
- grad_qkv_bias: float32 [6144], P(('row', 'col'))
- grad_up_weight: float32 [2048, 8192], P(('col', 'dp'), 'row')
- grad_up_bias: float32 [8192], P(('row', 'col'))
- grad_dense_weight: float32 [2048, 2048], P(('row', 'dp'), 'col')
- grad_down_weight: float32 [8192, 2048], P(('row', 'dp'), 'col')
- grad_out_bias: float32 [2048], P(('col', 'row'))
The draws below stay inside these ranges and needn't reach their ends.
Inputs may be any that keep to these rules, and one draw needn't show every extreme that they name: `seq_lengths`: the lengths of the sequences held by one index of dp sum to at most 512; in every draw one sequence is 512 long and is the only one of its index. `seq_owner`: loads differ between indices of dp; an index may hold no sequence.
All inputs are finite; a program needn't handle non-finite values.
Results may differ from the reference program's by a relative error of at most 0.0097.
Values may be sent and summed in bfloat16 or wider, within the bound.
A program may use at most 256 MiB of HBM per device.

```python
import jax
import jax.numpy as jnp
from jax import lax

D = 2048
HEADS = 32
HEAD_DIM = 64
ROT = 32
FF = 8192
CAP = 512
TOKENS = 4096
SEQS = 32
N_DP = 8


def sequence_plan(key):
    owner_key, share_key, fill_key, pick_key = jax.random.split(key, 4)
    chosen = jax.random.randint(pick_key, (), 0, SEQS)
    lonely = jax.random.randint(jax.random.fold_in(pick_key, 1), (), 0, N_DP)
    raw_owner = jax.random.randint(owner_key, (SEQS,), 0, N_DP)
    moved = jnp.where(raw_owner == lonely, (lonely + 1) % N_DP, raw_owner)
    seq_index = jnp.arange(SEQS, dtype=jnp.int32)
    owners = jnp.where(seq_index == chosen, lonely, moved).astype(jnp.int32)
    shares = jax.random.randint(share_key, (SEQS,), 1, 9)
    fill_to = jax.random.randint(fill_key, (N_DP,), CAP // 2, CAP + 1)
    onehot = (owners[:, None] == jnp.arange(N_DP, dtype=jnp.int32)[None, :]).astype(jnp.int32)
    share_total = jnp.sum(onehot * shares[:, None], axis=0)
    counts_dev = jnp.sum(onehot, axis=0)
    spare_rows = fill_to - counts_dev
    owner_spare = jnp.sum(onehot * spare_rows[None, :], axis=1)
    owner_total = jnp.maximum(jnp.sum(onehot * share_total[None, :], axis=1), 1)
    lengths = 1 + shares * owner_spare // owner_total
    lengths = jnp.where(seq_index == chosen, CAP, lengths)
    return (owners, lengths.astype(jnp.int32))


def draw_seq_lengths(key, part):
    owners, lengths = sequence_plan(key)
    return lengths


def draw_seq_owner(key, part):
    owners, lengths = sequence_plan(key)
    return owners


def draw_up_weight(key, part):
    key = jax.random.fold_in(key, 3)
    base_key, column_key = jax.random.split(key)
    base = jnp.clip(jax.random.normal(base_key, (D, FF), jnp.float32), -6.0, 6.0)
    column = jnp.clip(jax.random.normal(column_key, (1, FF), jnp.float32), -3.0, 3.0)
    return ((base + 0.5 * column) * D ** (-0.5)).astype(jnp.bfloat16)


def level_of(key, shape, cuts, smallest, high):
    gain, own = 1.0, jax.random.fold_in(key, 6)
    for dim, parts in cuts:
        steps = jnp.exp(jax.random.uniform(jax.random.fold_in(own, dim), (parts,), jnp.float32, smallest / len(cuts), high / len(cuts)))
        gain = gain * jnp.repeat(steps, shape[dim] // parts).reshape([-1 if axis == dim else 1 for axis in range(len(shape))])
    return gain


def normal_values(stream_key, dims, scale, most, pieces=(), held_as=jnp.bfloat16):
    entries = scale * jax.random.normal(stream_key, dims, jnp.float32)
    if pieces:
        entries = entries * level_of(stream_key, dims, pieces, -0.22, 0.18)
    return jnp.clip(entries, -most, most).astype(held_as)


def setup_inputs(seed: int = 0) -> dict:
    seeds = jax.random.split(jax.random.key(seed), 14)
    inputs = normal_values(seeds[0], (TOKENS, D), 1.0, 6.0, ((0, 8), (1, 4)))
    norm_gain = jnp.clip(1.0 + 0.1 * jax.random.normal(seeds[1], (D,), jnp.float32), 0.5, 1.5).astype(jnp.bfloat16)
    norm_shift = normal_values(seeds[2], (D,), 0.5, 3.0, ((0, 4),))
    qkv_weight = normal_values(seeds[3], (D, 3 * D), D ** -0.5, 0.125, ((0, 2), (1, 2)))
    qkv_bias = normal_values(seeds[4], (3 * D,), 0.5, 3.0, ((0, 4),))
    up_weight = draw_up_weight(jax.random.fold_in(seeds[13], 71), 0)
    up_bias = normal_values(seeds[6], (FF,), 0.5, 3.0, ((0, 4),))
    dense_weight = normal_values(seeds[7], (D, D), (D // 32) ** -0.5, 0.75, ((0, 2), (1, 2)))
    down_weight = normal_values(seeds[8], (FF, D), FF ** -0.5, 0.0625, ((0, 2), (1, 2)))
    out_bias = normal_values(seeds[9], (D,), 0.5, 3.0, ((0, 4),))
    cotangent = normal_values(seeds[10], (TOKENS, D), 1.0, 6.0, ((0, 8), (1, 4)))
    seq_lengths = draw_seq_lengths(jax.random.fold_in(seeds[13], 71), 0)
    seq_owner = draw_seq_owner(jax.random.fold_in(seeds[13], 71), 0)
    return {"inputs": inputs, "norm_gain": norm_gain, "norm_shift": norm_shift, "qkv_weight": qkv_weight, "qkv_bias": qkv_bias, "up_weight": up_weight, "up_bias": up_bias, "dense_weight": dense_weight, "down_weight": down_weight, "out_bias": out_bias, "cotangent": cotangent, "seq_lengths": seq_lengths, "seq_owner": seq_owner}


@jax.custom_vjp
def low(v):
    return lax.optimization_barrier(v.astype(jnp.bfloat16)).astype(jnp.float32)

@jax.custom_vjp
def low_back(v):
    return v

def low_keep(v):
    return (low(v), None)

def low_pass(kept, grad):
    return (grad,)

def back_keep(v):
    return (v, None)

def back_low(kept, grad):
    return (low(grad),)
low.defvjp(low_keep, low_pass)
low_back.defvjp(back_keep, back_low)
epsilon = 1e-05
masked_score = -1e+30
rope_base = 10000.0
highest = lax.Precision.HIGHEST

def layout(seq_lengths, seq_owner, device, row_count):
    owned = seq_owner == device
    lengths_owned = jnp.where(owned, seq_lengths, 0).astype(jnp.int32)
    seq_ends = jnp.cumsum(lengths_owned, dtype=jnp.int32)
    seq_starts = seq_ends - lengths_owned
    slot_index = jnp.arange(row_count, dtype=jnp.int32)
    segment = lax.optimization_barrier(jnp.sum((seq_ends[None, :] <= slot_index[:, None]).astype(jnp.int32), axis=1))
    picked = jnp.arange(seq_lengths.shape[0], dtype=jnp.int32)[None, :] == segment[:, None]
    seq_begin = lax.optimization_barrier(jnp.sum(jnp.where(picked, seq_starts[None, :], 0), axis=1)).astype(jnp.int32)
    position = slot_index - seq_begin
    is_valid = slot_index < seq_ends[-1]
    return (segment, position, is_valid)

def angles(position):
    index_range = jnp.arange(ROT // 2, dtype=jnp.float32)
    frequency = rope_base ** (-2.0 * index_range / ROT)
    phase = position.astype(jnp.float32)[:, None] * frequency[None, :]
    return (jnp.cos(phase)[:, None, :], jnp.sin(phase)[:, None, :])

def rotate(field, cosines, sines):
    half_rot = cosines.shape[-1]
    first_part = field[..., :half_rot]
    second_part = field[..., half_rot:2 * half_rot]
    return jnp.concatenate([first_part * cosines - second_part * sines, second_part * cosines + first_part * sines, field[..., 2 * half_rot:]], axis=-1)

def block_layer(rows_in, segment, position, valid_rows, norm_gain, norm_shift, qkv_weight, qkv_bias, up_weight, up_bias, dense_weight, down_weight, out_bias):
    average = lax.optimization_barrier(jnp.mean(rows_in, axis=-1, keepdims=True))
    square_mean = lax.optimization_barrier(jnp.mean(rows_in * rows_in, axis=-1, keepdims=True))
    scale_inv = lax.rsqrt(square_mean - average * average + epsilon)
    normed = (rows_in - average) * scale_inv
    hidden = low(normed * norm_gain + norm_shift)
    projected = low_back(jnp.dot(hidden, qkv_weight, precision=highest) + qkv_bias)
    before = low_back(jnp.dot(hidden, up_weight, precision=highest) + up_bias)
    activated = low(jax.nn.gelu(before, approximate=True))
    grouped = projected.reshape(CAP, HEADS, 3, HEAD_DIM)
    cosines, sines = angles(position)
    queries = low(rotate(grouped[:, :, 0], cosines, sines))
    key_rows = low(rotate(grouped[:, :, 1], cosines, sines))
    values = low(grouped[:, :, 2])
    scores = jnp.einsum('qhd,khd->hqk', queries, key_rows, precision=highest) * HEAD_DIM ** (-0.5)
    scores = low_back(scores)
    slot_index = jnp.arange(CAP, dtype=jnp.int32)
    allowed = (segment[:, None] == segment[None, :]) & (slot_index[None, :] <= slot_index[:, None])
    scores = jnp.where(allowed[None], scores, masked_score)
    row_max = lax.optimization_barrier(jnp.max(scores, axis=-1, keepdims=True))
    weights = jnp.exp(scores - row_max)
    probabilities = weights / lax.optimization_barrier(jnp.sum(weights, axis=-1, keepdims=True))
    mixed_heads = jnp.einsum('hqk,khd->qhd', low(probabilities), values, precision=highest)
    attended = low(low_back(mixed_heads.reshape(CAP, D)))
    branch = jnp.dot(attended, dense_weight, precision=highest) + jnp.dot(activated, down_weight, precision=highest) + out_bias
    return rows_in + valid_rows[:, None] * branch

def reference(inputs, norm_gain, norm_shift, qkv_weight, qkv_bias, up_weight, up_bias, dense_weight, down_weight, out_bias, cotangent, seq_lengths, seq_owner):
    devices_range = jnp.arange(N_DP, dtype=jnp.int32)
    segment, position, is_valid = jax.vmap(lambda device: layout(seq_lengths, seq_owner, device, CAP))(devices_range)
    valid_rows = is_valid.astype(jnp.float32)

    def forward(rows_all, gain_in, shift_in, qkv_in, qkv_bias_in, up_in, up_bias_in, dense_in, down_in, out_bias_in):

        def one_block(packed):
            return block_layer(packed[0], packed[1], packed[2], packed[3], gain_in, shift_in, qkv_in, qkv_bias_in, up_in, up_bias_in, dense_in, down_in, out_bias_in)
        blocks = rows_all.reshape(N_DP, CAP, D)
        result = lax.map(jax.checkpoint(one_block), (blocks, segment, position, valid_rows))
        return result.reshape(TOKENS, D)
    floats = tuple((item.astype(jnp.float32) for item in (inputs, norm_gain, norm_shift, qkv_weight, qkv_bias, up_weight, up_bias, dense_weight, down_weight, out_bias)))
    result, pullback = jax.vjp(forward, *floats)
    gradients = pullback(cotangent.astype(jnp.float32))
    return (result.astype(jnp.bfloat16), gradients[0], gradients[1], gradients[2], gradients[3], gradients[4], gradients[5], gradients[6], gradients[7], gradients[8], gradients[9])
```

```python
from functools import partial

import jax
import jax.numpy as jnp
from jax import lax
from jax.experimental import pallas as pl
from jax.experimental.pallas import tpu as pltpu
from jax.sharding import PartitionSpec as P

HEAD_DIM = 64
ROT = 32
HALF_ROT = ROT // 2
PAIR = 2 * HEAD_DIM
PAIR_QKV = 3 * PAIR

epsilon = 1e-05
masked_score = -1e30
rope_base = 10000.0
score_scale = HEAD_DIM ** (-0.5)
bf16 = jnp.bfloat16
f32 = jnp.float32


def layout(seq_lengths, seq_owner, device, row_count):
    owned = seq_owner == device
    lengths_owned = jnp.where(owned, seq_lengths, 0)
    seq_ends = jnp.cumsum(lengths_owned, dtype=jnp.int32)
    seq_starts = seq_ends - lengths_owned
    slot_index = jnp.arange(row_count, dtype=jnp.int32)
    segment = jnp.sum((seq_ends[None, :] <= slot_index[:, None]).astype(jnp.int32), axis=1)
    picked = jnp.arange(seq_lengths.shape[0], dtype=jnp.int32)[None, :] == segment[:, None]
    seq_begin = jnp.sum(jnp.where(picked, seq_starts[None, :], 0), axis=1)
    position = slot_index - seq_begin
    is_valid = slot_index < seq_ends[-1]
    return (segment, position, is_valid)


def rotation_tables(position):
    index_range = jnp.arange(HALF_ROT, dtype=f32)
    frequency = rope_base ** (-2.0 * index_range / ROT)
    phase = position.astype(f32)[:, None] * frequency[None, :]
    cosines, sines = jnp.cos(phase), jnp.sin(phase)
    rows = position.shape[0]
    ones = jnp.ones((rows, HEAD_DIM - ROT), f32)
    none = jnp.zeros((rows, HALF_ROT), f32)
    rest = jnp.zeros((rows, HEAD_DIM - ROT), f32)
    same = jnp.concatenate([cosines, cosines, ones], axis=1)
    from_right = jnp.concatenate([sines, none, rest], axis=1)
    from_left = jnp.concatenate([none, sines, rest], axis=1)
    return jnp.stack([same, from_right, from_left])


def attention_kernel(proj_ref, mixed_ref, tables_ref, seg_col_ref, seg_row_ref, attended_ref, grad_ref):
    rows = proj_ref.shape[0]
    block = min(256, rows)
    same, from_right, from_left = tables_ref[0], tables_ref[1], tables_ref[2]

    def rotate(part, sign):
        right = jnp.concatenate([part[:, HALF_ROT:], part[:, :HALF_ROT]], axis=1)
        left = jnp.concatenate([part[:, HEAD_DIM - HALF_ROT :], part[:, : HEAD_DIM - HALF_ROT]], axis=1)
        return part * same - sign * (right * from_right) + sign * (left * from_left)

    def dot(left, right, dims):
        return lax.dot_general(left, right, (dims, ((), ())), preferred_element_type=f32)

    attended_heads, grads = [], []
    for head in range(2):
        base = head * 3 * HEAD_DIM
        queries = rotate(proj_ref[:, base : base + HEAD_DIM], 1.0).astype(bf16)
        keys = rotate(proj_ref[:, base + HEAD_DIM : base + 2 * HEAD_DIM], 1.0).astype(bf16)
        values = proj_ref[:, base + 2 * HEAD_DIM : base + 3 * HEAD_DIM].astype(bf16)
        mixed = mixed_ref[:, head * HEAD_DIM : (head + 1) * HEAD_DIM]
        outs, d_queries, d_keys, d_values = [], [], None, None
        for first in range(0, rows, block):
            last = first + block
            q, d_out = queries[first:last], mixed[first:last]
            k, v = keys[:last], values[:last]
            row_index = first + lax.broadcasted_iota(jnp.int32, (block, last), 0)
            key_index = lax.broadcasted_iota(jnp.int32, (block, last), 1)
            allowed = (seg_col_ref[first:last, :] == seg_row_ref[:, :last]) & (key_index <= row_index)
            scores = jnp.where(allowed, dot(q, k, ((1,), (1,))) * score_scale, masked_score)
            weights = jnp.exp(scores - jnp.max(scores, axis=1, keepdims=True))
            probs = weights * (1.0 / jnp.sum(weights, axis=1, keepdims=True))
            probs_low = probs.astype(bf16)
            outs.append(dot(probs_low, v, ((1,), (0,))))
            d_probs = dot(d_out, v, ((1,), (1,)))
            row_dot = jnp.sum(probs * d_probs, axis=1, keepdims=True)
            d_scores = (probs * (d_probs - row_dot)).astype(bf16)
            d_queries.append(dot(d_scores, k, ((1,), (0,))))
            key_part = dot(d_scores, q, ((0,), (0,)))
            value_part = dot(probs_low, d_out, ((0,), (0,)))
            if d_keys is None:
                d_keys, d_values = key_part, value_part
            else:
                d_keys = jnp.concatenate([key_part[:first] + d_keys, key_part[first:]], axis=0)
                d_values = jnp.concatenate([value_part[:first] + d_values, value_part[first:]], axis=0)
        attended_heads.append(jnp.concatenate(outs, axis=0))
        grads.append(rotate(jnp.concatenate(d_queries, axis=0) * score_scale, -1.0))
        grads.append(rotate(d_keys * score_scale, -1.0))
        grads.append(d_values)
    attended_ref[...] = jnp.concatenate(attended_heads, axis=1).astype(bf16)
    grad_ref[...] = jnp.concatenate(grads, axis=1).astype(bf16)


def attention(projected, mixed, tables, segment):
    rows, width = projected.shape
    pairs = width // PAIR_QKV
    return pl.pallas_call(
        attention_kernel,
        grid=(pairs,),
        in_specs=[
            pl.BlockSpec((rows, PAIR_QKV), lambda i: (0, i)),
            pl.BlockSpec((rows, PAIR), lambda i: (0, i)),
            pl.BlockSpec((3, rows, HEAD_DIM), lambda i: (0, 0, 0)),
            pl.BlockSpec((rows, 1), lambda i: (0, 0)),
            pl.BlockSpec((1, rows), lambda i: (0, 0)),
        ],
        out_specs=[
            pl.BlockSpec((rows, PAIR), lambda i: (0, i)),
            pl.BlockSpec((rows, PAIR_QKV), lambda i: (0, i)),
        ],
        out_shape=[
            jax.ShapeDtypeStruct((rows, pairs * PAIR), bf16),
            jax.ShapeDtypeStruct((rows, width), bf16),
        ],
        compiler_params=pltpu.CompilerParams(vmem_limit_bytes=48 * 1024 * 1024),
        cost_estimate=pl.CostEstimate(
            flops=14 * 2 * pairs * rows * rows * HEAD_DIM * 2,
            bytes_accessed=rows * width * 7,
            transcendentals=2 * pairs * rows * rows,
        ),
        name="attention",
    )(projected, mixed, tables, segment[:, None], segment[None, :])


def dot_plain(left, right):
    return jnp.dot(left, right, preferred_element_type=f32)


def contract_rows(left, right):
    return lax.dot_general(left, right, (((0,), (0,)), ((), ())), preferred_element_type=f32)


def contract_cols(left, right):
    return lax.dot_general(left, right, (((1,), (1,)), ((), ())), preferred_element_type=f32)


def on_device(
    dp_size,
    inputs,
    norm_gain,
    norm_shift,
    qkv_weight,
    qkv_bias,
    up_weight,
    up_bias,
    dense_weight,
    down_weight,
    out_bias,
    cotangent,
    seq_lengths,
    seq_owner,
):
    row_count = inputs.shape[0]
    line = dp_size // 2
    device = lax.axis_index("dp")
    place = device // 2
    side = device % 2
    row = lax.axis_index("row")
    col = lax.axis_index("col")

    over_row = partial(lax.ppermute, axis_name="row", perm=[(0, 1), (1, 0)])
    over_col = partial(lax.ppermute, axis_name="col", perm=[(0, 1), (1, 0)])
    over_side = partial(lax.ppermute, axis_name="dp", perm=[(e, e ^ 1) for e in range(dp_size)])

    def in_order(index, mine, other, axis):
        first = jnp.where(index == 0, mine, other)
        second = jnp.where(index == 0, other, mine)
        return jnp.concatenate([first, second], axis=axis)

    def half_at(array, index, axis):
        width = array.shape[axis] // 2
        return lax.dynamic_slice_in_dim(array, index * width, width, axis)

    segment, position, is_valid = layout(seq_lengths, seq_owner, device, row_count)
    tables = rotation_tables(position)

    gains = jnp.stack([norm_gain, norm_shift])
    grad_branch = cotangent * is_valid.astype(bf16)[:, None]
    inputs_half = in_order(row, inputs, over_row(inputs), 1)
    gains_half = in_order(row, gains, over_row(gains), 1)
    inputs_other = over_col(inputs_half)
    gains_other = over_col(gains_half)
    branch_half = in_order(row, grad_branch, over_row(grad_branch), 1)
    branch_other = over_col(branch_half)

    up_mine, up_other = half_at(up_weight, col, 1), over_col(half_at(up_weight, 1 - col, 1))
    down_mine, down_other = half_at(down_weight, col, 0), over_col(half_at(down_weight, 1 - col, 0))
    qkv_mine, qkv_other = half_at(qkv_weight, col, 1), over_col(half_at(qkv_weight, 1 - col, 1))
    dense_mine, dense_other = half_at(dense_weight, col, 0), over_col(half_at(dense_weight, 1 - col, 0))

    width = 4 * inputs.shape[1]
    source, source_other = inputs_half.astype(f32), inputs_other.astype(f32)
    average = (jnp.sum(source, axis=1) + jnp.sum(source_other, axis=1)) / width
    square = (jnp.sum(source * source, axis=1) + jnp.sum(source_other * source_other, axis=1)) / width
    scale_inv = lax.rsqrt(square - average * average + epsilon)[:, None]

    def hidden_of(rows_in, gain_pair):
        normed = (rows_in - average[:, None]) * scale_inv
        pair = gain_pair.astype(f32)
        return (normed * pair[0] + pair[1]).astype(bf16)

    hidden, hidden_other = hidden_of(source, gains_half), hidden_of(source_other, gains_other)

    before = dot_plain(hidden, up_mine) + dot_plain(hidden_other, up_other) + up_bias.astype(f32)
    activated = jax.nn.gelu(before, approximate=True).astype(bf16)
    d_activated = contract_cols(branch_half, down_mine) + contract_cols(branch_other, down_other)
    unused_value, gelu_back = jax.vjp(partial(jax.nn.gelu, approximate=True), before)
    d_before = gelu_back(d_activated)[0].astype(bf16)

    projected = dot_plain(hidden, qkv_mine) + dot_plain(hidden_other, qkv_other) + qkv_bias.astype(f32)
    d_mixed = (contract_cols(branch_half, dense_mine) + contract_cols(branch_other, dense_other)).astype(bf16)
    attended, d_projected = attention(projected, d_mixed, tables, segment)

    def chunks_of(array, index):
        rows, columns = array.shape
        grouped = array.reshape(rows, columns // (2 * chunk), 2, chunk)
        return lax.dynamic_index_in_dim(grouped, index, 2, keepdims=False).reshape(rows, columns // 2)

    branch_pair = over_side(branch_half)

    def feature_sums(array):
        kept = chunks_of(array, side)
        got = over_side(chunks_of(array, 1 - side))
        own = in_order(col, kept, over_col(kept), 1)
        pair = in_order(col, got, over_col(got), 1)
        return (contract_rows(own, branch_half) + contract_rows(pair, branch_pair)).astype(bf16)

    def along_line(sums):
        depth = sums.shape[0] // line
        parts = sums.reshape(line, depth, sums.shape[1])

        def part(index):
            return lax.dynamic_index_in_dim(parts, jnp.clip(index, 0, line - 1), 0, keepdims=False).astype(f32)

        rightward, leftward = None, None
        for step in range(line - 1):
            right_part = part(line - 1 - step + place)
            left_part = part(place - (line - 1) + step)
            if step:
                right_part = right_part + rightward.astype(f32)
                left_part = left_part + leftward.astype(f32)
            to_right = [(2 * z + x, 2 * z + 2 + x) for z in range(min(step + 1, line - 1)) for x in range(2)]
            to_left = [(dp_size - 1 - p, dp_size - 1 - q) for p, q in to_right]
            rightward = lax.ppermute(right_part.astype(bf16), "dp", to_right)
            leftward = lax.ppermute(left_part.astype(bf16), "dp", to_left)
        return part(place) + rightward.astype(f32) + leftward.astype(f32)

    chunk = down_weight.shape[0] // dp_size
    grad_down = along_line(feature_sums(activated))

    chunk = up_weight.shape[0] // dp_size
    hidden_own = chunks_of(hidden, side)
    hidden_pair = over_side(chunks_of(hidden, 1 - side))

    def hidden_sums(array):
        pair = over_side(array)
        mine = (contract_rows(hidden_own, array) + contract_rows(hidden_pair, pair)).astype(bf16)
        theirs = (contract_rows(hidden_own, over_col(array)) + contract_rows(hidden_pair, over_col(pair))).astype(bf16)
        return in_order(col, along_line(mine), along_line(theirs), 1)

    grad_up = hidden_sums(d_before)
    chunk = dense_weight.shape[0] // dp_size
    grad_dense = along_line(feature_sums(attended))
    grad_qkv = hidden_sums(d_projected)

    def scatter(mine, other):
        half = mine + over_col(other.astype(bf16)).astype(f32)
        return half_at(half, row, 1) + over_row(half_at(half, 1 - row, 1).astype(bf16)).astype(f32)

    branch = scatter(
        dot_plain(attended, dense_mine) + dot_plain(activated, down_mine),
        dot_plain(attended, dense_other) + dot_plain(activated, down_other),
    )
    valid_col = is_valid.astype(f32)[:, None]
    outputs = (inputs.astype(f32) + valid_col * (branch + out_bias.astype(f32))).astype(bf16)

    d_hidden = scatter(
        contract_cols(d_projected, qkv_mine) + contract_cols(d_before, up_mine),
        contract_cols(d_projected, qkv_other) + contract_cols(d_before, up_other),
    )
    normed = (inputs.astype(f32) - average[:, None]) * scale_inv
    d_normed = d_hidden * norm_gain.astype(f32)
    row_sums = jnp.stack([jnp.sum(d_normed, axis=1), jnp.sum(d_normed * normed, axis=1)])
    row_sums = row_sums + over_row(row_sums)
    row_sums = row_sums + over_col(row_sums)
    grad_inputs = cotangent.astype(f32) + scale_inv * (
        d_normed - row_sums[0][:, None] / width - normed * row_sums[1][:, None] / width
    )

    small = [
        jnp.sum(d_hidden * normed, axis=0),
        jnp.sum(d_hidden, axis=0),
        jnp.sum(d_projected.astype(f32), axis=0),
        jnp.sum(d_before.astype(f32), axis=0),
        jnp.sum(grad_branch.astype(f32), axis=0),
    ]
    together = jnp.concatenate(small)
    bit = 1
    while bit < dp_size:
        together = together + lax.ppermute(together, "dp", [(e, e ^ bit) for e in range(dp_size)])
        bit *= 2
    ends = []
    for piece in small:
        ends.append((ends[-1] if ends else 0) + piece.shape[0])
    grad_gain, grad_shift, grad_qkv_bias, grad_up_bias, grad_out_bias = jnp.split(together, ends[:-1])
    return (
        outputs,
        grad_inputs,
        grad_gain,
        grad_shift,
        grad_qkv,
        grad_qkv_bias,
        grad_up,
        grad_up_bias,
        grad_dense,
        grad_down,
        grad_out_bias,
    )


def solution(mesh):
    in_specs = (
        P("dp", ("col", "row")),
        P(("col", "row")),
        P(("col", "row")),
        P("col", "row"),
        P(("row", "col")),
        P("col", "row"),
        P(("row", "col")),
        P("row", "col"),
        P("row", "col"),
        P(("col", "row")),
        P("dp", ("col", "row")),
        P(),
        P(),
    )
    out_specs = (
        P("dp", ("col", "row")),
        P("dp", ("col", "row")),
        P(("col", "row")),
        P(("col", "row")),
        P(("col", "dp"), "row"),
        P(("row", "col")),
        P(("col", "dp"), "row"),
        P(("row", "col")),
        P(("row", "dp"), "col"),
        P(("row", "dp"), "col"),
        P(("col", "row")),
    )
    return jax.shard_map(
        partial(on_device, mesh.shape["dp"]), mesh=mesh, in_specs=in_specs, out_specs=out_specs, check_vma=False
    )
```

```python
from functools import partial
import math

import jax
import jax.numpy as jnp
from jax import lax
from jax.experimental import pallas as pl
from jax.experimental.pallas import tpu as pltpu
from jax.sharding import PartitionSpec as P

HEAD_DIM = 64
ROT = 32
HALF_ROT = ROT // 2
PAIR = 2 * HEAD_DIM
PAIR_QKV = 3 * PAIR

epsilon = 1e-05
masked_score = -1e30
rope_base = 10000.0
VMEM_LIMIT = 67_000_000
SCRATCH_LIMIT = 58 * 1024 * 1024
SENDS = 40
score_scale = HEAD_DIM ** (-0.5)
bf16 = jnp.bfloat16
f32 = jnp.float32


def layout(seq_lengths, seq_owner, device, row_count):
    owned = seq_owner == device
    lengths_owned = jnp.where(owned, seq_lengths, 0)
    seq_ends = jnp.cumsum(lengths_owned, dtype=jnp.int32)
    seq_starts = seq_ends - lengths_owned
    slot_index = jnp.arange(row_count, dtype=jnp.int32)
    segment = jnp.sum((seq_ends[None, :] <= slot_index[:, None]).astype(jnp.int32), axis=1)
    picked = jnp.arange(seq_lengths.shape[0], dtype=jnp.int32)[None, :] == segment[:, None]
    seq_begin = jnp.sum(jnp.where(picked, seq_starts[None, :], 0), axis=1)
    position = slot_index - seq_begin
    is_valid = slot_index < seq_ends[-1]
    return (segment, position, is_valid)


def rotation_tables(position):
    index_range = jnp.arange(HALF_ROT, dtype=f32)
    frequency = rope_base ** (-2.0 * index_range / ROT)
    phase = position.astype(f32)[:, None] * frequency[None, :]
    cosines, sines = jnp.cos(phase), jnp.sin(phase)
    rows = position.shape[0]
    ones = jnp.ones((rows, HEAD_DIM - ROT), f32)
    none = jnp.zeros((rows, HALF_ROT), f32)
    rest = jnp.zeros((rows, HEAD_DIM - ROT), f32)
    same = jnp.concatenate([cosines, cosines, ones], axis=1)
    from_right = jnp.concatenate([sines, none, rest], axis=1)
    from_left = jnp.concatenate([none, sines, rest], axis=1)
    return jnp.stack([same, from_right, from_left])


def turned(array):
    return jnp.swapaxes(array, 0, 1)


def contract(left, right, left_dim, right_dim):
    dims = (((left_dim,), (right_dim,)), ((), ()))
    return lax.dot_general(left, right, dims, preferred_element_type=f32)


gelu_rate = math.sqrt(2.0 / math.pi)
gelu_cube = 0.044715


def gelu(x):
    return 0.5 * x * (1.0 + jnp.tanh(gelu_rate * (x + gelu_cube * x * x * x)))


def gelu_slope(x):
    square = x * x
    bent = jnp.tanh(gelu_rate * (x + gelu_cube * x * square))
    return 0.5 * (1.0 + bent) + 0.5 * x * (1.0 - bent * bent) * (gelu_rate * (1.0 + 3.0 * gelu_cube * square))


def attention_pair(proj, mixed, tables, seg_col, seg_row):
    rows = proj.shape[0]
    block = min(256, rows)
    same, from_right, from_left = tables[0], tables[1], tables[2]

    def rotate(part, sign):
        right = jnp.concatenate([part[:, HALF_ROT:], part[:, :HALF_ROT]], axis=1)
        left = jnp.concatenate([part[:, HEAD_DIM - HALF_ROT :], part[:, : HEAD_DIM - HALF_ROT]], axis=1)
        return part * same - sign * (right * from_right) + sign * (left * from_left)

    attended_heads, grads = [], []
    for head in range(2):
        base = head * 3 * HEAD_DIM
        queries = rotate(proj[:, base : base + HEAD_DIM], 1.0).astype(bf16)
        keys = rotate(proj[:, base + HEAD_DIM : base + 2 * HEAD_DIM], 1.0).astype(bf16)
        values = proj[:, base + 2 * HEAD_DIM : base + 3 * HEAD_DIM].astype(bf16)
        d_outs = mixed[:, head * HEAD_DIM : (head + 1) * HEAD_DIM]
        outs, d_queries, d_keys, d_values = [], [], None, None
        for first in range(0, rows, block):
            last = first + block
            q, d_out = queries[first:last], d_outs[first:last]
            k, v = keys[:last], values[:last]
            row_index = first + lax.broadcasted_iota(jnp.int32, (block, last), 0)
            key_index = lax.broadcasted_iota(jnp.int32, (block, last), 1)
            allowed = (seg_col[first:last, :] == seg_row[:, :last]) & (key_index <= row_index)
            scores = jnp.where(allowed, contract(q, k, 1, 1) * score_scale, masked_score)
            weights = jnp.exp(scores - jnp.max(scores, axis=1, keepdims=True))
            probs = weights * (1.0 / jnp.sum(weights, axis=1, keepdims=True))
            probs_low = probs.astype(bf16)
            outs.append(contract(probs_low, v, 1, 0))
            d_probs = contract(d_out, v, 1, 1)
            row_dot = jnp.sum(probs * d_probs, axis=1, keepdims=True)
            d_scores = (probs * (d_probs - row_dot)).astype(bf16)
            d_queries.append(contract(d_scores, k, 1, 0))
            key_part = contract(d_scores, q, 0, 0)
            value_part = contract(probs_low, d_out, 0, 0)
            if d_keys is None:
                d_keys, d_values = key_part, value_part
            else:
                d_keys = jnp.concatenate([key_part[:first] + d_keys, key_part[first:]], axis=0)
                d_values = jnp.concatenate([value_part[:first] + d_values, value_part[first:]], axis=0)
        attended_heads.append(jnp.concatenate(outs, axis=0))
        grads.append(rotate(jnp.concatenate(d_queries, axis=0) * score_scale, -1.0))
        grads.append(rotate(d_keys * score_scale, -1.0))
        grads.append(d_values)
    attended = jnp.concatenate(attended_heads, axis=1).astype(bf16)
    return attended, jnp.concatenate(grads, axis=1).astype(bf16)


class Sizes:
    def __init__(self, dp_size, inputs, qkv_weight, up_weight, dense_weight, down_weight, seq_lengths):
        self.dp = dp_size
        self.seqs = seq_lengths.shape[0]
        self.line = dp_size // 2
        self.rows, self.quarter = inputs.shape
        self.half = up_weight.shape[0]
        self.width = 2 * self.half
        self.up_chunk = self.half // dp_size
        self.down_chunk = down_weight.shape[0] // dp_size
        self.dense_chunk = dense_weight.shape[0] // dp_size
        self.hidden = up_weight.shape[1] // 2
        self.tiles = self.hidden // self.down_chunk
        self.qkv = qkv_weight.shape[1] // 2
        self.pairs = self.qkv // PAIR_QKV
        self.features = dense_weight.shape[0] // 2


def flows_of(z):
    return dict(
        down=(z.down_chunk // z.up_chunk, z.up_chunk, z.quarter),
        up=(z.tiles, z.up_chunk, z.down_chunk),
        dense=(1, z.dense_chunk, z.quarter),
        qkv=(z.pairs, z.up_chunk, PAIR_QKV),
    )


def scratch_of(z):
    rows, q, line, tiles, pairs = z.rows, z.quarter, z.line, z.tiles, z.pairs
    up, down, dense = z.up_chunk, z.down_chunk, z.dense_chunk
    shapes = dict(
        inq=((2, 2, rows, q), bf16),
        cotq=((2, 2, rows, q), bf16),
        cotp=((2, rows, q), bf16),
        gainq=((2, 2, 16, q), f32),
        hid=((2, rows, z.half), bf16),
        hid_own=((line, rows, up), bf16),
        hid_send=((line, rows, up), bf16),
        hid_pair=((line, rows, up), bf16),
        stat=((2, rows, 1), f32),
        before=((tiles, rows, down), f32),
        act=((tiles, rows, down), bf16),
        act_own=((line, rows, down), bf16),
        act_pair=((line, rows, down), bf16),
        db_own=((2, tiles, rows, down), bf16),
        db_pair=((2, tiles, rows, down), bf16),
        mixed=((pairs, rows, PAIR), bf16),
        att=((rows, z.features), bf16),
        att_part=((line, rows, dense), bf16),
        att_own=((line, rows, dense), bf16),
        att_pair=((line, rows, dense), bf16),
        dp_own=((2, pairs, rows, PAIR_QKV), bf16),
        dp_pair=((2, pairs, rows, PAIR_QKV), bf16),
        weight=((2, 2, z.half, 512), bf16),
        st_down=((line, 2) + flows_of(z)["down"], bf16),
        st_up=((line, 2) + flows_of(z)["up"], bf16),
        st_dense=((line, 2) + flows_of(z)["dense"], bf16),
        st_qkv=((line, 2) + flows_of(z)["qkv"], bf16),
        got_down=(flows_of(z)["down"], bf16),
        got_up=(flows_of(z)["up"], bf16),
        got_dense=(flows_of(z)["dense"], bf16),
        got_qkv=(flows_of(z)["qkv"], bf16),
        part_send=((2, rows, q), bf16),
        part_row=((rows, q), bf16),
        out_row=((rows, q), bf16),
        dh_row=((rows, q), bf16),
        sum_send=((2, 8, rows), f32),
        sum_got=((2, 8, rows), f32),
    )
    if shapes["before"][0] != (4, rows, q):
        shapes["total"] = ((4, rows, q), f32)
    if shapes["st_up"] == shapes["st_down"]:
        del shapes["st_up"], shapes["got_up"]
    return shapes


def fits(z):
    total = 0
    for shape, kind in scratch_of(z).values():
        total += math.prod(shape[:-1]) * -(-shape[-1] // 128) * 128 * jnp.dtype(kind).itemsize
    return z.line % 2 == 0 and total <= SCRATCH_LIMIT


def layer_kernel(z, names, *refs):
    r = dict(zip(names, refs))
    rows, q, line, tiles, pairs = z.rows, z.quarter, z.line, z.tiles, z.pairs
    half_line = line // 2
    if "total" not in r:
        r["total"] = r["before"]
    r["out_got"], r["dh_got"] = r["inq"].at[1], r["cotq"].at[1]
    shared = "st_up" not in r
    if shared:
        r["st_up"], r["got_up"] = r["st_down"], r["got_down"]
    dp = lax.axis_index("dp")
    row = lax.axis_index("row")
    col = lax.axis_index("col")
    place, side = dp // 2, lax.rem(dp, 2)
    other_row, other_col, other_side = 1 - row, 1 - col, 1 - side
    to_row = {"row": other_row}
    to_col = {"col": other_col}
    to_side = {"dp": dp + 1 - 2 * side}
    MESH = pl.DeviceIdType.MESH

    marks = dict(send=0, recv=0, local=0)

    def take(kind, count):
        first = marks[kind]
        marks[kind] += count
        return first

    def remote(src, dst, send, recv, device):
        return pltpu.make_async_remote_copy(
            src_ref=src,
            dst_ref=dst,
            send_sem=r["send_sem"].at[send],
            recv_sem=r["recv_sem"].at[recv],
            device_id=device,
            device_id_type=MESH,
        )

    pending = []

    class Message:
        def __init__(self, src, dst, device, got=None):
            index = (take("send", 1), take("recv", 1))
            self.copy = lambda: remote(src, dst, *index, device)
            self.got = lambda: remote(src if got is None else got, dst if got is None else got, *index, device)

        def start(self):
            self.copy().start()
            pending.append(self)

        def wait(self):
            self.got().wait_recv()

    right, left = {"dp": dp + 2}, {"dp": dp - 2}
    has_right, has_left = place < line - 1, place > 0
    barrier = pltpu.get_barrier_semaphore()
    for device in (to_row, to_col, to_side):
        pl.semaphore_signal(barrier, inc=1, device_id=device, device_id_type=MESH)

    @pl.when(has_right)
    def _():
        pl.semaphore_signal(barrier, inc=1, device_id=right, device_id_type=MESH)

    @pl.when(has_left)
    def _():
        pl.semaphore_signal(barrier, inc=1, device_id=left, device_id_type=MESH)

    cot = r["cot"]
    valid = (r["seg_col"][...] < z.seqs).astype(f32)
    r["cotq"][0, row] = cot[...] * valid.astype(bf16)
    pl.semaphore_wait(barrier, 3 + has_right.astype(jnp.int32) + has_left.astype(jnp.int32))

    def gather(src, held):
        over = Message(src, held.at[0, row], to_row, held.at[0, other_row])
        across = Message(src, held.at[1, row], to_col, held.at[1, row])
        onward = Message(held.at[0, other_row], held.at[1, other_row], to_col, held.at[1, other_row])
        return over, across, onward

    in_over, in_across, in_onward = gather(r["inputs"], r["inq"])
    gain_over, gain_across, gain_onward = gather(r["gains"], r["gainq"])
    cot_over, cot_across, cot_onward = gather(r["cotq"].at[0, row], r["cotq"])
    cot_side = Message(r["cotq"].at[0, row], r["cotp"].at[row], to_side)
    cot_side_onward = Message(r["cotq"].at[0, other_row], r["cotp"].at[other_row], to_side)
    hid_side = Message(r["hid_send"], r["hid_pair"], to_side)
    swaps = {
        "up": Message(r["up_w"].at[:, pl.ds(pl.multiple_of(other_col * z.hidden, 128), z.hidden)], r["up_o"], to_col, r["up_o"]),
        "qkv": Message(r["qkv_w"].at[:, pl.ds(pl.multiple_of(other_col * z.qkv, 128), z.qkv)], r["qkv_o"], to_col, r["qkv_o"]),
        "down": Message(r["down_w"].at[pl.ds(pl.multiple_of(other_col * z.hidden, 16), z.hidden), :], r["down_o"], to_col, r["down_o"]),
        "dense": Message(r["dense_w"].at[pl.ds(pl.multiple_of(other_col * z.features, 16), z.features), :], r["dense_o"], to_col, r["dense_o"]),
    }

    def local(src, dst, index):
        return pltpu.make_async_copy(src, dst, r["local_sem"].at[index])

    stream_base = take("local", 8)
    once = take("local", 4)

    in_over.start()
    gain_over.start()
    in_across.start()
    gain_across.start()
    keep_in = local(r["inputs"], r["inq"].at[0, row], once)
    keep_gain = local(r["gains"], r["gainq"].at[0, row], once + 1)
    keep_in.start()
    keep_gain.start()
    cot_side.start()
    swaps["up"].start()
    gain_over.wait()
    gain_onward.start()
    in_over.wait()
    in_onward.start()
    cot_over.start()
    cot_across.start()
    keep_in.wait()
    keep_gain.wait()
    gain_across.wait()
    gain_onward.wait()
    in_across.wait()
    in_onward.wait()

    block = min(64, rows)

    def norm_rows(step, carry):
        at = pl.ds(pl.multiple_of(step * block, block), block)
        parts = [r["inq"][h, p, at].astype(f32) for h in range(2) for p in range(2)]
        total = parts[0] + parts[1] + parts[2] + parts[3]
        squares = parts[0] * parts[0] + parts[1] * parts[1] + parts[2] * parts[2] + parts[3] * parts[3]
        average = jnp.sum(total, axis=1, keepdims=True) / z.width
        variance = jnp.sum(squares, axis=1, keepdims=True) / z.width - average * average
        scale_inv = lax.rsqrt(variance + epsilon)
        r["stat"][0, at] = average
        r["stat"][1, at] = scale_inv
        for h in range(2):
            for p in range(2):
                normed = (parts[2 * h + p] - average) * scale_inv
                gain, shift = r["gainq"][h, p, 0:1, :], r["gainq"][h, p, 8:9, :]
                r["hid"][h, at, p * q : (p + 1) * q] = (normed * gain + shift).astype(bf16)
        return carry

    lax.fori_loop(0, rows // block, norm_rows, 0)
    for c in range(line):
        even = r["hid"][0, :, 2 * c * z.up_chunk : (2 * c + 1) * z.up_chunk]
        odd = r["hid"][0, :, (2 * c + 1) * z.up_chunk : (2 * c + 2) * z.up_chunk]
        r["hid_own"][c] = jnp.where(side == 0, even, odd)
        r["hid_send"][c] = jnp.where(side == 0, odd, even)

    def stream(count, copies, work):
        for copy in copies(jnp.int32(0), jnp.int32(0)):
            copy.start()

        def one(step, carry):
            slot = lax.rem(step, 2)

            @pl.when(step + 1 < count)
            def _():
                for copy in copies(step + 1, 1 - slot):
                    copy.start()

            for copy in copies(step, slot):
                copy.wait()
            work(step, slot)
            return carry

        lax.fori_loop(0, count, one, 0)

    def column_tiles(name, each, tile_of=lambda step: step):
        def copies(step, slot):
            tile = tile_of(step)
            mine = r[name + "_w"].at[:, pl.ds(pl.multiple_of((col * r[name + "_o"].shape[1]) + tile * each, 128), each)]
            theirs = r[name + "_o"].at[:, pl.ds(pl.multiple_of(tile * each, 128), each)]
            return [
                local(mine, r["weight"].at[slot, 0, :, :each], stream_base + slot * 4),
                local(theirs, r["weight"].at[slot, 1, :, :each], stream_base + slot * 4 + 1),
            ]

        return copies

    def row_tiles(name, each, tile_of=lambda step: step):
        def copies(step, slot):
            tile = tile_of(step)
            found = []
            for h in range(2):
                start = tile * each + (col * r[name + "_o"].shape[0] if h == 0 else 0)
                src = r[name + ("_w" if h == 0 else "_o")]
                for p in range(2):
                    found.append(
                        local(
                            src.at[pl.ds(pl.multiple_of(start, 16), each), p * q : (p + 1) * q],
                            r["weight"].at[slot, h, p * q : p * q + each, :],
                            stream_base + slot * 4 + 2 * h + p,
                        )
                    )
            return found

        return copies

    def tile_at(step):
        later = (step >= half_line).astype(jnp.int32)
        turn = step - later * half_line
        return 2 * turn + jnp.where(later == 1, side, other_side)

    act_side_send, act_side_recv = take("send", half_line), take("recv", half_line)
    act_col_send, act_col_recv = take("send", half_line), take("recv", half_line)
    act_on_send, act_on_recv = take("send", half_line), take("recv", half_line)

    def act_side(k):
        slot = col * half_line + k
        tile = 2 * k + other_side
        return remote(r["act"].at[tile], r["act_pair"].at[slot], act_side_send + k, act_side_recv + k, to_side)

    def act_col(k):
        slot = col * half_line + k
        return remote(r["act_own"].at[slot], r["act_own"].at[slot], act_col_send + k, act_col_recv + k, to_col)

    def act_on(k):
        slot = col * half_line + k
        return remote(r["act_pair"].at[slot], r["act_pair"].at[slot], act_on_send + k, act_on_recv + k, to_col)

    def up_work(step, slot):
        tile = tile_at(step)
        before = contract(r["hid"][0], r["weight"][slot, 0, :, : z.down_chunk], 1, 0)
        before = before + contract(r["hid"][1], r["weight"][slot, 1, :, : z.down_chunk], 1, 0)
        before = before + r["up_b"][tile]
        r["before"][tile] = before
        activated = gelu(before).astype(bf16)
        r["act"][tile] = activated

        @pl.when(step < half_line)
        def _():
            act_side(step).start()

        @pl.when(step >= half_line)
        def _():
            k = step - half_line
            r["act_own"][col * half_line + k] = activated
            act_col(k).start()

    swaps["down"].start()
    swaps["up"].wait()
    stream(tiles, column_tiles("up", z.down_chunk, tile_at), up_work)

    cot_over.wait()
    cot_onward.start()
    cot_side_onward.start()
    hid_side.start()
    swaps["qkv"].start()
    swaps["dense"].start()
    cot_across.wait()
    cot_onward.wait()
    swaps["down"].wait()

    def each_side(name_own, name_pair, count):
        side_send, side_recv = take("send", count), take("recv", count)
        col_send, col_recv = take("send", count), take("recv", count)
        on_send, on_recv = take("send", count), take("recv", count)
        own, pair = r[name_own], r[name_pair]

        def to_side_peer(k):
            return remote(own.at[col, k], pair.at[col, k], side_send + k, side_recv + k, to_side)

        def to_col_peer(k):
            return remote(own.at[col, k], own.at[col, k], col_send + k, col_recv + k, to_col)

        def onward(k):
            return remote(pair.at[col, k], pair.at[col, k], on_send + k, on_recv + k, to_col)

        return to_side_peer, to_col_peer, onward

    db_side, db_col, db_on = each_side("db_own", "db_pair", tiles)
    dp_side, dp_col, dp_on = each_side("dp_own", "dp_pair", pairs)

    def over_weight_rows(slot, each, lefts):
        total = None
        for h in range(2):
            for p in range(2):
                part = contract(lefts(h, p), r["weight"][slot, h, p * q : p * q + each, :], 1, 1)
                total = part if total is None else total + part
        return total

    def down_work(step, slot):
        tile = tile_at(step)
        d_activated = over_weight_rows(slot, z.down_chunk, lambda h, p: r["cotq"][h, p])
        d_before = (d_activated * gelu_slope(r["before"][tile])).astype(bf16)
        r["db_own"][col, tile] = d_before
        r["sum_before"][tile] = jnp.sum(d_before.astype(f32), axis=0, keepdims=True)
        db_side(tile).start()
        db_col(tile).start()

    stream(tiles, row_tiles("down", z.down_chunk, tile_at), down_work)

    def loop(first, last, work):
        def one(k, carry):
            work(k)
            return carry

        lax.fori_loop(first, last, one, 0)

    def pass_on(got, onward):
        def work(k):
            got(k).wait_recv()
            onward(k).start()

        return work

    def waits(*copies):
        def work(k):
            for copy in copies:
                copy(k).wait_recv()

        return work

    class Flow:
        def __init__(self, name, own_rows, pair_rows, own_columns, pair_columns, split=False, earlier=None):
            self.name, self.split, self.earlier = name, split, earlier
            self.own_rows, self.pair_rows = own_rows, pair_rows
            self.own_columns, self.pair_columns = own_columns, pair_columns
            self.stage, self.land, self.got = r["st_" + name], r["land_" + name], r["got_" + name]
            self.count, self.depth = flows_of(z)[name][:2]
            self.send = take("send", 2 * line)
            self.recv = take("recv", 2 * (line + 1))
            self.local = take("local", 1)
            self.later = False

        def copy(self, chunk, group, slot, device):
            return remote(
                self.stage.at[chunk, group],
                self.land.at[slot, group],
                self.send + 2 * chunk + group,
                self.recv + 2 * slot + group,
                device,
            )

        def sums(self, chunk):
            own, pair = turned(self.own_rows[chunk]), turned(self.pair_rows[chunk])

            def tile_sums(group, tile):
                at = slice(tile * self.depth, (tile + 1) * self.depth) if self.split else slice(None)
                column = 0 if self.split else tile
                part = contract(own[at], self.own_columns(group, column), 1, 0)
                return part + contract(pair[at], self.pair_columns(group, column), 1, 0)

            return tile_sums

        def step(self, number):
            def one(way, carry):
                rightward = way == 0
                rank = jnp.where(rightward, place, line - 1 - place)
                chunk = jnp.where(rightward, line - 1 - number + place, place - (line - 1) + number)
                last = (chunk == place - 1) & jnp.logical_not(rightward)
                slot = jnp.where(last, line, chunk)
                device = {"dp": dp + 2 - 4 * way}

                @pl.when((rank <= number) & (rank < line - 1))
                def _():
                    tile_sums = self.sums(chunk)
                    for group in range(2):
                        if self.earlier is not None:
                            self.earlier.copy(chunk, group, chunk, device).wait_send()

                        @pl.when(rank > 0)
                        def _():
                            self.copy(chunk, group, chunk, device).wait_recv()
                            bring = local(self.land.at[chunk, group], self.got, self.local)
                            bring.start()
                            bring.wait()

                        @pl.when(rank == 0)
                        def _():
                            self.got[...] = jnp.zeros_like(self.got)

                        for tile in range(self.count):
                            whole = tile_sums(group, tile) + self.got[tile].astype(f32)
                            self.stage[chunk, group, tile] = whole.astype(bf16)
                        self.copy(chunk, group, slot, device).start()

                return carry

            lax.fori_loop(0, 2, one, 0)

        def steps(self, first, last):
            if last - first == 1:
                self.step(first)
            elif last > first:
                loop(first, last, self.step)

        def own(self):
            if self.earlier is not None:
                self.earlier.out.wait()
                self.earlier.later = True
            tile_sums = self.sums(place)
            for group in range(2):
                for tile in range(self.count):
                    self.stage[place, group, tile] = tile_sums(group, tile).astype(bf16)
            self.out = local(self.stage.at[place], r["own_" + self.name], self.local)
            self.out.start()

        def finish(self):
            if not self.later:
                self.out.wait()
            for group in range(2):

                @pl.when(has_left)
                def _():
                    self.copy(place, group, place, left).wait_recv()

                @pl.when(has_right)
                def _():
                    self.copy(place, group, line, right).wait_recv()

            def sent(chunk):
                @pl.when(chunk != place)
                def _():
                    for group in range(2):
                        self.copy(chunk, group, chunk, right).wait_send()

            if not self.later:
                loop(0, line, sent)

    cot_own_tile = lambda group, tile: r["cotq"][0, group]
    cot_pair_tile = lambda group, tile: r["cotp"][group]
    down = Flow("down", r["act_own"], r["act_pair"], cot_own_tile, cot_pair_tile, split=True)
    up = Flow(
        "up",
        r["hid_own"],
        r["hid_pair"],
        lambda group, tile: r["db_own"][group, tile],
        lambda group, tile: r["db_pair"][group, tile],
        earlier=down if shared else None,
    )
    dense = Flow("dense", r["att_own"], r["att_pair"], cot_own_tile, cot_pair_tile)
    qkv = Flow(
        "qkv",
        r["hid_own"],
        r["hid_pair"],
        lambda group, tile: r["dp_own"][group, tile],
        lambda group, tile: r["dp_pair"][group, tile],
    )
    cuts = (0, 1, line // 2, line - 1)

    loop(0, half_line, pass_on(act_side, act_on))
    loop(0, half_line, waits(act_col, act_on))
    cot_side.wait()
    cot_side_onward.wait()
    down.steps(cuts[0], cuts[1])

    swaps["qkv"].wait()

    def qkv_work(step, slot):
        part = contract(r["hid"][0], r["weight"][slot, 0, :, :PAIR_QKV], 1, 0)
        part = part + contract(r["hid"][1], r["weight"][slot, 1, :, :PAIR_QKV], 1, 0)
        r["total"][step, :, :PAIR_QKV] = part + r["qkv_b"][step]

    stream(pairs, column_tiles("qkv", PAIR_QKV), qkv_work)
    swaps["dense"].wait()

    def dense_work(step, slot):
        d_mixed = over_weight_rows(slot, z.features, lambda h, p: r["cotq"][h, p]).astype(bf16)
        for pair in range(pairs):
            r["mixed"][pair] = d_mixed[:, pair * PAIR : (pair + 1) * PAIR]

    stream(1, row_tiles("dense", z.features), dense_work)
    down.steps(cuts[1], cuts[2])

    att_side_send, att_side_recv = take("send", half_line), take("recv", half_line)
    att_col_send, att_col_recv = take("send", half_line), take("recv", half_line)
    att_on_send, att_on_recv = take("send", half_line), take("recv", half_line)

    def att_side(k):
        slot = col * half_line + k
        return remote(
            r["att_part"].at[2 * k + other_side], r["att_pair"].at[slot], att_side_send + k, att_side_recv + k, to_side
        )

    def att_col(k):
        slot = col * half_line + k
        return remote(r["att_own"].at[slot], r["att_own"].at[slot], att_col_send + k, att_col_recv + k, to_col)

    def att_on(k):
        slot = col * half_line + k
        return remote(r["att_pair"].at[slot], r["att_pair"].at[slot], att_on_send + k, att_on_recv + k, to_col)

    def head_pair(pair):
        attended, d_projected = attention_pair(
            r["total"][pair, :, :PAIR_QKV], r["mixed"][pair], r["tables"], r["seg_col"][...], r["seg_row"][...]
        )
        r["dp_own"][col, pair] = d_projected
        dp_side(pair).start()
        dp_col(pair).start()
        r["sum_projected"][pair] = jnp.sum(d_projected.astype(f32), axis=0, keepdims=True)
        r["att"][:, pl.ds(pl.multiple_of(pair * PAIR, PAIR), PAIR)] = attended
        each = PAIR // z.dense_chunk
        for part in range(each):
            chunk = pair * each + part
            k = chunk // 2
            piece = attended[:, part * z.dense_chunk : (part + 1) * z.dense_chunk]

            @pl.when(lax.rem(chunk, 2) == side)
            def _():
                r["att_own"][col * half_line + k] = piece
                att_col(k).start()

            @pl.when(lax.rem(chunk, 2) == other_side)
            def _():
                r["att_part"][chunk] = piece
                att_side(k).start()

    loop(0, pairs // 2, head_pair)
    down.steps(cuts[2], cuts[3])
    loop(pairs // 2, pairs, head_pair)

    hid_side.wait()
    loop(0, tiles, pass_on(db_side, db_on))

    loop(0, tiles, waits(db_col, db_on))
    up.steps(cuts[0], cuts[1])

    def scatter(name, total, earlier=None):
        across = Message(r["part_send"], r[name + "_got"], to_col)
        over = Message(r["part_row"], r[name + "_row"], to_row)

        def free(message):
            message.copy().wait_send()
            pending.remove(message)

        def first():
            if earlier is not None:
                free(earlier[0])
            for p in range(2):
                r["part_send"][p] = total[2 + p].astype(bf16)
            across.start()

        def second():
            across.wait()
            if earlier is not None:
                free(earlier[1])
            for p in range(2):
                total[p] = total[p] + r[name + "_got"][p].astype(f32)
            r["part_row"][...] = total[other_row].astype(bf16)
            over.start()

        def third():
            over.wait()
            return total[row] + r[name + "_row"][...].astype(f32)

        return first, second, third, (across, over)

    total = r["total"]

    def down_out(step, slot):
        for h in range(2):
            for p in range(2):
                part = contract(r["act"][step], r["weight"][slot, h, p * q : p * q + z.down_chunk, :], 1, 0)

                @pl.when(step == 0)
                def _():
                    total[2 * h + p] = part

                @pl.when(step > 0)
                def _():
                    total[2 * h + p] = total[2 * h + p] + part

    def dense_out(step, slot):
        for h in range(2):
            for p in range(2):
                part = contract(r["att"][...], r["weight"][slot, h, p * q : p * q + z.features, :], 1, 0)
                total[2 * h + p] = total[2 * h + p] + part

    stream(tiles, row_tiles("down", z.down_chunk), down_out)
    stream(1, row_tiles("dense", z.features), dense_out)
    out_first, out_second, out_third, out_messages = scatter("out", total)
    out_first()
    loop(0, pairs, pass_on(dp_side, dp_on))
    loop(0, half_line, pass_on(att_side, att_on))
    up.steps(cuts[1], cuts[2])
    out_second()
    loop(0, half_line, waits(att_col, att_on))
    loop(0, pairs, waits(dp_col, dp_on))
    up.steps(cuts[2], cuts[3])
    dense.steps(cuts[0], cuts[1])
    qkv.steps(cuts[0], cuts[1])
    branch = out_third()
    bias = r["out_b"][...]
    r["outputs"][...] = (r["inq"][0, row].astype(f32) + (r["seg_col"][...] < z.seqs).astype(f32) * (branch + bias)).astype(bf16)
    r["sum_quarter"][2] = jnp.sum(r["cotq"][0, row].astype(f32), axis=0, keepdims=True)

    def up_back(step, slot):
        for h in range(2):
            for p in range(2):
                part = contract(r["db_own"][col, step], r["weight"][slot, h, p * q : (p + 1) * q, : z.down_chunk], 1, 1)

                @pl.when(step == 0)
                def _():
                    total[2 * h + p] = part

                @pl.when(step > 0)
                def _():
                    total[2 * h + p] = total[2 * h + p] + part

    def qkv_back(step, slot):
        for h in range(2):
            for p in range(2):
                part = contract(r["dp_own"][col, step], r["weight"][slot, h, p * q : (p + 1) * q, :PAIR_QKV], 1, 1)
                total[2 * h + p] = total[2 * h + p] + part

    stream(tiles, column_tiles("up", z.down_chunk), up_back)
    stream(pairs, column_tiles("qkv", PAIR_QKV), qkv_back)
    dh_first, dh_second, dh_third, dh_messages = scatter("dh", total, out_messages)
    dh_first()
    dense.steps(cuts[1], cuts[2])
    qkv.steps(cuts[1], cuts[2])
    dh_second()

    d_hidden = dh_third()
    total[0] = d_hidden
    own_in = r["inq"].at[0, row]
    gain = r["gainq"][0, row, 0:1, :]
    sums_row = Message(r["sum_send"].at[0], r["sum_got"].at[0], to_row)
    sums_col = Message(r["sum_send"].at[1], r["sum_got"].at[1], to_col)
    normed = (own_in[...].astype(f32) - r["stat"][0]) * r["stat"][1]
    d_normed = d_hidden * gain
    lane = lax.broadcasted_iota(jnp.int32, (rows, 128), 1)
    one = jnp.sum(d_normed, axis=1, keepdims=True)
    two = jnp.sum(d_normed * normed, axis=1, keepdims=True)
    packed = jnp.where(lane == 0, one, jnp.where(lane == 1, two, 0.0))
    r["sum_send"][0] = turned(packed)[:8]
    sums_row.start()
    r["sum_quarter"][0] = jnp.sum(d_hidden * normed, axis=0, keepdims=True)
    r["sum_quarter"][1] = jnp.sum(d_hidden, axis=0, keepdims=True)
    dense.steps(cuts[2], cuts[3])
    qkv.steps(cuts[2], cuts[3])
    sums_row.wait()
    r["sum_send"][1] = r["sum_send"][0] + r["sum_got"][0]
    sums_col.start()
    for flow in (down, up, dense, qkv):
        flow.own()
    sums_col.wait()
    both = r["sum_send"][1] + r["sum_got"][1]
    spread = turned(jnp.concatenate([both, jnp.zeros((120, rows), f32)], axis=0))
    part_one, part_two = spread[:, 0:1] / z.width, spread[:, 1:2] / z.width
    d_hidden = total[0]
    normed = (own_in[...].astype(f32) - r["stat"][0]) * r["stat"][1]
    r["grad_inputs"][...] = cot[...].astype(f32) + r["stat"][1] * (d_hidden * gain - part_one - normed * part_two)

    for flow in (down, up, dense, qkv):
        flow.finish()
    for message in pending:
        message.copy().wait_send()

    def sent(*copies):
        def work(k):
            for copy in copies:
                copy(k).wait_send()

        return work

    loop(0, half_line, sent(act_side, act_col, act_on, att_side, att_col, att_on))
    loop(0, tiles, sent(db_side, db_col, db_on))
    loop(0, pairs, sent(dp_side, dp_col, dp_on))
    assert marks["send"] <= SENDS * line and marks["recv"] <= SENDS * line and marks["local"] <= 16


def on_device(
    dp_size,
    inputs,
    norm_gain,
    norm_shift,
    qkv_weight,
    qkv_bias,
    up_weight,
    up_bias,
    dense_weight,
    down_weight,
    out_bias,
    cotangent,
    seq_lengths,
    seq_owner,
):
    z = Sizes(dp_size, inputs, qkv_weight, up_weight, dense_weight, down_weight, seq_lengths)
    if not fits(z):
        return on_device_plain(
            dp_size,
            inputs,
            norm_gain,
            norm_shift,
            qkv_weight,
            qkv_bias,
            up_weight,
            up_bias,
            dense_weight,
            down_weight,
            out_bias,
            cotangent,
            seq_lengths,
            seq_owner,
        )
    rows, q, line = z.rows, z.quarter, z.line
    device = lax.axis_index("dp")
    place = device // 2
    segment, position, is_valid = layout(seq_lengths, seq_owner, device, rows)
    tables = rotation_tables(position)
    gains = jnp.concatenate(
        [jnp.broadcast_to(norm_gain.astype(f32)[None], (8, q)), jnp.broadcast_to(norm_shift.astype(f32)[None], (8, q))]
    )
    operands = dict(
        inputs=(inputs, pl.ANY),
        cot=(cotangent, pltpu.VMEM),
        gains=(gains, pl.ANY),
        seg_col=(segment[:, None], pltpu.VMEM),
        seg_row=(segment[None, :], pltpu.VMEM),
        tables=(tables, pltpu.VMEM),
        up_b=(up_bias.astype(f32).reshape(z.tiles, 1, z.down_chunk), pltpu.VMEM),
        qkv_b=(qkv_bias.astype(f32).reshape(z.pairs, 1, PAIR_QKV), pltpu.VMEM),
        out_b=(out_bias.astype(f32)[None], pltpu.VMEM),
        up_w=(up_weight, pl.ANY),
        down_w=(down_weight, pl.ANY),
        qkv_w=(qkv_weight, pl.ANY),
        dense_w=(dense_weight, pl.ANY),
    )
    results = dict(
        outputs=((rows, q), bf16, pltpu.VMEM),
        grad_inputs=((rows, q), f32, pltpu.VMEM),
        sum_before=((z.tiles, 1, z.down_chunk), f32, pltpu.VMEM),
        sum_projected=((z.pairs, 1, PAIR_QKV), f32, pltpu.VMEM),
        sum_quarter=((3, 1, q), f32, pltpu.VMEM),
        up_o=((z.half, z.hidden), bf16, pl.ANY),
        down_o=((z.hidden, z.half), bf16, pl.ANY),
        qkv_o=((z.half, z.qkv), bf16, pl.ANY),
        dense_o=((z.features, z.half), bf16, pl.ANY),
    )
    for name, shape in flows_of(z).items():
        results["land_" + name] = ((line + 1, 2) + shape, bf16, pl.ANY)
        results["own_" + name] = ((2,) + shape, bf16, pl.ANY)
    scratch = scratch_of(z)
    names = list(operands) + list(results) + list(scratch) + ["send_sem", "recv_sem", "local_sem"]
    found = pl.pallas_call(
        partial(layer_kernel, z, names),
        in_specs=[pl.BlockSpec(memory_space=space) for value, space in operands.values()],
        out_specs=[pl.BlockSpec(memory_space=space) for shape, kind, space in results.values()],
        out_shape=[jax.ShapeDtypeStruct(shape, kind) for shape, kind, space in results.values()],
        scratch_shapes=[pltpu.VMEM(shape, kind) for shape, kind in scratch.values()]
        + [pltpu.SemaphoreType.DMA((SENDS * line,)), pltpu.SemaphoreType.DMA((SENDS * line,)), pltpu.SemaphoreType.DMA((16,))],
        compiler_params=pltpu.CompilerParams(
            collective_id=0, has_side_effects=True, vmem_limit_bytes=VMEM_LIMIT
        ),
        name="layer",
    )(*[value for value, space in operands.values()])
    got = dict(zip(results, found))

    def whole(name, split=False):
        land = got["land_" + name]
        from_left = lax.dynamic_index_in_dim(land, place, 0, keepdims=False).astype(f32)
        from_right = land[line].astype(f32)
        total = got["own_" + name].astype(f32)
        total = total + jnp.where(place > 0, from_left, 0.0) + jnp.where(place < line - 1, from_right, 0.0)
        groups, tiles, depth, each = total.shape
        if split:
            return total.transpose(1, 2, 0, 3).reshape(tiles * depth, groups * each)
        return total.transpose(2, 0, 1, 3).reshape(depth, groups * tiles * each)

    small = [
        got["sum_quarter"][0, 0],
        got["sum_quarter"][1, 0],
        got["sum_projected"].reshape(-1),
        got["sum_before"].reshape(-1),
        got["sum_quarter"][2, 0],
    ]
    together = jnp.concatenate(small)
    bit = 1
    while bit < dp_size:
        together = together + lax.ppermute(together, "dp", [(e, e ^ bit) for e in range(dp_size)])
        bit *= 2
    ends = []
    for piece in small:
        ends.append((ends[-1] if ends else 0) + piece.shape[0])
    grad_gain, grad_shift, grad_qkv_bias, grad_up_bias, grad_out_bias = jnp.split(together, ends[:-1])
    return (
        got["outputs"],
        got["grad_inputs"],
        grad_gain,
        grad_shift,
        whole("qkv"),
        grad_qkv_bias,
        whole("up"),
        grad_up_bias,
        whole("dense"),
        whole("down", split=True),
        grad_out_bias,
    )


def attention_kernel(proj_ref, mixed_ref, tables_ref, seg_col_ref, seg_row_ref, attended_ref, grad_ref):
    attended_ref[...], grad_ref[...] = attention_pair(
        proj_ref[...], mixed_ref[...], tables_ref, seg_col_ref[...], seg_row_ref[...]
    )


def attention(projected, mixed, tables, segment):
    rows, width = projected.shape
    pairs = width // PAIR_QKV
    return pl.pallas_call(
        attention_kernel,
        grid=(pairs,),
        in_specs=[
            pl.BlockSpec((rows, PAIR_QKV), lambda i: (0, i)),
            pl.BlockSpec((rows, PAIR), lambda i: (0, i)),
            pl.BlockSpec((3, rows, HEAD_DIM), lambda i: (0, 0, 0)),
            pl.BlockSpec((rows, 1), lambda i: (0, 0)),
            pl.BlockSpec((1, rows), lambda i: (0, 0)),
        ],
        out_specs=[
            pl.BlockSpec((rows, PAIR), lambda i: (0, i)),
            pl.BlockSpec((rows, PAIR_QKV), lambda i: (0, i)),
        ],
        out_shape=[
            jax.ShapeDtypeStruct((rows, pairs * PAIR), bf16),
            jax.ShapeDtypeStruct((rows, width), bf16),
        ],
        compiler_params=pltpu.CompilerParams(vmem_limit_bytes=48 * 1024 * 1024),
        cost_estimate=pl.CostEstimate(
            flops=14 * 2 * pairs * rows * rows * HEAD_DIM * 2,
            bytes_accessed=rows * width * 7,
            transcendentals=2 * pairs * rows * rows,
        ),
        name="attention",
    )(projected, mixed, tables, segment[:, None], segment[None, :])


def dot_plain(left, right):
    return jnp.dot(left, right, preferred_element_type=f32)


def contract_rows(left, right):
    return lax.dot_general(left, right, (((0,), (0,)), ((), ())), preferred_element_type=f32)


def contract_cols(left, right):
    return lax.dot_general(left, right, (((1,), (1,)), ((), ())), preferred_element_type=f32)


def on_device_plain(
    dp_size,
    inputs,
    norm_gain,
    norm_shift,
    qkv_weight,
    qkv_bias,
    up_weight,
    up_bias,
    dense_weight,
    down_weight,
    out_bias,
    cotangent,
    seq_lengths,
    seq_owner,
):
    row_count = inputs.shape[0]
    line = dp_size // 2
    device = lax.axis_index("dp")
    place = device // 2
    side = device % 2
    row = lax.axis_index("row")
    col = lax.axis_index("col")

    over_row = partial(lax.ppermute, axis_name="row", perm=[(0, 1), (1, 0)])
    over_col = partial(lax.ppermute, axis_name="col", perm=[(0, 1), (1, 0)])
    over_side = partial(lax.ppermute, axis_name="dp", perm=[(e, e ^ 1) for e in range(dp_size)])

    def in_order(index, mine, other, axis):
        first = jnp.where(index == 0, mine, other)
        second = jnp.where(index == 0, other, mine)
        return jnp.concatenate([first, second], axis=axis)

    def half_at(array, index, axis):
        width = array.shape[axis] // 2
        return lax.dynamic_slice_in_dim(array, index * width, width, axis)

    segment, position, is_valid = layout(seq_lengths, seq_owner, device, row_count)
    tables = rotation_tables(position)

    gains = jnp.stack([norm_gain, norm_shift])
    grad_branch = cotangent * is_valid.astype(bf16)[:, None]
    inputs_half = in_order(row, inputs, over_row(inputs), 1)
    gains_half = in_order(row, gains, over_row(gains), 1)
    inputs_other = over_col(inputs_half)
    gains_other = over_col(gains_half)
    branch_half = in_order(row, grad_branch, over_row(grad_branch), 1)
    branch_other = over_col(branch_half)

    up_mine, up_other = half_at(up_weight, col, 1), over_col(half_at(up_weight, 1 - col, 1))
    down_mine, down_other = half_at(down_weight, col, 0), over_col(half_at(down_weight, 1 - col, 0))
    qkv_mine, qkv_other = half_at(qkv_weight, col, 1), over_col(half_at(qkv_weight, 1 - col, 1))
    dense_mine, dense_other = half_at(dense_weight, col, 0), over_col(half_at(dense_weight, 1 - col, 0))

    width = 4 * inputs.shape[1]
    source, source_other = inputs_half.astype(f32), inputs_other.astype(f32)
    average = (jnp.sum(source, axis=1) + jnp.sum(source_other, axis=1)) / width
    square = (jnp.sum(source * source, axis=1) + jnp.sum(source_other * source_other, axis=1)) / width
    scale_inv = lax.rsqrt(square - average * average + epsilon)[:, None]

    def hidden_of(rows_in, gain_pair):
        normed = (rows_in - average[:, None]) * scale_inv
        pair = gain_pair.astype(f32)
        return (normed * pair[0] + pair[1]).astype(bf16)

    hidden, hidden_other = hidden_of(source, gains_half), hidden_of(source_other, gains_other)

    before = dot_plain(hidden, up_mine) + dot_plain(hidden_other, up_other) + up_bias.astype(f32)
    activated = jax.nn.gelu(before, approximate=True).astype(bf16)
    d_activated = contract_cols(branch_half, down_mine) + contract_cols(branch_other, down_other)
    unused_value, gelu_back = jax.vjp(partial(jax.nn.gelu, approximate=True), before)
    d_before = gelu_back(d_activated)[0].astype(bf16)

    projected = dot_plain(hidden, qkv_mine) + dot_plain(hidden_other, qkv_other) + qkv_bias.astype(f32)
    d_mixed = (contract_cols(branch_half, dense_mine) + contract_cols(branch_other, dense_other)).astype(bf16)
    attended, d_projected = attention(projected, d_mixed, tables, segment)

    def chunks_of(array, index):
        rows, columns = array.shape
        grouped = array.reshape(rows, columns // (2 * chunk), 2, chunk)
        return lax.dynamic_index_in_dim(grouped, index, 2, keepdims=False).reshape(rows, columns // 2)

    branch_pair = over_side(branch_half)

    def feature_sums(array):
        kept = chunks_of(array, side)
        got = over_side(chunks_of(array, 1 - side))
        own = in_order(col, kept, over_col(kept), 1)
        pair = in_order(col, got, over_col(got), 1)
        return (contract_rows(own, branch_half) + contract_rows(pair, branch_pair)).astype(bf16)

    def along_line(sums):
        depth = sums.shape[0] // line
        parts = sums.reshape(line, depth, sums.shape[1])

        def part(index):
            return lax.dynamic_index_in_dim(parts, jnp.clip(index, 0, line - 1), 0, keepdims=False).astype(f32)

        rightward, leftward = None, None
        for step in range(line - 1):
            right_part = part(line - 1 - step + place)
            left_part = part(place - (line - 1) + step)
            if step:
                right_part = right_part + rightward.astype(f32)
                left_part = left_part + leftward.astype(f32)
            to_right = [(2 * z + x, 2 * z + 2 + x) for z in range(min(step + 1, line - 1)) for x in range(2)]
            to_left = [(dp_size - 1 - p, dp_size - 1 - q) for p, q in to_right]
            rightward = lax.ppermute(right_part.astype(bf16), "dp", to_right)
            leftward = lax.ppermute(left_part.astype(bf16), "dp", to_left)
        return part(place) + rightward.astype(f32) + leftward.astype(f32)

    chunk = down_weight.shape[0] // dp_size
    grad_down = along_line(feature_sums(activated))

    chunk = up_weight.shape[0] // dp_size
    hidden_own = chunks_of(hidden, side)
    hidden_pair = over_side(chunks_of(hidden, 1 - side))

    def hidden_sums(array):
        pair = over_side(array)
        mine = (contract_rows(hidden_own, array) + contract_rows(hidden_pair, pair)).astype(bf16)
        theirs = (contract_rows(hidden_own, over_col(array)) + contract_rows(hidden_pair, over_col(pair))).astype(bf16)
        return in_order(col, along_line(mine), along_line(theirs), 1)

    grad_up = hidden_sums(d_before)
    chunk = dense_weight.shape[0] // dp_size
    grad_dense = along_line(feature_sums(attended))
    grad_qkv = hidden_sums(d_projected)

    def scatter(mine, other):
        half = mine + over_col(other.astype(bf16)).astype(f32)
        return half_at(half, row, 1) + over_row(half_at(half, 1 - row, 1).astype(bf16)).astype(f32)

    branch = scatter(
        dot_plain(attended, dense_mine) + dot_plain(activated, down_mine),
        dot_plain(attended, dense_other) + dot_plain(activated, down_other),
    )
    valid_col = is_valid.astype(f32)[:, None]
    outputs = (inputs.astype(f32) + valid_col * (branch + out_bias.astype(f32))).astype(bf16)

    d_hidden = scatter(
        contract_cols(d_projected, qkv_mine) + contract_cols(d_before, up_mine),
        contract_cols(d_projected, qkv_other) + contract_cols(d_before, up_other),
    )
    normed = (inputs.astype(f32) - average[:, None]) * scale_inv
    d_normed = d_hidden * norm_gain.astype(f32)
    row_sums = jnp.stack([jnp.sum(d_normed, axis=1), jnp.sum(d_normed * normed, axis=1)])
    row_sums = row_sums + over_row(row_sums)
    row_sums = row_sums + over_col(row_sums)
    grad_inputs = cotangent.astype(f32) + scale_inv * (
        d_normed - row_sums[0][:, None] / width - normed * row_sums[1][:, None] / width
    )

    small = [
        jnp.sum(d_hidden * normed, axis=0),
        jnp.sum(d_hidden, axis=0),
        jnp.sum(d_projected.astype(f32), axis=0),
        jnp.sum(d_before.astype(f32), axis=0),
        jnp.sum(grad_branch.astype(f32), axis=0),
    ]
    together = jnp.concatenate(small)
    bit = 1
    while bit < dp_size:
        together = together + lax.ppermute(together, "dp", [(e, e ^ bit) for e in range(dp_size)])
        bit *= 2
    ends = []
    for piece in small:
        ends.append((ends[-1] if ends else 0) + piece.shape[0])
    grad_gain, grad_shift, grad_qkv_bias, grad_up_bias, grad_out_bias = jnp.split(together, ends[:-1])
    return (
        outputs,
        grad_inputs,
        grad_gain,
        grad_shift,
        grad_qkv,
        grad_qkv_bias,
        grad_up,
        grad_up_bias,
        grad_dense,
        grad_down,
        grad_out_bias,
    )


def solution(mesh):
    in_specs = (
        P("dp", ("col", "row")),
        P(("col", "row")),
        P(("col", "row")),
        P("col", "row"),
        P(("row", "col")),
        P("col", "row"),
        P(("row", "col")),
        P("row", "col"),
        P("row", "col"),
        P(("col", "row")),
        P("dp", ("col", "row")),
        P(),
        P(),
    )
    out_specs = (
        P("dp", ("col", "row")),
        P("dp", ("col", "row")),
        P(("col", "row")),
        P(("col", "row")),
        P(("col", "dp"), "row"),
        P(("row", "col")),
        P(("col", "dp"), "row"),
        P(("row", "col")),
        P(("row", "dp"), "col"),
        P(("row", "dp"), "col"),
        P(("col", "row")),
    )
    return jax.shard_map(
        partial(on_device, mesh.shape["dp"]), mesh=mesh, in_specs=in_specs, out_specs=out_specs, check_vma=False
    )
```

```python
from functools import partial
import math

import jax
import jax.numpy as jnp
import numpy as np
from jax import lax
from jax.experimental import pallas as pl
from jax.experimental.pallas import tpu as pltpu
from jax.sharding import PartitionSpec as P

HEAD_DIM = 64
ROT = 32
HALF_ROT = ROT // 2
PAIR = 2 * HEAD_DIM
PAIR_QKV = 3 * PAIR

epsilon = 1e-05
masked_score = -1e30
rope_base = 10000.0
VMEM_LIMIT = 67_000_000
SCRATCH_LIMIT = 58 * 1024 * 1024
SENDS = 40
score_scale = HEAD_DIM ** (-0.5)
bf16 = jnp.bfloat16
f32 = jnp.float32


def layout(seq_lengths, seq_owner, device, row_count):
    owned = seq_owner == device
    lengths_owned = jnp.where(owned, seq_lengths, 0)
    seq_ends = jnp.cumsum(lengths_owned, dtype=jnp.int32)
    seq_starts = seq_ends - lengths_owned
    slot_index = jnp.arange(row_count, dtype=jnp.int32)
    segment = jnp.sum((seq_ends[None, :] <= slot_index[:, None]).astype(jnp.int32), axis=1)
    picked = jnp.arange(seq_lengths.shape[0], dtype=jnp.int32)[None, :] == segment[:, None]
    seq_begin = jnp.sum(jnp.where(picked, seq_starts[None, :], 0), axis=1)
    position = slot_index - seq_begin
    is_valid = slot_index < seq_ends[-1]
    return (segment, position, is_valid)


def rotation_tables(position):
    index_range = jnp.arange(HALF_ROT, dtype=f32)
    frequency = rope_base ** (-2.0 * index_range / ROT)
    phase = position.astype(f32)[:, None] * frequency[None, :]
    cosines, sines = jnp.cos(phase), jnp.sin(phase)
    rows = position.shape[0]
    ones = jnp.ones((rows, HEAD_DIM - ROT), f32)
    none = jnp.zeros((rows, HALF_ROT), f32)
    rest = jnp.zeros((rows, HEAD_DIM - ROT), f32)
    same = jnp.concatenate([cosines, cosines, ones], axis=1)
    from_right = jnp.concatenate([sines, none, rest], axis=1)
    from_left = jnp.concatenate([none, sines, rest], axis=1)
    return jnp.stack([same, from_right, from_left])


def turned(array):
    return jnp.swapaxes(array, 0, 1)


def contract(left, right, left_dim, right_dim):
    dims = (((left_dim,), (right_dim,)), ((), ()))
    return lax.dot_general(left, right, dims, preferred_element_type=f32)


gelu_rate = math.sqrt(2.0 / math.pi)
gelu_cube = 0.044715


def gelu(x):
    return 0.5 * x * (1.0 + jnp.tanh(gelu_rate * (x + gelu_cube * x * x * x)))


def gelu_slope(x):
    square = x * x
    bent = jnp.tanh(gelu_rate * (x + gelu_cube * x * square))
    return 0.5 * (1.0 + bent) + 0.5 * x * (1.0 - bent * bent) * (gelu_rate * (1.0 + 3.0 * gelu_cube * square))


def attention_pair(proj, mixed, tables, seg_col, seg_row):
    rows = proj.shape[0]
    block = min(256, rows)
    same, from_right, from_left = tables[0], tables[1], tables[2]

    def rotate(part, sign):
        right = jnp.concatenate([part[:, HALF_ROT:], part[:, :HALF_ROT]], axis=1)
        left = jnp.concatenate([part[:, HEAD_DIM - HALF_ROT :], part[:, : HEAD_DIM - HALF_ROT]], axis=1)
        return part * same - sign * (right * from_right) + sign * (left * from_left)

    attended_heads, grads = [], []
    for head in range(2):
        base = head * 3 * HEAD_DIM
        queries = rotate(proj[:, base : base + HEAD_DIM], 1.0).astype(bf16)
        keys = rotate(proj[:, base + HEAD_DIM : base + 2 * HEAD_DIM], 1.0).astype(bf16)
        values = proj[:, base + 2 * HEAD_DIM : base + 3 * HEAD_DIM].astype(bf16)
        d_outs = mixed[:, head * HEAD_DIM : (head + 1) * HEAD_DIM]
        outs, d_queries, d_keys, d_values = [], [], None, None
        for first in range(0, rows, block):
            last = first + block
            q, d_out = queries[first:last], d_outs[first:last]
            k, v = keys[:last], values[:last]
            row_index = first + lax.broadcasted_iota(jnp.int32, (block, last), 0)
            key_index = lax.broadcasted_iota(jnp.int32, (block, last), 1)
            allowed = (seg_col[first:last, :] == seg_row[:, :last]) & (key_index <= row_index)
            scores = jnp.where(allowed, contract(q, k, 1, 1) * score_scale, masked_score)
            weights = jnp.exp(scores - jnp.max(scores, axis=1, keepdims=True))
            probs = weights * (1.0 / jnp.sum(weights, axis=1, keepdims=True))
            probs_low = probs.astype(bf16)
            outs.append(contract(probs_low, v, 1, 0))
            d_probs = contract(d_out, v, 1, 1)
            row_dot = jnp.sum(probs * d_probs, axis=1, keepdims=True)
            d_scores = (probs * (d_probs - row_dot)).astype(bf16)
            d_queries.append(contract(d_scores, k, 1, 0))
            key_part = contract(d_scores, q, 0, 0)
            value_part = contract(probs_low, d_out, 0, 0)
            if d_keys is None:
                d_keys, d_values = key_part, value_part
            else:
                d_keys = jnp.concatenate([key_part[:first] + d_keys, key_part[first:]], axis=0)
                d_values = jnp.concatenate([value_part[:first] + d_values, value_part[first:]], axis=0)
        attended_heads.append(jnp.concatenate(outs, axis=0))
        grads.append(rotate(jnp.concatenate(d_queries, axis=0) * score_scale, -1.0))
        grads.append(rotate(d_keys * score_scale, -1.0))
        grads.append(d_values)
    attended = jnp.concatenate(attended_heads, axis=1).astype(bf16)
    return attended, jnp.concatenate(grads, axis=1).astype(bf16)


class Sizes:
    def __init__(self, dp_size, inputs, qkv_weight, up_weight, dense_weight, down_weight, seq_lengths):
        self.dp = dp_size
        self.seqs = seq_lengths.shape[0]
        self.line = dp_size // 2
        self.rows, self.quarter = inputs.shape
        self.half = up_weight.shape[0]
        self.width = 2 * self.half
        self.up_chunk = self.half // dp_size
        self.down_chunk = down_weight.shape[0] // dp_size
        self.dense_chunk = dense_weight.shape[0] // dp_size
        self.hidden = up_weight.shape[1] // 2
        self.tiles = self.hidden // self.down_chunk
        self.qkv = qkv_weight.shape[1] // 2
        self.pairs = self.qkv // PAIR_QKV
        self.features = dense_weight.shape[0] // 2


def flows_of(z):
    return dict(
        down=(z.down_chunk // z.up_chunk, z.up_chunk, z.quarter),
        up=(z.tiles, z.up_chunk, z.down_chunk),
        dense=(1, z.dense_chunk, z.quarter),
        qkv=(z.pairs, z.up_chunk, PAIR_QKV),
    )


def scratch_of(z):
    rows, q, line, tiles, pairs = z.rows, z.quarter, z.line, z.tiles, z.pairs
    up, down, dense = z.up_chunk, z.down_chunk, z.dense_chunk
    shapes = dict(
        inq=((2, 2, rows, q), bf16),
        cotq=((2, 2, rows, q), bf16),
        cotp=((2, rows, q), bf16),
        gainq=((2, 2, 16, q), f32),
        seg_col=((rows, 1), f32),
        seg_row=((1, rows), f32),
        tables=((3, rows, HEAD_DIM), f32),
        up_b=((tiles, 1, down), f32),
        qkv_b=((pairs, 1, PAIR_QKV), f32),
        sums=((1, 3 * q + z.qkv + z.hidden), f32),
        sums_got=((3, 1, 3 * q + z.qkv + z.hidden), f32),
        sums_send=((2, 1, 3 * q + z.qkv + z.hidden), f32),
        hid=((2, rows, z.half), bf16),
        hid_own=((line, rows, up), bf16),
        hid_send=((line, rows, up), bf16),
        hid_pair=((line, rows, up), bf16),
        stat=((2, rows, 1), f32),
        before=((tiles, rows, down), f32),
        act=((tiles, rows, down), bf16),
        act_own=((line, rows, down), bf16),
        act_pair=((line, rows, down), bf16),
        db_mine=((tiles, rows, down), bf16),
        db_theirs=((tiles, rows, down), bf16),
        db_mine_pair=((tiles, rows, down), bf16),
        db_theirs_pair=((tiles, rows, down), bf16),
        mixed=((pairs, rows, PAIR), bf16),
        att=((rows, z.features), bf16),
        att_part=((line, rows, dense), bf16),
        att_own=((line, rows, dense), bf16),
        att_pair=((line, rows, dense), bf16),
        dp_mine=((pairs, rows, PAIR_QKV), bf16),
        dp_theirs=((pairs, rows, PAIR_QKV), bf16),
        dp_mine_pair=((pairs, rows, PAIR_QKV), bf16),
        dp_theirs_pair=((pairs, rows, PAIR_QKV), bf16),
        weight=((2, 2, z.half, 512), bf16),
        st_down=((line, 2) + flows_of(z)["down"], bf16),
        st_up=((line, 2) + flows_of(z)["up"], bf16),
        st_dense=((line, 2) + flows_of(z)["dense"], bf16),
        st_qkv=((line, 2) + flows_of(z)["qkv"], bf16),
        got_down=(flows_of(z)["down"], bf16),
        got_up=(flows_of(z)["up"], bf16),
        got_dense=(flows_of(z)["dense"], bf16),
        got_qkv=(flows_of(z)["qkv"], bf16),
        part_send=((2, rows, q), bf16),
        part_row=((rows, q), bf16),
        out_row=((rows, q), bf16),
        dh_row=((rows, q), bf16),
        sum_send=((2, 8, rows), f32),
        sum_got=((2, 8, rows), f32),
    )
    if shapes["before"][0] != (4, rows, q):
        shapes["total"] = ((4, rows, q), f32)
    if shapes["st_up"] == shapes["st_down"]:
        del shapes["st_up"], shapes["got_up"]
    return shapes


def fits(z):
    total = 0
    for shape, kind in scratch_of(z).values():
        total += math.prod(shape[:-1]) * -(-shape[-1] // 128) * 128 * jnp.dtype(kind).itemsize
    return z.line % 2 == 0 and total <= SCRATCH_LIMIT


def layer_kernel(z, names, *refs):
    r = dict(zip(names, refs))
    rows, q, line, tiles, pairs = z.rows, z.quarter, z.line, z.tiles, z.pairs
    half_line = line // 2
    if "total" not in r:
        r["total"] = r["before"]
    r["dh_got"], r["out_got"] = r["inq"].at[1], r["cotq"].at[1]
    shared = "st_up" not in r
    if shared:
        r["st_up"], r["got_up"] = r["st_down"], r["got_down"]
    dp = lax.axis_index("dp")
    row = lax.axis_index("row")
    col = lax.axis_index("col")
    place, side = dp // 2, lax.rem(dp, 2)
    other_row, other_col, other_side = 1 - row, 1 - col, 1 - side
    to_row = {"row": other_row}
    to_col = {"col": other_col}
    to_side = {"dp": dp + 1 - 2 * side}
    MESH = pl.DeviceIdType.MESH

    marks = dict(send=0, recv=0, local=0)

    def take(kind, count):
        first = marks[kind]
        marks[kind] += count
        return first

    def remote(src, dst, send, recv, device):
        return pltpu.make_async_remote_copy(
            src_ref=src,
            dst_ref=dst,
            send_sem=r["send_sem"].at[send],
            recv_sem=r["recv_sem"].at[recv],
            device_id=device,
            device_id_type=MESH,
        )

    pending = []

    class Message:
        def __init__(self, src, dst, device, got=None):
            index = (take("send", 1), take("recv", 1))
            self.copy = lambda: remote(src, dst, *index, device)
            self.got = lambda: remote(src if got is None else got, dst if got is None else got, *index, device)

        def start(self):
            self.copy().start()
            pending.append(self)

        def wait(self):
            self.got().wait_recv()

    right, left = {"dp": dp + 2}, {"dp": dp - 2}
    has_right, has_left = place < line - 1, place > 0
    barrier = pltpu.get_barrier_semaphore()
    for device in (to_row, to_col, to_side):
        pl.semaphore_signal(barrier, inc=1, device_id=device, device_id_type=MESH)

    @pl.when(has_right)
    def _():
        pl.semaphore_signal(barrier, inc=1, device_id=right, device_id_type=MESH)

    @pl.when(has_left)
    def _():
        pl.semaphore_signal(barrier, inc=1, device_id=left, device_id_type=MESH)

    slots = lax.broadcasted_iota(jnp.int32, (8, rows), 1)

    def add_sequence(number, carry):
        end, segments, begins = carry
        start = end
        end = start + jnp.where(r["seq_owner"][number] == dp, r["seq_lengths"][number], 0)
        segments = segments + (end <= slots).astype(jnp.int32)
        begins = jnp.where((start <= slots) & (slots < end), start, begins)
        return end, segments, begins

    nothing = jnp.zeros((8, rows), jnp.int32)
    segments, begins = lax.fori_loop(0, z.seqs, add_sequence, (jnp.int32(0), nothing, nothing))[1:]
    segments = segments.astype(f32)
    r["seg_row"][...] = segments[:1]
    r["seg_col"][...] = turned(segments)[:, :1]
    cot = r["cot"]
    valid = (r["seg_col"][...] < z.seqs).astype(f32)
    r["cotq"][0, row] = cot[...] * valid.astype(bf16)

    def as_row(vector):
        return vector.astype(f32).reshape(1, vector.shape[0])

    r["gainq"][0, row] = jnp.concatenate(
        [
            jnp.broadcast_to(as_row(r["norm_gain"][...]), (8, q)),
            jnp.broadcast_to(as_row(r["norm_shift"][...]), (8, q)),
        ]
    )
    pl.semaphore_wait(barrier, 3 + has_right.astype(jnp.int32) + has_left.astype(jnp.int32))

    def gather(src, held):
        over = Message(src, held.at[0, row], to_row, held.at[0, other_row])
        across = Message(src, held.at[1, row], to_col, held.at[1, row])
        onward = Message(held.at[0, other_row], held.at[1, other_row], to_col, held.at[1, other_row])
        return over, across, onward

    in_over, in_across, in_onward = gather(r["inputs"], r["inq"])
    gain_over, gain_across, gain_onward = gather(r["gainq"].at[0, row], r["gainq"])
    cot_over, cot_across, cot_onward = gather(r["cotq"].at[0, row], r["cotq"])
    cot_side = Message(r["cotq"].at[0, row], r["cotp"].at[row], to_side)
    cot_side_onward = Message(r["cotq"].at[0, other_row], r["cotp"].at[other_row], to_side)
    hid_side = Message(r["hid_send"], r["hid_pair"], to_side)
    swaps = {
        "up": Message(r["up_w"].at[:, pl.ds(pl.multiple_of(other_col * z.hidden, 128), z.hidden)], r["up_o"], to_col, r["up_o"]),
        "qkv": Message(r["qkv_w"].at[:, pl.ds(pl.multiple_of(other_col * z.qkv, 128), z.qkv)], r["qkv_o"], to_col, r["qkv_o"]),
        "down": Message(r["down_w"].at[pl.ds(pl.multiple_of(other_col * z.hidden, 16), z.hidden), :], r["down_o"], to_col, r["down_o"]),
        "dense": Message(r["dense_w"].at[pl.ds(pl.multiple_of(other_col * z.features, 16), z.features), :], r["dense_o"], to_col, r["dense_o"]),
    }

    def local(src, dst, index):
        return pltpu.make_async_copy(src, dst, r["local_sem"].at[index])

    stream_base = take("local", 8)
    once = take("local", 4)

    in_over.start()
    gain_over.start()
    in_across.start()
    gain_across.start()
    keep_in = local(r["inputs"], r["inq"].at[0, row], once)
    keep_in.start()
    cot_side.start()
    swaps["up"].start()
    up_bias, qkv_bias = as_row(r["up_bias"][...]), as_row(r["qkv_bias"][...])
    for tile in range(tiles):
        r["up_b"][tile] = up_bias[:, tile * z.down_chunk : (tile + 1) * z.down_chunk]
    for pair in range(pairs):
        r["qkv_b"][pair] = qkv_bias[:, pair * PAIR_QKV : (pair + 1) * PAIR_QKV]
    position = turned((slots - begins).astype(f32))[:, :1]
    phase = position * r["frequency"][...]
    lane = lax.broadcasted_iota(jnp.int32, (1, HEAD_DIM), 1)
    sines = jnp.sin(phase)
    r["tables"][0] = jnp.where(lane < ROT, jnp.cos(phase), 1.0)
    r["tables"][1] = jnp.where(lane < HALF_ROT, sines, 0.0)
    r["tables"][2] = jnp.where((lane >= HALF_ROT) & (lane < ROT), sines, 0.0)
    gain_over.wait()
    gain_onward.start()
    in_over.wait()
    in_onward.start()
    cot_over.start()
    cot_across.start()
    keep_in.wait()
    gain_across.wait()
    gain_onward.wait()
    in_across.wait()
    in_onward.wait()

    block = min(64, rows)

    def norm_rows(step, carry):
        at = pl.ds(pl.multiple_of(step * block, block), block)
        parts = [r["inq"][h, p, at].astype(f32) for h in range(2) for p in range(2)]
        total = parts[0] + parts[1] + parts[2] + parts[3]
        squares = parts[0] * parts[0] + parts[1] * parts[1] + parts[2] * parts[2] + parts[3] * parts[3]
        average = jnp.sum(total, axis=1, keepdims=True) / z.width
        variance = jnp.sum(squares, axis=1, keepdims=True) / z.width - average * average
        scale_inv = lax.rsqrt(variance + epsilon)
        r["stat"][0, at] = average
        r["stat"][1, at] = scale_inv
        for h in range(2):
            for p in range(2):
                normed = (parts[2 * h + p] - average) * scale_inv
                gain, shift = r["gainq"][h, p, 0:1, :], r["gainq"][h, p, 8:9, :]
                r["hid"][h, at, p * q : (p + 1) * q] = (normed * gain + shift).astype(bf16)
        return carry

    lax.fori_loop(0, rows // block, norm_rows, 0)
    for c in range(line):
        even = r["hid"][0, :, 2 * c * z.up_chunk : (2 * c + 1) * z.up_chunk]
        odd = r["hid"][0, :, (2 * c + 1) * z.up_chunk : (2 * c + 2) * z.up_chunk]
        r["hid_own"][c] = jnp.where(side == 0, even, odd)
        r["hid_send"][c] = jnp.where(side == 0, odd, even)

    def stream(count, copies, work):
        for copy in copies(jnp.int32(0), jnp.int32(0)):
            copy.start()

        def one(step, carry):
            slot = lax.rem(step, 2)

            @pl.when(step + 1 < count)
            def _():
                for copy in copies(step + 1, 1 - slot):
                    copy.start()

            for copy in copies(step, slot):
                copy.wait()
            work(step, slot)
            return carry

        lax.fori_loop(0, count, one, 0)

    def column_tiles(name, each, tile_of=lambda step: step):
        def copies(step, slot):
            tile = tile_of(step)
            mine = r[name + "_w"].at[:, pl.ds(pl.multiple_of((col * r[name + "_o"].shape[1]) + tile * each, 128), each)]
            theirs = r[name + "_o"].at[:, pl.ds(pl.multiple_of(tile * each, 128), each)]
            return [
                local(mine, r["weight"].at[slot, 0, :, :each], stream_base + slot * 4),
                local(theirs, r["weight"].at[slot, 1, :, :each], stream_base + slot * 4 + 1),
            ]

        return copies

    def row_tiles(name, each, tile_of=lambda step: step):
        def copies(step, slot):
            tile = tile_of(step)
            found = []
            for h in range(2):
                start = tile * each + (col * r[name + "_o"].shape[0] if h == 0 else 0)
                src = r[name + ("_w" if h == 0 else "_o")]
                for p in range(2):
                    found.append(
                        local(
                            src.at[pl.ds(pl.multiple_of(start, 16), each), p * q : (p + 1) * q],
                            r["weight"].at[slot, h, p * q : p * q + each, :],
                            stream_base + slot * 4 + 2 * h + p,
                        )
                    )
            return found

        return copies

    def rank_of(j):
        return jnp.where(col == 1, half_line - 1 - j, j)

    def tile_at(step):
        later = (step >= half_line).astype(jnp.int32)
        return 2 * rank_of(step - later * half_line) + jnp.where(later == 1, side, other_side)

    act_side_send, act_side_recv = take("send", half_line), take("recv", half_line)
    act_col_send, act_col_recv = take("send", half_line), take("recv", half_line)
    act_on_send, act_on_recv = take("send", half_line), take("recv", half_line)

    def act_side(j):
        tile, slot = 2 * rank_of(j) + other_side, col * half_line + rank_of(j)
        return remote(r["act"].at[tile], r["act_pair"].at[slot], act_side_send + j, act_side_recv + j, to_side)

    def act_col(j):
        slot = col * half_line + rank_of(j)
        return remote(r["act_own"].at[slot], r["act_own"].at[slot], act_col_send + j, act_col_recv + j, to_col)

    def act_on(j):
        slot = col * half_line + rank_of(j)
        return remote(r["act_pair"].at[slot], r["act_pair"].at[slot], act_on_send + j, act_on_recv + j, to_col)

    def up_work(step, slot):
        tile = tile_at(step)
        before = contract(r["hid"][0], r["weight"][slot, 0, :, : z.down_chunk], 1, 0)
        before = before + contract(r["hid"][1], r["weight"][slot, 1, :, : z.down_chunk], 1, 0)
        before = before + r["up_b"][tile]
        r["before"][tile] = before
        activated = gelu(before).astype(bf16)
        r["act"][tile] = activated

        @pl.when(step < half_line)
        def _():
            act_side(step).start()

        @pl.when(step >= half_line)
        def _():
            j = step - half_line
            r["act_own"][col * half_line + rank_of(j)] = activated
            act_col(j).start()

    swaps["down"].start()
    swaps["up"].wait()
    stream(tiles, column_tiles("up", z.down_chunk, tile_at), up_work)

    cot_over.wait()
    cot_onward.start()
    cot_side_onward.start()
    swaps["qkv"].start()
    swaps["dense"].start()
    cot_across.wait()
    cot_onward.wait()
    swaps["down"].wait()

    def each_side(name, count):
        side_send, side_recv = take("send", count), take("recv", count)
        col_send, col_recv = take("send", count), take("recv", count)
        on_send, on_recv = take("send", count), take("recv", count)
        mine, theirs = r[name + "_mine"], r[name + "_theirs"]
        mine_pair, theirs_pair = r[name + "_mine_pair"], r[name + "_theirs_pair"]

        def to_side_peer(k):
            return remote(mine.at[k], mine_pair.at[k], side_send + k, side_recv + k, to_side)

        def to_col_peer(k):
            return remote(mine.at[k], theirs.at[k], col_send + k, col_recv + k, to_col)

        def onward(k):
            return remote(mine_pair.at[k], theirs_pair.at[k], on_send + k, on_recv + k, to_col)

        return to_side_peer, to_col_peer, onward

    db_side, db_col, db_on = each_side("db", tiles)
    dp_side, dp_col, dp_on = each_side("dp", pairs)

    def over_weight_rows(slot, each, lefts):
        total = None
        for h in range(2):
            for p in range(2):
                part = contract(lefts(h, p), r["weight"][slot, h, p * q : p * q + each, :], 1, 1)
                total = part if total is None else total + part
        return total

    def down_work(step, slot):
        tile = tile_at(step)
        d_activated = over_weight_rows(slot, z.down_chunk, lambda h, p: r["cotq"][h, p])
        d_before = (d_activated * gelu_slope(r["before"][tile])).astype(bf16)
        r["db_mine"][tile] = d_before
        sums = jnp.sum(d_before.astype(f32), axis=0, keepdims=True)
        r["sums"][:, pl.ds(pl.multiple_of(2 * q + z.qkv + tile * z.down_chunk, 128), z.down_chunk)] = sums
        db_col(tile).start()

    stream(tiles, row_tiles("down", z.down_chunk, tile_at), down_work)

    def loop(first, last, work):
        def one(k, carry):
            work(k)
            return carry

        lax.fori_loop(first, last, one, 0)

    def pass_on(got, onward):
        def work(k):
            got(k).wait_recv()
            onward(k).start()

        return work

    def waits(*copies):
        def work(k):
            for copy in copies:
                copy(k).wait_recv()

        return work

    class Flow:
        def __init__(self, name, own_rows, pair_rows, own_columns, pair_columns, split=False, by_col=False, earlier=None):
            self.name, self.split, self.by_col, self.earlier = name, split, by_col, earlier
            self.own_rows, self.pair_rows = own_rows, pair_rows
            self.own_columns, self.pair_columns = own_columns, pair_columns
            self.stage, self.land, self.got = r["st_" + name], r["land_" + name], r["got_" + name]
            self.count, self.depth = flows_of(z)[name][:2]
            self.send = take("send", 2 * line)
            self.recv = take("recv", 2 * (line + 2))
            self.local = take("local", 1)
            self.later = False

        def half(self, group):
            return jnp.where(col == 0, group, 1 - group) if self.by_col else group

        def copy(self, chunk, group, slot, device):
            half = self.half(group)
            return remote(
                self.stage.at[chunk, half],
                self.land.at[slot, half],
                self.send + 2 * chunk + group,
                self.recv + 2 * slot + group,
                device,
            )

        def sums(self, chunk):
            own, pair = turned(self.own_rows[chunk]), turned(self.pair_rows[chunk])

            def tile_sums(group, tile):
                at = slice(tile * self.depth, (tile + 1) * self.depth) if self.split else slice(None)
                column = 0 if self.split else tile
                part = contract(own[at], self.own_columns(group, column), 1, 0)
                return part + contract(pair[at], self.pair_columns(group, column), 1, 0)

            return tile_sums

        def add(self, rank, chunk, slot, device):
            tile_sums = self.sums(chunk)
            if self.earlier is not None:
                for group in range(2):
                    self.earlier.copy(chunk, group, chunk, device).wait_send()
            for group in range(2):
                half = self.half(group)

                @pl.when(rank > 0)
                def _():
                    self.copy(chunk, group, chunk, device).wait_recv()
                    bring = local(self.land.at[chunk, half], self.got, self.local)
                    bring.start()
                    bring.wait()

                @pl.when(rank == 0)
                def _():
                    self.got[...] = jnp.zeros_like(self.got)

                for tile in range(self.count):
                    whole = tile_sums(group, tile) + self.got[tile].astype(f32)
                    self.stage[chunk, half, tile] = whole.astype(bf16)
                self.copy(chunk, group, slot, device).start()

        def start(self):
            for way, end, device in ((0, 0, right), (1, line - 1, left)):

                @pl.when(place == end)
                def _():
                    chunk = (line - 1) * (1 - way)
                    last = chunk == end + 1 - 2 * way
                    self.add(jnp.int32(0), chunk, line + way if last else chunk, device)

        def step(self, number):
            def one(way, carry):
                rightward = way == 0
                rank = jnp.where(rightward, place, line - 1 - place)
                chunk = jnp.where(rightward, line - 1 - number + place, place - (line - 1) + number)
                slot = jnp.where(chunk == place + 1 - 2 * way, line + way, chunk)
                device = {"dp": dp + 2 - 4 * way}

                @pl.when((rank <= number) & (rank < line - 1))
                def _():
                    self.add(rank, chunk, slot, device)

                return carry

            lax.fori_loop(0, 2, one, 0)

        def steps(self, first, last):
            if last - first == 1:
                self.step(first)
            elif last > first:
                loop(first, last, self.step)

        def own(self):
            if self.earlier is not None:
                self.earlier.out.wait()
                self.earlier.later = True
            tile_sums = self.sums(place)
            for group in range(2):
                for tile in range(self.count):
                    self.stage[place, self.half(group), tile] = tile_sums(group, tile).astype(bf16)
            self.out = local(self.stage.at[place], r["own_" + self.name], self.local)
            self.out.start()

        def finish(self):
            if not self.later:
                self.out.wait()
            for group in range(2):

                @pl.when(has_left)
                def _():
                    self.copy(place, group, line, left).wait_recv()

                @pl.when(has_right)
                def _():
                    self.copy(place, group, line + 1, right).wait_recv()

            def sent(chunk):
                @pl.when(chunk != place)
                def _():
                    for group in range(2):
                        self.copy(chunk, group, chunk, right).wait_send()

            if not self.later:
                loop(0, line, sent)

    cot_own_tile = lambda group, tile: r["cotq"][0, group]
    cot_pair_tile = lambda group, tile: r["cotp"][group]
    down = Flow("down", r["act_own"], r["act_pair"], cot_own_tile, cot_pair_tile, split=True)
    up = Flow(
        "up",
        r["hid_own"],
        r["hid_pair"],
        lambda group, tile: r[("db_mine", "db_theirs")[group]][tile],
        lambda group, tile: r[("db_mine_pair", "db_theirs_pair")[group]][tile],
        by_col=True,
        earlier=down if shared else None,
    )
    dense = Flow("dense", r["att_own"], r["att_pair"], cot_own_tile, cot_pair_tile)
    qkv = Flow(
        "qkv",
        r["hid_own"],
        r["hid_pair"],
        lambda group, tile: r[("dp_mine", "dp_theirs")[group]][tile],
        lambda group, tile: r[("dp_mine_pair", "dp_theirs_pair")[group]][tile],
        by_col=True,
    )
    cuts = (0, 1, line // 2, line - 1)

    loop(0, 1, pass_on(act_side, act_on))
    loop(0, 1, waits(act_col, act_on))
    cot_side.wait()
    cot_side_onward.wait()
    down.start()
    hid_side.start()

    def send_side(k):
        db_side(k).start()

    loop(0, tiles, send_side)

    swaps["qkv"].wait()

    def qkv_work(step, slot):
        part = contract(r["hid"][0], r["weight"][slot, 0, :, :PAIR_QKV], 1, 0)
        part = part + contract(r["hid"][1], r["weight"][slot, 1, :, :PAIR_QKV], 1, 0)
        r["total"][step, :, :PAIR_QKV] = part + r["qkv_b"][step]

    stream(pairs, column_tiles("qkv", PAIR_QKV), qkv_work)
    swaps["dense"].wait()

    def dense_work(step, slot):
        d_mixed = over_weight_rows(slot, z.features, lambda h, p: r["cotq"][h, p]).astype(bf16)
        for pair in range(pairs):
            r["mixed"][pair] = d_mixed[:, pair * PAIR : (pair + 1) * PAIR]

    stream(1, row_tiles("dense", z.features), dense_work)
    loop(1, half_line, pass_on(act_side, act_on))
    loop(1, half_line, waits(act_col, act_on))
    down.steps(cuts[1], cuts[2])

    att_side_send, att_side_recv = take("send", half_line), take("recv", half_line)
    att_col_send, att_col_recv = take("send", half_line), take("recv", half_line)
    att_on_send, att_on_recv = take("send", half_line), take("recv", half_line)

    def att_side(k):
        slot = col * half_line + k
        return remote(
            r["att_part"].at[2 * k + other_side], r["att_pair"].at[slot], att_side_send + k, att_side_recv + k, to_side
        )

    def att_col(k):
        slot = col * half_line + k
        return remote(r["att_own"].at[slot], r["att_own"].at[slot], att_col_send + k, att_col_recv + k, to_col)

    def att_on(k):
        slot = col * half_line + k
        return remote(r["att_pair"].at[slot], r["att_pair"].at[slot], att_on_send + k, att_on_recv + k, to_col)

    def head_pair(pair):
        attended, d_projected = attention_pair(
            r["total"][pair, :, :PAIR_QKV], r["mixed"][pair], r["tables"], r["seg_col"][...], r["seg_row"][...]
        )
        r["dp_mine"][pair] = d_projected
        dp_side(pair).start()
        dp_col(pair).start()
        sums = jnp.sum(d_projected.astype(f32), axis=0, keepdims=True)
        r["sums"][:, pl.ds(pl.multiple_of(2 * q + pair * PAIR_QKV, 128), PAIR_QKV)] = sums
        r["att"][:, pl.ds(pl.multiple_of(pair * PAIR, PAIR), PAIR)] = attended
        each = PAIR // z.dense_chunk
        for part in range(each):
            chunk = pair * each + part
            k = chunk // 2
            piece = attended[:, part * z.dense_chunk : (part + 1) * z.dense_chunk]

            @pl.when(lax.rem(chunk, 2) == side)
            def _():
                r["att_own"][col * half_line + k] = piece
                att_col(k).start()

            @pl.when(lax.rem(chunk, 2) == other_side)
            def _():
                r["att_part"][chunk] = piece
                att_side(k).start()

    loop(0, pairs // 2, head_pair)
    down.steps(cuts[2], cuts[3])
    loop(pairs // 2, pairs, head_pair)

    def scatter(name, total, earlier=None):
        across = Message(r["part_send"], r[name + "_got"], to_col)
        over = Message(r["part_row"], r[name + "_row"], to_row)

        def free(message):
            message.copy().wait_send()
            pending.remove(message)

        def first():
            if earlier is not None:
                free(earlier[0])
            for p in range(2):
                r["part_send"][p] = total[2 + p].astype(bf16)
            across.start()

        def second():
            across.wait()
            if earlier is not None:
                free(earlier[1])
            for p in range(2):
                total[p] = total[p] + r[name + "_got"][p].astype(f32)
            r["part_row"][...] = total[other_row].astype(bf16)
            over.start()

        def third():
            over.wait()
            return total[row] + r[name + "_row"][...].astype(f32)

        return first, second, third, (across, over)

    total = r["total"]

    def down_out(step, slot):
        for h in range(2):
            for p in range(2):
                part = contract(r["act"][step], r["weight"][slot, h, p * q : p * q + z.down_chunk, :], 1, 0)

                @pl.when(step == 0)
                def _():
                    total[2 * h + p] = part

                @pl.when(step > 0)
                def _():
                    total[2 * h + p] = total[2 * h + p] + part

    def dense_out(step, slot):
        for h in range(2):
            for p in range(2):
                part = contract(r["att"][...], r["weight"][slot, h, p * q : p * q + z.features, :], 1, 0)
                total[2 * h + p] = total[2 * h + p] + part

    def up_back(step, slot):
        for h in range(2):
            for p in range(2):
                part = contract(r["db_mine"][step], r["weight"][slot, h, p * q : (p + 1) * q, : z.down_chunk], 1, 1)

                @pl.when(step == 0)
                def _():
                    total[2 * h + p] = part

                @pl.when(step > 0)
                def _():
                    total[2 * h + p] = total[2 * h + p] + part

    def qkv_back(step, slot):
        for h in range(2):
            for p in range(2):
                part = contract(r["dp_mine"][step], r["weight"][slot, h, p * q : (p + 1) * q, :PAIR_QKV], 1, 1)
                total[2 * h + p] = total[2 * h + p] + part

    stream(tiles, column_tiles("up", z.down_chunk), up_back)
    stream(pairs, column_tiles("qkv", PAIR_QKV), qkv_back)
    dh_first, dh_second, dh_third, dh_messages = scatter("dh", total)
    dh_first()
    hid_side.wait()
    loop(0, tiles, pass_on(db_side, db_on))
    loop(0, tiles, waits(db_col, db_on))
    up.steps(cuts[0], cuts[1])
    dh_second()
    up.steps(cuts[1], cuts[2])

    d_hidden = dh_third()
    r["grad_inputs"][...] = d_hidden
    own_in = r["inq"].at[0, row]
    gain = r["gainq"][0, row, 0:1, :]
    sums_row = Message(r["sum_send"].at[0], r["sum_got"].at[0], to_row)
    sums_col = Message(r["sum_send"].at[1], r["sum_got"].at[1], to_col)
    normed = (own_in[...].astype(f32) - r["stat"][0]) * r["stat"][1]
    d_normed = d_hidden * gain
    lane = lax.broadcasted_iota(jnp.int32, (rows, 128), 1)
    one = jnp.sum(d_normed, axis=1, keepdims=True)
    two = jnp.sum(d_normed * normed, axis=1, keepdims=True)
    packed = jnp.where(lane == 0, one, jnp.where(lane == 1, two, 0.0))
    r["sum_send"][0] = turned(packed)[:8]
    sums_row.start()
    r["sums"][:, 0:q] = jnp.sum(d_hidden * normed, axis=0, keepdims=True)
    r["sums"][:, q : 2 * q] = jnp.sum(d_hidden, axis=0, keepdims=True)
    r["sums"][:, 2 * q + z.qkv + z.hidden :] = jnp.sum(r["cotq"][0, row].astype(f32), axis=0, keepdims=True)
    small_side = Message(r["sums"], r["sums_got"].at[0], to_side)
    small_side.start()

    stream(tiles, row_tiles("down", z.down_chunk), down_out)
    stream(1, row_tiles("dense", z.features), dense_out)
    out_first, out_second, out_third, out_messages = scatter("out", total, dh_messages)
    out_first()
    sums_row.wait()
    r["sum_send"][1] = r["sum_send"][0] + r["sum_got"][0]
    sums_col.start()
    up.steps(cuts[2], cuts[3])
    out_second()
    sums_col.wait()
    both = r["sum_send"][1] + r["sum_got"][1]
    spread = turned(jnp.concatenate([both, jnp.zeros((120, rows), f32)], axis=0))
    part_one, part_two = spread[:, 0:1] / z.width, spread[:, 1:2] / z.width
    normed = (own_in[...].astype(f32) - r["stat"][0]) * r["stat"][1]
    d_normed = r["grad_inputs"][...] * gain
    r["grad_inputs"][...] = cot[...].astype(f32) + r["stat"][1] * (d_normed - part_one - normed * part_two)

    small_send, small_recv = take("send", 2), take("recv", 2)

    def small(way, device):
        return remote(r["sums_send"].at[way], r["sums_got"].at[1 + way], small_send + way, small_recv + way, device)

    def hop(number):
        for way, rank, device, last in ((0, place, right, has_right), (1, line - 1 - place, left, has_left)):

            @pl.when((rank == number) & last)
            def _():
                @pl.when(rank == 0)
                def _():
                    r["sums_send"][way] = r["sums"][...]

                @pl.when(rank > 0)
                def _():
                    small(way, device).wait_recv()
                    r["sums_send"][way] = r["sums"][...] + r["sums_got"][1 + way]

                small(way, device).start()

    def hops(first, last):
        if last - first == 1:
            hop(first)
        elif last > first:
            loop(first, last, hop)

    loop(0, pairs, pass_on(dp_side, dp_on))
    loop(0, half_line, pass_on(att_side, att_on))
    loop(0, half_line, waits(att_col, att_on))
    loop(0, pairs, waits(dp_col, dp_on))
    dense.steps(cuts[0], cuts[1])
    qkv.steps(cuts[0], cuts[1])
    branch = out_third()
    bias = as_row(r["out_bias"][...])
    valid = (r["seg_col"][...] < z.seqs).astype(f32)
    r["outputs"][...] = (r["inq"][0, row].astype(f32) + valid * (branch + bias)).astype(bf16)
    small_side.wait()
    small_side.copy().wait_send()
    pending.remove(small_side)
    r["sums"][...] = r["sums"][...] + r["sums_got"][0]
    hops(cuts[0], cuts[1])
    down.own()
    dense.steps(cuts[1], cuts[2])
    qkv.steps(cuts[1], cuts[2])
    hops(cuts[1], cuts[2])
    up.own()
    dense.steps(cuts[2], cuts[3])
    qkv.steps(cuts[2], cuts[3])
    hops(cuts[2], cuts[3])
    dense.own()
    qkv.own()

    r["small"][...] = r["sums"][...]

    @pl.when(place == line - 1)
    def _():
        small(0, left).wait_recv()

    @pl.when(place == 0)
    def _():
        small(1, right).wait_recv()

    @pl.when(has_left)
    def _():
        r["small"][...] = r["small"][...] + r["sums_got"][1]

    @pl.when(has_right)
    def _():
        r["small"][...] = r["small"][...] + r["sums_got"][2]

    @pl.when(has_right)
    def _():
        small(0, right).wait_send()

    @pl.when(has_left)
    def _():
        small(1, left).wait_send()

    for flow in (down, up, dense, qkv):
        flow.finish()
    for message in pending:
        message.copy().wait_send()

    def sent(*copies):
        def work(k):
            for copy in copies:
                copy(k).wait_send()

        return work

    loop(0, half_line, sent(act_side, act_col, act_on, att_side, att_col, att_on))
    loop(0, tiles, sent(db_side, db_col, db_on))
    loop(0, pairs, sent(dp_side, dp_col, dp_on))
    assert marks["send"] <= SENDS * line and marks["recv"] <= SENDS * line and marks["local"] <= 16


def on_device(
    dp_size,
    inputs,
    norm_gain,
    norm_shift,
    qkv_weight,
    qkv_bias,
    up_weight,
    up_bias,
    dense_weight,
    down_weight,
    out_bias,
    cotangent,
    seq_lengths,
    seq_owner,
):
    z = Sizes(dp_size, inputs, qkv_weight, up_weight, dense_weight, down_weight, seq_lengths)
    if not fits(z):
        return on_device_plain(
            dp_size,
            inputs,
            norm_gain,
            norm_shift,
            qkv_weight,
            qkv_bias,
            up_weight,
            up_bias,
            dense_weight,
            down_weight,
            out_bias,
            cotangent,
            seq_lengths,
            seq_owner,
        )
    rows, q, line = z.rows, z.quarter, z.line
    lane_rate = np.zeros((1, HEAD_DIM), np.float32)
    lane_rate[0, :ROT] = rope_base ** (-2.0 * (np.arange(ROT) % HALF_ROT) / ROT)
    operands = dict(
        inputs=(inputs, pl.ANY),
        cot=(cotangent, pltpu.VMEM),
        norm_gain=(norm_gain, pltpu.VMEM),
        norm_shift=(norm_shift, pltpu.VMEM),
        qkv_bias=(qkv_bias, pltpu.VMEM),
        up_bias=(up_bias, pltpu.VMEM),
        out_bias=(out_bias, pltpu.VMEM),
        frequency=(jnp.asarray(lane_rate), pltpu.VMEM),
        seq_lengths=(seq_lengths, pltpu.SMEM),
        seq_owner=(seq_owner, pltpu.SMEM),
        up_w=(up_weight, pl.ANY),
        down_w=(down_weight, pl.ANY),
        qkv_w=(qkv_weight, pl.ANY),
        dense_w=(dense_weight, pl.ANY),
    )
    results = dict(
        outputs=((rows, q), bf16, pltpu.VMEM),
        grad_inputs=((rows, q), f32, pltpu.VMEM),
        small=((1, 3 * q + z.qkv + z.hidden), f32, pltpu.VMEM),
        up_o=((z.half, z.hidden), bf16, pl.ANY),
        down_o=((z.hidden, z.half), bf16, pl.ANY),
        qkv_o=((z.half, z.qkv), bf16, pl.ANY),
        dense_o=((z.features, z.half), bf16, pl.ANY),
    )
    for name, shape in flows_of(z).items():
        results["land_" + name] = ((line + 2, 2) + shape, bf16, pl.ANY)
        results["own_" + name] = ((2,) + shape, bf16, pl.ANY)
    scratch = scratch_of(z)
    names = list(operands) + list(results) + list(scratch) + ["send_sem", "recv_sem", "local_sem"]
    found = pl.pallas_call(
        partial(layer_kernel, z, names),
        in_specs=[pl.BlockSpec(memory_space=space) for value, space in operands.values()],
        out_specs=[pl.BlockSpec(memory_space=space) for shape, kind, space in results.values()],
        out_shape=[jax.ShapeDtypeStruct(shape, kind) for shape, kind, space in results.values()],
        scratch_shapes=[pltpu.VMEM(shape, kind) for shape, kind in scratch.values()]
        + [pltpu.SemaphoreType.DMA((SENDS * line,)), pltpu.SemaphoreType.DMA((SENDS * line,)), pltpu.SemaphoreType.DMA((16,))],
        compiler_params=pltpu.CompilerParams(
            collective_id=0, has_side_effects=True, vmem_limit_bytes=VMEM_LIMIT
        ),
        name="layer",
    )(*[value for value, space in operands.values()])
    got = dict(zip(results, found))
    big, small = finish(z, got)
    return (
        big["outputs"],
        big["grad_inputs"],
        small["gain"],
        small["shift"],
        big["qkv"],
        small["qkv"],
        big["up"],
        small["up"],
        big["dense"],
        big["down"],
        small["out"],
    )


def finish(z, got):
    line, steps = z.line, 8
    flows = flows_of(z)
    names = list(flows)
    pieces = dict(gain=z.quarter, shift=z.quarter, qkv=z.qkv, up=z.hidden, out=z.quarter)

    def kernel(*refs):
        place = lax.axis_index("dp") // 2
        fed = refs[: 3 * len(names) + 3]
        made = refs[3 * len(names) + 3 :]
        for index in range(len(names)):
            own, from_left, from_right = (ref[...].astype(f32) for ref in fed[3 * index : 3 * index + 3])
            total = own + jnp.where(place > 0, from_left, 0.0) + jnp.where(place < line - 1, from_right, 0.0)
            made[index][...] = total.reshape(made[index].shape)
        outputs, grad_inputs, small = fed[3 * len(names) :]
        made[len(names)][...] = outputs[...]
        made[len(names) + 1][...] = grad_inputs[...]

        @pl.when(pl.program_id(0) == 0)
        def _():
            start = 0
            for index, width in enumerate(pieces.values()):
                made[len(names) + 2 + index][...] = small[:, start : start + width].reshape(width)
                start += width

    in_specs, out_specs, out_shape, fed = [], [], [], []
    for name in names:
        count, depth, each = flows[name]
        group = count // (steps // 2) or 1

        def tile_index(step, name=name):
            half, tile = step // (steps // 2), lax.rem(step, steps // 2)
            return half, tile if flows[name][0] >= steps // 2 else 0

        block = (None, group, depth, each)
        land_block = (None, None, group, depth, each)
        in_specs.append(pl.BlockSpec(block, lambda i, f=tile_index: (*f(i), 0, 0)))
        in_specs.append(pl.BlockSpec(land_block, lambda i, f=tile_index: (line, *f(i), 0, 0)))
        in_specs.append(pl.BlockSpec(land_block, lambda i, f=tile_index: (line + 1, *f(i), 0, 0)))
        fed += [got["own_" + name], got["land_" + name], got["land_" + name]]
        if name == "down":
            out_shape.append(jax.ShapeDtypeStruct((count * depth, 2 * each), f32))
            out_specs.append(pl.BlockSpec((group * depth, each), lambda i, f=tile_index: f(i)[::-1]))
        else:
            assert group == 1
            out_shape.append(jax.ShapeDtypeStruct((depth, 2 * count * each), f32))
            out_specs.append(
                pl.BlockSpec((depth, each), lambda i, f=tile_index, count=count: (0, f(i)[0] * count + f(i)[1]))
            )
    for name in ("outputs", "grad_inputs"):
        rows, columns = got[name].shape
        spec = pl.BlockSpec((rows // steps, columns), lambda i: (i, 0))
        in_specs.append(spec)
        out_specs.append(spec)
        out_shape.append(jax.ShapeDtypeStruct((rows, columns), got[name].dtype))
        fed.append(got[name])
    in_specs.append(pl.BlockSpec(memory_space=pltpu.VMEM))
    fed.append(got["small"])
    for width in pieces.values():
        out_specs.append(pl.BlockSpec(memory_space=pltpu.VMEM))
        out_shape.append(jax.ShapeDtypeStruct((width,), f32))
    made = pl.pallas_call(
        kernel, grid=(steps,), in_specs=in_specs, out_specs=out_specs, out_shape=out_shape, name="finish"
    )(*fed)
    big = dict(zip(names + ["outputs", "grad_inputs"], made))
    return big, dict(zip(pieces, made[len(names) + 2 :]))


def attention_kernel(proj_ref, mixed_ref, tables_ref, seg_col_ref, seg_row_ref, attended_ref, grad_ref):
    attended_ref[...], grad_ref[...] = attention_pair(
        proj_ref[...], mixed_ref[...], tables_ref, seg_col_ref[...], seg_row_ref[...]
    )


def attention(projected, mixed, tables, segment):
    rows, width = projected.shape
    pairs = width // PAIR_QKV
    return pl.pallas_call(
        attention_kernel,
        grid=(pairs,),
        in_specs=[
            pl.BlockSpec((rows, PAIR_QKV), lambda i: (0, i)),
            pl.BlockSpec((rows, PAIR), lambda i: (0, i)),
            pl.BlockSpec((3, rows, HEAD_DIM), lambda i: (0, 0, 0)),
            pl.BlockSpec((rows, 1), lambda i: (0, 0)),
            pl.BlockSpec((1, rows), lambda i: (0, 0)),
        ],
        out_specs=[
            pl.BlockSpec((rows, PAIR), lambda i: (0, i)),
            pl.BlockSpec((rows, PAIR_QKV), lambda i: (0, i)),
        ],
        out_shape=[
            jax.ShapeDtypeStruct((rows, pairs * PAIR), bf16),
            jax.ShapeDtypeStruct((rows, width), bf16),
        ],
        compiler_params=pltpu.CompilerParams(vmem_limit_bytes=48 * 1024 * 1024),
        cost_estimate=pl.CostEstimate(
            flops=14 * 2 * pairs * rows * rows * HEAD_DIM * 2,
            bytes_accessed=rows * width * 7,
            transcendentals=2 * pairs * rows * rows,
        ),
        name="attention",
    )(projected, mixed, tables, segment[:, None], segment[None, :])


def dot_plain(left, right):
    return jnp.dot(left, right, preferred_element_type=f32)


def contract_rows(left, right):
    return lax.dot_general(left, right, (((0,), (0,)), ((), ())), preferred_element_type=f32)


def contract_cols(left, right):
    return lax.dot_general(left, right, (((1,), (1,)), ((), ())), preferred_element_type=f32)


def on_device_plain(
    dp_size,
    inputs,
    norm_gain,
    norm_shift,
    qkv_weight,
    qkv_bias,
    up_weight,
    up_bias,
    dense_weight,
    down_weight,
    out_bias,
    cotangent,
    seq_lengths,
    seq_owner,
):
    row_count = inputs.shape[0]
    line = dp_size // 2
    device = lax.axis_index("dp")
    place = device // 2
    side = device % 2
    row = lax.axis_index("row")
    col = lax.axis_index("col")

    over_row = partial(lax.ppermute, axis_name="row", perm=[(0, 1), (1, 0)])
    over_col = partial(lax.ppermute, axis_name="col", perm=[(0, 1), (1, 0)])
    over_side = partial(lax.ppermute, axis_name="dp", perm=[(e, e ^ 1) for e in range(dp_size)])

    def in_order(index, mine, other, axis):
        first = jnp.where(index == 0, mine, other)
        second = jnp.where(index == 0, other, mine)
        return jnp.concatenate([first, second], axis=axis)

    def half_at(array, index, axis):
        width = array.shape[axis] // 2
        return lax.dynamic_slice_in_dim(array, index * width, width, axis)

    segment, position, is_valid = layout(seq_lengths, seq_owner, device, row_count)
    tables = rotation_tables(position)

    gains = jnp.stack([norm_gain, norm_shift])
    grad_branch = cotangent * is_valid.astype(bf16)[:, None]
    inputs_half = in_order(row, inputs, over_row(inputs), 1)
    gains_half = in_order(row, gains, over_row(gains), 1)
    inputs_other = over_col(inputs_half)
    gains_other = over_col(gains_half)
    branch_half = in_order(row, grad_branch, over_row(grad_branch), 1)
    branch_other = over_col(branch_half)

    up_mine, up_other = half_at(up_weight, col, 1), over_col(half_at(up_weight, 1 - col, 1))
    down_mine, down_other = half_at(down_weight, col, 0), over_col(half_at(down_weight, 1 - col, 0))
    qkv_mine, qkv_other = half_at(qkv_weight, col, 1), over_col(half_at(qkv_weight, 1 - col, 1))
    dense_mine, dense_other = half_at(dense_weight, col, 0), over_col(half_at(dense_weight, 1 - col, 0))

    width = 4 * inputs.shape[1]
    source, source_other = inputs_half.astype(f32), inputs_other.astype(f32)
    average = (jnp.sum(source, axis=1) + jnp.sum(source_other, axis=1)) / width
    square = (jnp.sum(source * source, axis=1) + jnp.sum(source_other * source_other, axis=1)) / width
    scale_inv = lax.rsqrt(square - average * average + epsilon)[:, None]

    def hidden_of(rows_in, gain_pair):
        normed = (rows_in - average[:, None]) * scale_inv
        pair = gain_pair.astype(f32)
        return (normed * pair[0] + pair[1]).astype(bf16)

    hidden, hidden_other = hidden_of(source, gains_half), hidden_of(source_other, gains_other)

    before = dot_plain(hidden, up_mine) + dot_plain(hidden_other, up_other) + up_bias.astype(f32)
    activated = jax.nn.gelu(before, approximate=True).astype(bf16)
    d_activated = contract_cols(branch_half, down_mine) + contract_cols(branch_other, down_other)
    unused_value, gelu_back = jax.vjp(partial(jax.nn.gelu, approximate=True), before)
    d_before = gelu_back(d_activated)[0].astype(bf16)

    projected = dot_plain(hidden, qkv_mine) + dot_plain(hidden_other, qkv_other) + qkv_bias.astype(f32)
    d_mixed = (contract_cols(branch_half, dense_mine) + contract_cols(branch_other, dense_other)).astype(bf16)
    attended, d_projected = attention(projected, d_mixed, tables, segment)

    def chunks_of(array, index):
        rows, columns = array.shape
        grouped = array.reshape(rows, columns // (2 * chunk), 2, chunk)
        return lax.dynamic_index_in_dim(grouped, index, 2, keepdims=False).reshape(rows, columns // 2)

    branch_pair = over_side(branch_half)

    def feature_sums(array):
        kept = chunks_of(array, side)
        got = over_side(chunks_of(array, 1 - side))
        own = in_order(col, kept, over_col(kept), 1)
        pair = in_order(col, got, over_col(got), 1)
        return (contract_rows(own, branch_half) + contract_rows(pair, branch_pair)).astype(bf16)

    def along_line(sums):
        depth = sums.shape[0] // line
        parts = sums.reshape(line, depth, sums.shape[1])

        def part(index):
            return lax.dynamic_index_in_dim(parts, jnp.clip(index, 0, line - 1), 0, keepdims=False).astype(f32)

        rightward, leftward = None, None
        for step in range(line - 1):
            right_part = part(line - 1 - step + place)
            left_part = part(place - (line - 1) + step)
            if step:
                right_part = right_part + rightward.astype(f32)
                left_part = left_part + leftward.astype(f32)
            to_right = [(2 * z + x, 2 * z + 2 + x) for z in range(min(step + 1, line - 1)) for x in range(2)]
            to_left = [(dp_size - 1 - p, dp_size - 1 - q) for p, q in to_right]
            rightward = lax.ppermute(right_part.astype(bf16), "dp", to_right)
            leftward = lax.ppermute(left_part.astype(bf16), "dp", to_left)
        return part(place) + rightward.astype(f32) + leftward.astype(f32)

    chunk = down_weight.shape[0] // dp_size
    grad_down = along_line(feature_sums(activated))

    chunk = up_weight.shape[0] // dp_size
    hidden_own = chunks_of(hidden, side)
    hidden_pair = over_side(chunks_of(hidden, 1 - side))

    def hidden_sums(array):
        pair = over_side(array)
        mine = (contract_rows(hidden_own, array) + contract_rows(hidden_pair, pair)).astype(bf16)
        theirs = (contract_rows(hidden_own, over_col(array)) + contract_rows(hidden_pair, over_col(pair))).astype(bf16)
        return in_order(col, along_line(mine), along_line(theirs), 1)

    grad_up = hidden_sums(d_before)
    chunk = dense_weight.shape[0] // dp_size
    grad_dense = along_line(feature_sums(attended))
    grad_qkv = hidden_sums(d_projected)

    def scatter(mine, other):
        half = mine + over_col(other.astype(bf16)).astype(f32)
        return half_at(half, row, 1) + over_row(half_at(half, 1 - row, 1).astype(bf16)).astype(f32)

    branch = scatter(
        dot_plain(attended, dense_mine) + dot_plain(activated, down_mine),
        dot_plain(attended, dense_other) + dot_plain(activated, down_other),
    )
    valid_col = is_valid.astype(f32)[:, None]
    outputs = (inputs.astype(f32) + valid_col * (branch + out_bias.astype(f32))).astype(bf16)

    d_hidden = scatter(
        contract_cols(d_projected, qkv_mine) + contract_cols(d_before, up_mine),
        contract_cols(d_projected, qkv_other) + contract_cols(d_before, up_other),
    )
    normed = (inputs.astype(f32) - average[:, None]) * scale_inv
    d_normed = d_hidden * norm_gain.astype(f32)
    row_sums = jnp.stack([jnp.sum(d_normed, axis=1), jnp.sum(d_normed * normed, axis=1)])
    row_sums = row_sums + over_row(row_sums)
    row_sums = row_sums + over_col(row_sums)
    grad_inputs = cotangent.astype(f32) + scale_inv * (
        d_normed - row_sums[0][:, None] / width - normed * row_sums[1][:, None] / width
    )

    small = [
        jnp.sum(d_hidden * normed, axis=0),
        jnp.sum(d_hidden, axis=0),
        jnp.sum(d_projected.astype(f32), axis=0),
        jnp.sum(d_before.astype(f32), axis=0),
        jnp.sum(grad_branch.astype(f32), axis=0),
    ]
    together = jnp.concatenate(small)
    bit = 1
    while bit < dp_size:
        together = together + lax.ppermute(together, "dp", [(e, e ^ bit) for e in range(dp_size)])
        bit *= 2
    ends = []
    for piece in small:
        ends.append((ends[-1] if ends else 0) + piece.shape[0])
    grad_gain, grad_shift, grad_qkv_bias, grad_up_bias, grad_out_bias = jnp.split(together, ends[:-1])
    return (
        outputs,
        grad_inputs,
        grad_gain,
        grad_shift,
        grad_qkv,
        grad_qkv_bias,
        grad_up,
        grad_up_bias,
        grad_dense,
        grad_down,
        grad_out_bias,
    )


def solution(mesh):
    in_specs = (
        P("dp", ("col", "row")),
        P(("col", "row")),
        P(("col", "row")),
        P("col", "row"),
        P(("row", "col")),
        P("col", "row"),
        P(("row", "col")),
        P("row", "col"),
        P("row", "col"),
        P(("col", "row")),
        P("dp", ("col", "row")),
        P(),
        P(),
    )
    out_specs = (
        P("dp", ("col", "row")),
        P("dp", ("col", "row")),
        P(("col", "row")),
        P(("col", "row")),
        P(("col", "dp"), "row"),
        P(("row", "col")),
        P(("col", "dp"), "row"),
        P(("row", "col")),
        P(("row", "dp"), "col"),
        P(("row", "dp"), "col"),
        P(("col", "row")),
    )
    return jax.shard_map(
        partial(on_device, mesh.shape["dp"]), mesh=mesh, in_specs=in_specs, out_specs=out_specs, check_vma=False
    )
```

```python
from functools import partial
import math

import jax
import jax.numpy as jnp
import numpy as np
from jax import lax
from jax.experimental import pallas as pl
from jax.experimental.pallas import tpu as pltpu
from jax.sharding import PartitionSpec as P

HEAD_DIM = 64
ROT = 32
HALF_ROT = ROT // 2
PAIR = 2 * HEAD_DIM
PAIR_QKV = 3 * PAIR

epsilon = 1e-05
masked_score = -1e30
rope_base = 10000.0
VMEM_LIMIT = 67_000_000
SCRATCH_LIMIT = 58 * 1024 * 1024
SENDS = 48
score_scale = HEAD_DIM ** (-0.5)
bf16 = jnp.bfloat16
f32 = jnp.float32


def layout(seq_lengths, seq_owner, device, row_count):
    owned = seq_owner == device
    lengths_owned = jnp.where(owned, seq_lengths, 0)
    seq_ends = jnp.cumsum(lengths_owned, dtype=jnp.int32)
    seq_starts = seq_ends - lengths_owned
    slot_index = jnp.arange(row_count, dtype=jnp.int32)
    segment = jnp.sum((seq_ends[None, :] <= slot_index[:, None]).astype(jnp.int32), axis=1)
    picked = jnp.arange(seq_lengths.shape[0], dtype=jnp.int32)[None, :] == segment[:, None]
    seq_begin = jnp.sum(jnp.where(picked, seq_starts[None, :], 0), axis=1)
    position = slot_index - seq_begin
    is_valid = slot_index < seq_ends[-1]
    return (segment, position, is_valid)


def rotation_tables(position):
    index_range = jnp.arange(HALF_ROT, dtype=f32)
    frequency = rope_base ** (-2.0 * index_range / ROT)
    phase = position.astype(f32)[:, None] * frequency[None, :]
    cosines, sines = jnp.cos(phase), jnp.sin(phase)
    rows = position.shape[0]
    ones = jnp.ones((rows, HEAD_DIM - ROT), f32)
    none = jnp.zeros((rows, HALF_ROT), f32)
    rest = jnp.zeros((rows, HEAD_DIM - ROT), f32)
    same = jnp.concatenate([cosines, cosines, ones], axis=1)
    from_right = jnp.concatenate([sines, none, rest], axis=1)
    from_left = jnp.concatenate([none, sines, rest], axis=1)
    return jnp.stack([same, from_right, from_left])


def turned(array):
    return jnp.swapaxes(array, 0, 1)


def contract(left, right, left_dim, right_dim):
    dims = (((left_dim,), (right_dim,)), ((), ()))
    return lax.dot_general(left, right, dims, preferred_element_type=f32)


gelu_rate = math.sqrt(2.0 / math.pi)
gelu_cube = 0.044715


def gelu(x):
    return 0.5 * x * (1.0 + jnp.tanh(gelu_rate * (x + gelu_cube * x * x * x)))


def gelu_slope(x):
    square = x * x
    bent = jnp.tanh(gelu_rate * (x + gelu_cube * x * square))
    return 0.5 * (1.0 + bent) + 0.5 * x * (1.0 - bent * bent) * (gelu_rate * (1.0 + 3.0 * gelu_cube * square))


def attention_pair(proj, mixed, tables, seg_col, seg_row):
    rows = proj.shape[0]
    block = min(256, rows)
    same, from_right, from_left = tables[0], tables[1], tables[2]

    def rotate(part, sign):
        right = jnp.concatenate([part[:, HALF_ROT:], part[:, :HALF_ROT]], axis=1)
        left = jnp.concatenate([part[:, HEAD_DIM - HALF_ROT :], part[:, : HEAD_DIM - HALF_ROT]], axis=1)
        return part * same - sign * (right * from_right) + sign * (left * from_left)

    attended_heads, grads = [], []
    for head in range(2):
        base = head * 3 * HEAD_DIM
        queries = rotate(proj[:, base : base + HEAD_DIM], 1.0).astype(bf16)
        keys = rotate(proj[:, base + HEAD_DIM : base + 2 * HEAD_DIM], 1.0).astype(bf16)
        values = proj[:, base + 2 * HEAD_DIM : base + 3 * HEAD_DIM].astype(bf16)
        d_outs = mixed[:, head * HEAD_DIM : (head + 1) * HEAD_DIM]
        outs, d_queries, d_keys, d_values = [], [], None, None
        for first in range(0, rows, block):
            last = first + block
            q, d_out = queries[first:last], d_outs[first:last]
            k, v = keys[:last], values[:last]
            row_index = first + lax.broadcasted_iota(jnp.int32, (block, last), 0)
            key_index = lax.broadcasted_iota(jnp.int32, (block, last), 1)
            allowed = (seg_col[first:last, :] == seg_row[:, :last]) & (key_index <= row_index)
            scores = jnp.where(allowed, contract(q, k, 1, 1) * score_scale, masked_score)
            weights = jnp.exp(scores - jnp.max(scores, axis=1, keepdims=True))
            probs = weights * (1.0 / jnp.sum(weights, axis=1, keepdims=True))
            probs_low = probs.astype(bf16)
            outs.append(contract(probs_low, v, 1, 0))
            d_probs = contract(d_out, v, 1, 1)
            row_dot = jnp.sum(probs * d_probs, axis=1, keepdims=True)
            d_scores = (probs * (d_probs - row_dot)).astype(bf16)
            d_queries.append(contract(d_scores, k, 1, 0))
            key_part = contract(d_scores, q, 0, 0)
            value_part = contract(probs_low, d_out, 0, 0)
            if d_keys is None:
                d_keys, d_values = key_part, value_part
            else:
                d_keys = jnp.concatenate([key_part[:first] + d_keys, key_part[first:]], axis=0)
                d_values = jnp.concatenate([value_part[:first] + d_values, value_part[first:]], axis=0)
        attended_heads.append(jnp.concatenate(outs, axis=0))
        grads.append(rotate(jnp.concatenate(d_queries, axis=0) * score_scale, -1.0))
        grads.append(rotate(d_keys * score_scale, -1.0))
        grads.append(d_values)
    attended = jnp.concatenate(attended_heads, axis=1).astype(bf16)
    return attended, jnp.concatenate(grads, axis=1).astype(bf16)


class Sizes:
    def __init__(self, dp_size, inputs, qkv_weight, up_weight, dense_weight, down_weight, seq_lengths):
        self.dp = dp_size
        self.seqs = seq_lengths.shape[0]
        self.line = dp_size // 2
        self.rows, self.quarter = inputs.shape
        self.half = up_weight.shape[0]
        self.width = 2 * self.half
        self.up_chunk = self.half // dp_size
        self.down_chunk = down_weight.shape[0] // dp_size
        self.dense_chunk = dense_weight.shape[0] // dp_size
        self.hidden = up_weight.shape[1] // 2
        self.tiles = self.hidden // self.down_chunk
        self.qkv = qkv_weight.shape[1] // 2
        self.pairs = self.qkv // PAIR_QKV
        self.features = dense_weight.shape[0] // 2


def flows_of(z):
    return dict(
        down=(z.down_chunk // z.up_chunk, z.up_chunk, z.quarter),
        up=(z.tiles, z.up_chunk, z.down_chunk),
        dense=(1, z.dense_chunk, z.quarter),
        qkv=(z.pairs, z.up_chunk, PAIR_QKV),
    )


def scratch_of(z):
    rows, q, line, tiles, pairs = z.rows, z.quarter, z.line, z.tiles, z.pairs
    up, down, dense = z.up_chunk, z.down_chunk, z.dense_chunk
    shapes = dict(
        inq=((2, 2, rows, q), bf16),
        cotq=((2, 2, rows, q), bf16),
        cotp=((2, rows, q), bf16),
        gainq=((2, 2, 16, q), f32),
        seg_col=((rows, 1), f32),
        seg_row=((1, rows), f32),
        tables=((3, rows, HEAD_DIM), f32),
        up_b=((tiles, 1, down), f32),
        qkv_b=((pairs, 1, PAIR_QKV), f32),
        sums=((1, 3 * q + z.qkv + z.hidden), f32),
        sums_got=((3, 1, 3 * q + z.qkv + z.hidden), f32),
        sums_send=((2, 1, 3 * q + z.qkv + z.hidden), f32),
        hid=((2, rows, z.half), bf16),
        hid_own=((line, rows, up), bf16),
        hid_send=((line, rows, up), bf16),
        hid_pair=((line, rows, up), bf16),
        stat=((2, rows, 1), f32),
        before=((tiles, rows, down), f32),
        act=((tiles, rows, down), bf16),
        act_own=((line, rows, down), bf16),
        act_pair=((line, rows, down), bf16),
        db_mine=((tiles, rows, down), bf16),
        db_theirs=((tiles, rows, down), bf16),
        db_mine_pair=((tiles, rows, down), bf16),
        db_theirs_pair=((tiles, rows, down), bf16),
        mixed=((pairs, rows, PAIR), bf16),
        att=((rows, z.features), bf16),
        att_part=((line, rows, dense), bf16),
        att_own=((line, rows, dense), bf16),
        att_pair=((line, rows, dense), bf16),
        dp_mine=((pairs, rows, PAIR_QKV), bf16),
        dp_theirs=((pairs, rows, PAIR_QKV), bf16),
        dp_mine_pair=((pairs, rows, PAIR_QKV), bf16),
        dp_theirs_pair=((pairs, rows, PAIR_QKV), bf16),
        weight=((2, 2, z.half, 512), bf16),
        st_down=((line, 2) + flows_of(z)["down"], bf16),
        st_up=((line, 2) + flows_of(z)["up"], bf16),
        st_dense=((line, 2) + flows_of(z)["dense"], bf16),
        st_qkv=((line, 2) + flows_of(z)["qkv"], bf16),
        got_down=(flows_of(z)["down"], bf16),
        got_up=(flows_of(z)["up"], bf16),
        got_dense=(flows_of(z)["dense"], bf16),
        got_qkv=(flows_of(z)["qkv"], bf16),
        part_send=((2, rows, q), bf16),
        part_row=((rows, q), bf16),
        out_row=((rows, q), bf16),
        dh_row=((rows, q), bf16),
        sum_send=((2, 8, rows), f32),
        sum_got=((2, 8, rows), f32),
    )
    if shapes["before"][0] != (4, rows, q):
        shapes["total"] = ((4, rows, q), f32)
    if shapes["st_up"] == shapes["st_down"]:
        del shapes["st_up"], shapes["got_up"]
    return shapes


def fits(z):
    total = 0
    for shape, kind in scratch_of(z).values():
        total += math.prod(shape[:-1]) * -(-shape[-1] // 128) * 128 * jnp.dtype(kind).itemsize
    return z.line >= 4 and z.line % 2 == 0 and total <= SCRATCH_LIMIT


def layer_kernel(z, names, *refs):
    r = dict(zip(names, refs))
    rows, q, line, tiles, pairs = z.rows, z.quarter, z.line, z.tiles, z.pairs
    half_line = line // 2
    if "total" not in r:
        r["total"] = r["before"]
    r["dh_got"], r["out_got"] = r["inq"].at[1], r["cotq"].at[1]
    shared = "st_up" not in r
    if shared:
        r["st_up"], r["got_up"] = r["st_down"], r["got_down"]
    dp = lax.axis_index("dp")
    row = lax.axis_index("row")
    col = lax.axis_index("col")
    place, side = dp // 2, lax.rem(dp, 2)
    other_row, other_col, other_side = 1 - row, 1 - col, 1 - side
    to_row = {"row": other_row}
    to_col = {"col": other_col}
    to_side = {"dp": dp + 1 - 2 * side}
    MESH = pl.DeviceIdType.MESH

    marks = dict(send=0, recv=0, local=0)

    def take(kind, count):
        first = marks[kind]
        marks[kind] += count
        return first

    def remote(src, dst, send, recv, device):
        return pltpu.make_async_remote_copy(
            src_ref=src,
            dst_ref=dst,
            send_sem=r["send_sem"].at[send],
            recv_sem=r["recv_sem"].at[recv],
            device_id=device,
            device_id_type=MESH,
        )

    pending = []

    class Message:
        def __init__(self, src, dst, device, got=None):
            index = (take("send", 1), take("recv", 1))
            self.copy = lambda: remote(src, dst, *index, device)
            self.got = lambda: remote(src if got is None else got, dst if got is None else got, *index, device)

        def start(self):
            self.copy().start()
            pending.append(self)

        def wait(self):
            self.got().wait_recv()

    right, left = {"dp": dp + 2}, {"dp": dp - 2}
    has_right, has_left = place < line - 1, place > 0
    at_end, near_end = (place == 0) | (place == line - 1), (place == 1) | (place == line - 2)
    inward, outward = {"dp": dp + 2 - 4 * (place > 0)}, {"dp": dp + 2 - 4 * (place == 1)}
    barrier = pltpu.get_barrier_semaphore()
    for device in (to_row, to_col, to_side):
        pl.semaphore_signal(barrier, inc=1, device_id=device, device_id_type=MESH)

    @pl.when(has_right)
    def _():
        pl.semaphore_signal(barrier, inc=1, device_id=right, device_id_type=MESH)

    @pl.when(has_left)
    def _():
        pl.semaphore_signal(barrier, inc=1, device_id=left, device_id_type=MESH)

    slots = lax.broadcasted_iota(jnp.int32, (8, rows), 1)

    def add_sequence(number, carry):
        end, segments, begins = carry
        start = end
        end = start + jnp.where(r["seq_owner"][number] == dp, r["seq_lengths"][number], 0)
        segments = segments + (end <= slots).astype(jnp.int32)
        begins = jnp.where((start <= slots) & (slots < end), start, begins)
        return end, segments, begins

    nothing = jnp.zeros((8, rows), jnp.int32)
    segments, begins = lax.fori_loop(0, z.seqs, add_sequence, (jnp.int32(0), nothing, nothing))[1:]
    segments = segments.astype(f32)
    r["seg_row"][...] = segments[:1]
    r["seg_col"][...] = turned(segments)[:, :1]
    cot = r["cot"]
    valid = (r["seg_col"][...] < z.seqs).astype(f32)
    r["cotq"][0, row] = cot[...] * valid.astype(bf16)

    def as_row(vector):
        return vector.astype(f32).reshape(1, vector.shape[0])

    r["gainq"][0, row] = jnp.concatenate(
        [
            jnp.broadcast_to(as_row(r["norm_gain"][...]), (8, q)),
            jnp.broadcast_to(as_row(r["norm_shift"][...]), (8, q)),
        ]
    )
    pl.semaphore_wait(barrier, 3 + has_right.astype(jnp.int32) + has_left.astype(jnp.int32))

    def gather(src, held):
        over = Message(src, held.at[0, row], to_row, held.at[0, other_row])
        across = Message(src, held.at[1, row], to_col, held.at[1, row])
        onward = Message(held.at[0, other_row], held.at[1, other_row], to_col, held.at[1, other_row])
        return over, across, onward

    in_over, in_across, in_onward = gather(r["inputs"], r["inq"])
    gain_over, gain_across, gain_onward = gather(r["gainq"].at[0, row], r["gainq"])
    cot_over, cot_across, cot_onward = gather(r["cotq"].at[0, row], r["cotq"])
    cot_side = Message(r["cotq"].at[0, row], r["cotp"].at[row], to_side)
    cot_side_onward = Message(r["cotq"].at[0, other_row], r["cotp"].at[other_row], to_side)
    hid_side = Message(r["hid_send"], r["hid_pair"], to_side)

    end_cot_send, end_cot_recv = take("send", 4), take("recv", 4)

    def end_cot(pair, part, device):
        src = r["cotp"].at[part] if pair else r["cotq"].at[0, part]
        index = 2 * pair + part
        return remote(src, r["end_cot"].at[pair, part], end_cot_send + index, end_cot_recv + index, device)

    def send_end_cot(pair, part):
        @pl.when(at_end)
        def _():
            end_cot(pair, part, inward).start()

    def loop(first, last, work):
        def one(k, carry):
            work(k)
            return carry

        lax.fori_loop(first, last, one, 0)

    def pass_on(got, onward):
        def work(k):
            got(k).wait_recv()
            onward(k).start()

        return work

    def waits(*copies):
        def work(k):
            for copy in copies:
                copy(k).wait_recv()

        return work

    class EndRows:
        def __init__(self, own, pair, land):
            self.own, self.pair, self.land = own, pair, land
            self.send, self.recv = take("send", line), take("recv", line)
            self.on_send, self.on_recv = take("send", line), take("recv", line)

        def copy(self, chunk, device, pair):
            src = (self.pair if pair else self.own).at[chunk]
            return remote(src, self.land.at[chunk, int(pair)], self.send + chunk, self.recv + chunk, device)

        def onward(self, chunk):
            part = self.land.at[chunk, col]
            return remote(part, part, self.on_send + chunk, self.on_recv + chunk, to_col)

        def start(self, pair, first, last):
            kind = 1 if pair else 0

            @pl.when(at_end & (col == kind))
            def _():
                def one(number):
                    chunk = jnp.where(place == 0, line - 1 - number, number)
                    self.copy(chunk, inward, pair).start()

                loop(first, last, one)

        def bring(self, chunk):
            self.copy(chunk, outward, False).wait_recv()
            self.onward(chunk).start()
            self.onward(chunk).wait_recv()

        def finish(self):
            def one(chunk):
                @pl.when(at_end & (chunk != place))
                def _():
                    self.copy(chunk, inward, False).wait_send()

                @pl.when(near_end)
                def _():
                    gone = jnp.where(place == 1, 0, line - 1)

                    @pl.when(chunk != gone)
                    def _():
                        self.onward(chunk).wait_send()

            loop(0, line, one)

    end_act = EndRows(r["act_own"], r["act_pair"], r["end_act"])
    end_att = EndRows(r["att_own"], r["att_pair"], r["end_att"])
    swaps = {
        "up": Message(r["up_w"].at[:, pl.ds(pl.multiple_of(other_col * z.hidden, 128), z.hidden)], r["up_o"], to_col, r["up_o"]),
        "qkv": Message(r["qkv_w"].at[:, pl.ds(pl.multiple_of(other_col * z.qkv, 128), z.qkv)], r["qkv_o"], to_col, r["qkv_o"]),
        "down": Message(r["down_w"].at[pl.ds(pl.multiple_of(other_col * z.hidden, 16), z.hidden), :], r["down_o"], to_col, r["down_o"]),
        "dense": Message(r["dense_w"].at[pl.ds(pl.multiple_of(other_col * z.features, 16), z.features), :], r["dense_o"], to_col, r["dense_o"]),
    }

    def local(src, dst, index):
        return pltpu.make_async_copy(src, dst, r["local_sem"].at[index])

    stream_base = take("local", 8)
    once = take("local", 4)

    in_over.start()
    gain_over.start()
    in_across.start()
    gain_across.start()
    keep_in = local(r["inputs"], r["inq"].at[0, row], once)
    keep_in.start()
    cot_side.start()
    send_end_cot(0, row)
    swaps["up"].start()
    up_bias, qkv_bias = as_row(r["up_bias"][...]), as_row(r["qkv_bias"][...])
    for tile in range(tiles):
        r["up_b"][tile] = up_bias[:, tile * z.down_chunk : (tile + 1) * z.down_chunk]
    for pair in range(pairs):
        r["qkv_b"][pair] = qkv_bias[:, pair * PAIR_QKV : (pair + 1) * PAIR_QKV]
    position = turned((slots - begins).astype(f32))[:, :1]
    phase = position * r["frequency"][...]
    lane = lax.broadcasted_iota(jnp.int32, (1, HEAD_DIM), 1)
    sines = jnp.sin(phase)
    r["tables"][0] = jnp.where(lane < ROT, jnp.cos(phase), 1.0)
    r["tables"][1] = jnp.where(lane < HALF_ROT, sines, 0.0)
    r["tables"][2] = jnp.where((lane >= HALF_ROT) & (lane < ROT), sines, 0.0)
    gain_over.wait()
    gain_onward.start()
    in_over.wait()
    in_onward.start()
    cot_over.start()
    cot_across.start()
    cot_side.wait()
    send_end_cot(1, row)
    keep_in.wait()
    gain_across.wait()
    gain_onward.wait()
    in_across.wait()
    in_onward.wait()

    block = min(64, rows)

    def norm_rows(step, carry):
        at = pl.ds(pl.multiple_of(step * block, block), block)
        parts = [r["inq"][h, p, at].astype(f32) for h in range(2) for p in range(2)]
        total = parts[0] + parts[1] + parts[2] + parts[3]
        squares = parts[0] * parts[0] + parts[1] * parts[1] + parts[2] * parts[2] + parts[3] * parts[3]
        average = jnp.sum(total, axis=1, keepdims=True) / z.width
        variance = jnp.sum(squares, axis=1, keepdims=True) / z.width - average * average
        scale_inv = lax.rsqrt(variance + epsilon)
        r["stat"][0, at] = average
        r["stat"][1, at] = scale_inv
        for h in range(2):
            for p in range(2):
                normed = (parts[2 * h + p] - average) * scale_inv
                gain, shift = r["gainq"][h, p, 0:1, :], r["gainq"][h, p, 8:9, :]
                r["hid"][h, at, p * q : (p + 1) * q] = (normed * gain + shift).astype(bf16)
        return carry

    lax.fori_loop(0, rows // block, norm_rows, 0)
    for c in range(line):
        even = r["hid"][0, :, 2 * c * z.up_chunk : (2 * c + 1) * z.up_chunk]
        odd = r["hid"][0, :, (2 * c + 1) * z.up_chunk : (2 * c + 2) * z.up_chunk]
        r["hid_own"][c] = jnp.where(side == 0, even, odd)
        r["hid_send"][c] = jnp.where(side == 0, odd, even)

    def stream(count, copies, work):
        for copy in copies(jnp.int32(0), jnp.int32(0)):
            copy.start()

        def one(step, carry):
            slot = lax.rem(step, 2)

            @pl.when(step + 1 < count)
            def _():
                for copy in copies(step + 1, 1 - slot):
                    copy.start()

            for copy in copies(step, slot):
                copy.wait()
            work(step, slot)
            return carry

        lax.fori_loop(0, count, one, 0)

    def column_tiles(name, each, tile_of=lambda step: step):
        def copies(step, slot):
            tile = tile_of(step)
            mine = r[name + "_w"].at[:, pl.ds(pl.multiple_of((col * r[name + "_o"].shape[1]) + tile * each, 128), each)]
            theirs = r[name + "_o"].at[:, pl.ds(pl.multiple_of(tile * each, 128), each)]
            return [
                local(mine, r["weight"].at[slot, 0, :, :each], stream_base + slot * 4),
                local(theirs, r["weight"].at[slot, 1, :, :each], stream_base + slot * 4 + 1),
            ]

        return copies

    def row_tiles(name, each, tile_of=lambda step: step):
        def copies(step, slot):
            tile = tile_of(step)
            found = []
            for h in range(2):
                start = tile * each + (col * r[name + "_o"].shape[0] if h == 0 else 0)
                src = r[name + ("_w" if h == 0 else "_o")]
                for p in range(2):
                    found.append(
                        local(
                            src.at[pl.ds(pl.multiple_of(start, 16), each), p * q : (p + 1) * q],
                            r["weight"].at[slot, h, p * q : p * q + each, :],
                            stream_base + slot * 4 + 2 * h + p,
                        )
                    )
            return found

        return copies

    def rank_of(j):
        return jnp.where(col == 1, half_line - 1 - j, j)

    def tile_at(step):
        later = (step >= half_line).astype(jnp.int32)
        return 2 * rank_of(step - later * half_line) + jnp.where(later == 1, side, other_side)

    act_side_send, act_side_recv = take("send", half_line), take("recv", half_line)
    act_col_send, act_col_recv = take("send", half_line), take("recv", half_line)
    act_on_send, act_on_recv = take("send", half_line), take("recv", half_line)

    def act_side(j):
        tile, slot = 2 * rank_of(j) + other_side, col * half_line + rank_of(j)
        return remote(r["act"].at[tile], r["act_pair"].at[slot], act_side_send + j, act_side_recv + j, to_side)

    def act_col(j):
        slot = col * half_line + rank_of(j)
        return remote(r["act_own"].at[slot], r["act_own"].at[slot], act_col_send + j, act_col_recv + j, to_col)

    def act_on(j):
        slot = col * half_line + rank_of(j)
        return remote(r["act_pair"].at[slot], r["act_pair"].at[slot], act_on_send + j, act_on_recv + j, to_col)

    def up_work(step, slot):
        tile = tile_at(step)
        before = contract(r["hid"][0], r["weight"][slot, 0, :, : z.down_chunk], 1, 0)
        before = before + contract(r["hid"][1], r["weight"][slot, 1, :, : z.down_chunk], 1, 0)
        before = before + r["up_b"][tile]
        r["before"][tile] = before
        activated = gelu(before).astype(bf16)
        r["act"][tile] = activated

        @pl.when(step < half_line)
        def _():
            act_side(step).start()

        @pl.when(step >= half_line)
        def _():
            j = step - half_line
            r["act_own"][col * half_line + rank_of(j)] = activated
            act_col(j).start()

    hid_side.start()
    swaps["down"].start()
    swaps["up"].wait()
    stream(tiles, column_tiles("up", z.down_chunk, tile_at), up_work)

    cot_over.wait()
    cot_onward.start()
    cot_side_onward.start()
    send_end_cot(0, other_row)
    loop(0, half_line, waits(act_col))
    end_act.start(False, 0, line - 1)
    swaps["qkv"].start()
    swaps["dense"].start()
    cot_across.wait()
    cot_onward.wait()
    swaps["down"].wait()

    def each_side(name, count):
        side_send, side_recv = take("send", count), take("recv", count)
        col_send, col_recv = take("send", count), take("recv", count)
        on_send, on_recv = take("send", count), take("recv", count)
        mine, theirs = r[name + "_mine"], r[name + "_theirs"]
        mine_pair, theirs_pair = r[name + "_mine_pair"], r[name + "_theirs_pair"]

        def to_side_peer(k):
            return remote(mine.at[k], mine_pair.at[k], side_send + k, side_recv + k, to_side)

        def to_col_peer(k):
            return remote(mine.at[k], theirs.at[k], col_send + k, col_recv + k, to_col)

        def onward(k):
            return remote(mine_pair.at[k], theirs_pair.at[k], on_send + k, on_recv + k, to_col)

        return to_side_peer, to_col_peer, onward

    db_side, db_col, db_on = each_side("db", tiles)
    dp_side, dp_col, dp_on = each_side("dp", pairs)

    def over_weight_rows(slot, each, lefts):
        total = None
        for h in range(2):
            for p in range(2):
                part = contract(lefts(h, p), r["weight"][slot, h, p * q : p * q + each, :], 1, 1)
                total = part if total is None else total + part
        return total

    def down_work(step, slot):
        tile = step
        d_activated = over_weight_rows(slot, z.down_chunk, lambda h, p: r["cotq"][h, p])
        d_before = (d_activated * gelu_slope(r["before"][tile])).astype(bf16)
        r["db_mine"][tile] = d_before
        sums = jnp.sum(d_before.astype(f32), axis=0, keepdims=True)
        r["sums"][:, pl.ds(pl.multiple_of(2 * q + z.qkv + tile * z.down_chunk, 128), z.down_chunk)] = sums
        db_col(tile).start()
        db_side(tile).start()

    stream(tiles, row_tiles("down", z.down_chunk), down_work)

    class Flow:
        def __init__(self, name, own_rows, pair_rows, own_columns, pair_columns, split=False, by_col=False, earlier=None, ends=None):
            self.name, self.split, self.by_col, self.earlier, self.ends = name, split, by_col, earlier, ends
            self.own_rows, self.pair_rows = own_rows, pair_rows
            self.own_columns, self.pair_columns = own_columns, pair_columns
            self.stage, self.land, self.got = r["st_" + name], r["land_" + name], r["got_" + name]
            self.count, self.depth = flows_of(z)[name][:2]
            self.send = take("send", 2 * line)
            self.recv = take("recv", 2 * (line + 2))
            self.local = take("local", 1)
            self.later = False

        def half(self, group):
            return jnp.where(col == 0, group, 1 - group) if self.by_col else group

        def copy(self, chunk, group, slot, device):
            half = self.half(group)
            return remote(
                self.stage.at[chunk, half],
                self.land.at[slot, half],
                self.send + 2 * chunk + group,
                self.recv + 2 * slot + group,
                device,
            )

        def sums(self, chunk):
            own, pair = turned(self.own_rows[chunk]), turned(self.pair_rows[chunk])

            def tile_sums(group, tile):
                at = slice(tile * self.depth, (tile + 1) * self.depth) if self.split else slice(None)
                column = 0 if self.split else tile
                part = contract(own[at], self.own_columns(group, column), 1, 0)
                return part + contract(pair[at], self.pair_columns(group, column), 1, 0)

            return tile_sums

        def add(self, rank, chunk, slot, device):
            tile_sums = self.sums(chunk)
            self.free(chunk, device)
            if self.ends is not None:

                @pl.when(rank == 1)
                def _():
                    self.bring_end(chunk)

            for group in range(2):
                half = self.half(group)

                @pl.when(rank > (0 if self.ends is None else 1))
                def _():
                    self.copy(chunk, group, chunk, device).wait_recv()
                    bring = local(self.land.at[chunk, half], self.got, self.local)
                    bring.start()
                    bring.wait()

                if self.ends is None:

                    @pl.when(rank == 0)
                    def _():
                        self.got[...] = jnp.zeros_like(self.got)

                else:

                    @pl.when(rank == 1)
                    def _():
                        self.end_sums(group)

                for tile in range(self.count):
                    whole = tile_sums(group, tile) + self.got[tile].astype(f32)
                    self.stage[chunk, half, tile] = whole.astype(bf16)
                self.copy(chunk, group, slot, device).start()

        def free(self, chunk, device):
            if self.earlier is not None:

                @pl.when(jnp.logical_not(at_end))
                def _():
                    for group in range(2):
                        self.earlier.copy(chunk, group, chunk, device).wait_send()

        def bring_end(self, chunk):
            self.ends.bring(chunk)
            copies = []
            for pair in range(2):
                rows_in = self.ends.land.at[chunk, pair]
                copies.append(local(rows_in, r["weight"].at[1, pair, :rows, : rows_in.shape[1]], stream_base + pair))
                for part in range(2):
                    at = r["weight"].at[0, pair, part * rows : (part + 1) * rows, :q]
                    copies.append(local(r["end_cot"].at[pair, part], at, stream_base + 2 + 2 * pair + part))
            for copy in copies:
                copy.start()
            for copy in copies:
                copy.wait()

        def end_sums(self, group):
            columns = self.depth * self.count if self.split else self.depth
            for tile in range(self.count):
                at = slice(tile * self.depth, (tile + 1) * self.depth)
                total = None
                for pair in range(2):
                    left = turned(r["weight"][1, pair, :rows, :columns][:, at])
                    part = contract(left, r["weight"][0, pair, group * rows : (group + 1) * rows, :q], 1, 0)
                    total = part if total is None else total + part
                self.got[tile] = total.astype(bf16)

        def start(self, tile):
            for way, end, device in ((0, 0, right), (1, line - 1, left)):

                @pl.when(place == end)
                def _():
                    chunk = (line - 1) * (1 - way)
                    if tile == 0:
                        self.free(chunk, device)
                    tile_sums = self.sums(chunk)
                    for group in range(2):
                        half = self.half(group)
                        self.stage[chunk, half, tile] = tile_sums(group, tile).astype(bf16)
                        remote(
                            self.stage.at[chunk, half, tile],
                            self.land.at[chunk, half, tile],
                            self.send + 2 * chunk + group,
                            self.recv + 2 * chunk + group,
                            device,
                        ).start()

        def step(self, number):
            def one(way, carry):
                rightward = way == 0
                rank = jnp.where(rightward, place, line - 1 - place)
                chunk = jnp.where(rightward, line - 1 - number + place, place - (line - 1) + number)
                slot = jnp.where(chunk == place + 1 - 2 * way, line + way, chunk)
                device = {"dp": dp + 2 - 4 * way}

                @pl.when((rank <= number) & (rank < line - 1) & (rank >= (0 if self.ends is None else 1)))
                def _():
                    self.add(rank, chunk, slot, device)

                return carry

            lax.fori_loop(0, 2, one, 0)

        def steps(self, first, last):
            if last - first == 1:
                self.step(first)
            elif last > first:
                loop(first, last, self.step)

        def own(self):
            if self.earlier is not None:
                self.earlier.out.wait()
                self.earlier.later = True
            tile_sums = self.sums(place)
            if self.ends is not None:

                @pl.when(near_end)
                def _():
                    self.bring_end(place)

            for group in range(2):
                if self.ends is not None:

                    @pl.when(near_end)
                    def _():
                        self.end_sums(group)

                    @pl.when(jnp.logical_not(near_end))
                    def _():
                        self.got[...] = jnp.zeros_like(self.got)

                for tile in range(self.count):
                    whole = tile_sums(group, tile)
                    if self.ends is not None:
                        whole = whole + self.got[tile].astype(f32)
                    self.stage[place, self.half(group), tile] = whole.astype(bf16)
            self.out = local(self.stage.at[place], r["own_" + self.name], self.local)
            self.out.start()

        def finish(self):
            if not self.later:
                self.out.wait()
            far = 0 if self.ends is None else 1
            for group in range(2):

                @pl.when(place > far)
                def _():
                    self.copy(place, group, line, left).wait_recv()

                @pl.when(place < line - 1 - far)
                def _():
                    self.copy(place, group, line + 1, right).wait_recv()

            def sent(chunk):
                @pl.when((chunk != place) & (jnp.logical_not(at_end) if far else True))
                def _():
                    for group in range(2):
                        self.copy(chunk, group, chunk, right).wait_send()

            if not self.later:
                loop(0, line, sent)

    cot_own_tile = lambda group, tile: r["cotq"][0, group]
    cot_pair_tile = lambda group, tile: r["cotp"][group]
    down = Flow("down", r["act_own"], r["act_pair"], cot_own_tile, cot_pair_tile, split=True, ends=end_act)
    up = Flow(
        "up",
        r["hid_own"],
        r["hid_pair"],
        lambda group, tile: r[("db_mine", "db_theirs")[group]][tile],
        lambda group, tile: r[("db_mine_pair", "db_theirs_pair")[group]][tile],
        by_col=True,
        earlier=down if shared else None,
    )
    dense = Flow("dense", r["att_own"], r["att_pair"], cot_own_tile, cot_pair_tile, ends=end_att)
    qkv = Flow(
        "qkv",
        r["hid_own"],
        r["hid_pair"],
        lambda group, tile: r[("dp_mine", "dp_theirs")[group]][tile],
        lambda group, tile: r[("dp_mine_pair", "dp_theirs_pair")[group]][tile],
        by_col=True,
    )
    cuts = (0, 1, line // 2, line - 1)

    swaps["qkv"].wait()

    def qkv_work(step, slot):
        part = contract(r["hid"][0], r["weight"][slot, 0, :, :PAIR_QKV], 1, 0)
        part = part + contract(r["hid"][1], r["weight"][slot, 1, :, :PAIR_QKV], 1, 0)
        r["total"][step, :, :PAIR_QKV] = part + r["qkv_b"][step]

    stream(pairs, column_tiles("qkv", PAIR_QKV), qkv_work)
    swaps["dense"].wait()

    def dense_work(step, slot):
        d_mixed = over_weight_rows(slot, z.features, lambda h, p: r["cotq"][h, p]).astype(bf16)
        for pair in range(pairs):
            r["mixed"][pair] = d_mixed[:, pair * PAIR : (pair + 1) * PAIR]

    stream(1, row_tiles("dense", z.features), dense_work)
    loop(0, 1, pass_on(act_side, act_on))
    loop(0, 1, waits(act_on))
    end_act.start(True, 0, 1)

    att_side_send, att_side_recv = take("send", half_line), take("recv", half_line)
    att_col_send, att_col_recv = take("send", half_line), take("recv", half_line)
    att_on_send, att_on_recv = take("send", half_line), take("recv", half_line)

    def att_side(k):
        slot = col * half_line + k
        return remote(
            r["att_part"].at[2 * k + other_side], r["att_pair"].at[slot], att_side_send + k, att_side_recv + k, to_side
        )

    def att_col(k):
        slot = col * half_line + k
        return remote(r["att_own"].at[slot], r["att_own"].at[slot], att_col_send + k, att_col_recv + k, to_col)

    def att_on(k):
        slot = col * half_line + k
        return remote(r["att_pair"].at[slot], r["att_pair"].at[slot], att_on_send + k, att_on_recv + k, to_col)

    def head_pair(pair):
        attended, d_projected = attention_pair(
            r["total"][pair, :, :PAIR_QKV], r["mixed"][pair], r["tables"], r["seg_col"][...], r["seg_row"][...]
        )
        r["dp_mine"][pair] = d_projected
        dp_side(pair).start()
        dp_col(pair).start()
        sums = jnp.sum(d_projected.astype(f32), axis=0, keepdims=True)
        r["sums"][:, pl.ds(pl.multiple_of(2 * q + pair * PAIR_QKV, 128), PAIR_QKV)] = sums
        r["att"][:, pl.ds(pl.multiple_of(pair * PAIR, PAIR), PAIR)] = attended
        each = PAIR // z.dense_chunk
        for part in range(each):
            chunk = pair * each + part
            k = chunk // 2
            piece = attended[:, part * z.dense_chunk : (part + 1) * z.dense_chunk]

            @pl.when(lax.rem(chunk, 2) == side)
            def _():
                r["att_own"][col * half_line + k] = piece
                att_col(k).start()

            @pl.when(lax.rem(chunk, 2) == other_side)
            def _():
                r["att_part"][chunk] = piece
                att_side(k).start()

    loop(0, pairs // 2, head_pair)
    cot_side_onward.wait()
    send_end_cot(1, other_row)
    loop(1, half_line, pass_on(act_side, act_on))
    loop(1, half_line, waits(act_on))
    end_act.start(True, 1, line - 1)
    loop(pairs // 2, pairs, head_pair)

    def near_end_cot():
        @pl.when(near_end)
        def _():
            for pair in range(2):
                for part in range(2):
                    end_cot(pair, part, outward).wait_recv()

    near_end_cot()
    down.steps(cuts[1], cuts[2])

    def scatter(name, total, earlier=None):
        across = Message(r["part_send"], r[name + "_got"], to_col)
        over = Message(r["part_row"], r[name + "_row"], to_row)

        def free(message):
            message.copy().wait_send()
            pending.remove(message)

        def first():
            if earlier is not None:
                free(earlier[0])
            for p in range(2):
                r["part_send"][p] = total[2 + p].astype(bf16)
            across.start()

        def second():
            across.wait()
            if earlier is not None:
                free(earlier[1])
            for p in range(2):
                total[p] = total[p] + r[name + "_got"][p].astype(f32)
            r["part_row"][...] = total[other_row].astype(bf16)
            over.start()

        def third():
            over.wait()
            return total[row] + r[name + "_row"][...].astype(f32)

        return first, second, third, (across, over)

    total = r["total"]

    def down_out(step, slot):
        for h in range(2):
            for p in range(2):
                part = contract(r["act"][step], r["weight"][slot, h, p * q : p * q + z.down_chunk, :], 1, 0)

                @pl.when(step == 0)
                def _():
                    total[2 * h + p] = part

                @pl.when(step > 0)
                def _():
                    total[2 * h + p] = total[2 * h + p] + part

    def dense_out(step, slot):
        for h in range(2):
            for p in range(2):
                part = contract(r["att"][...], r["weight"][slot, h, p * q : p * q + z.features, :], 1, 0)
                total[2 * h + p] = total[2 * h + p] + part

    def up_back(step, slot):
        for h in range(2):
            for p in range(2):
                part = contract(r["db_mine"][step], r["weight"][slot, h, p * q : (p + 1) * q, : z.down_chunk], 1, 1)

                @pl.when(step == 0)
                def _():
                    total[2 * h + p] = part

                @pl.when(step > 0)
                def _():
                    total[2 * h + p] = total[2 * h + p] + part

    def qkv_back(step, slot):
        for h in range(2):
            for p in range(2):
                part = contract(r["dp_mine"][step], r["weight"][slot, h, p * q : (p + 1) * q, :PAIR_QKV], 1, 1)
                total[2 * h + p] = total[2 * h + p] + part

    stream(tiles, column_tiles("up", z.down_chunk), up_back)
    stream(pairs, column_tiles("qkv", PAIR_QKV), qkv_back)
    dh_first, dh_second, dh_third, dh_messages = scatter("dh", total)
    dh_first()
    hid_side.wait()
    for tile in range(tiles):
        loop(tile, tile + 1, pass_on(db_side, db_on))
        loop(tile, tile + 1, waits(db_col, db_on))
        up.start(tile)
        if tile == tiles // 2:
            down.steps(cuts[2], cuts[3])
    dh_second()
    up.steps(cuts[1], cuts[2])

    d_hidden = dh_third()
    r["grad_inputs"][...] = d_hidden
    own_in = r["inq"].at[0, row]
    gain = r["gainq"][0, row, 0:1, :]
    sums_row = Message(r["sum_send"].at[0], r["sum_got"].at[0], to_row)
    sums_col = Message(r["sum_send"].at[1], r["sum_got"].at[1], to_col)
    normed = (own_in[...].astype(f32) - r["stat"][0]) * r["stat"][1]
    d_normed = d_hidden * gain
    lane = lax.broadcasted_iota(jnp.int32, (rows, 128), 1)
    one = jnp.sum(d_normed, axis=1, keepdims=True)
    two = jnp.sum(d_normed * normed, axis=1, keepdims=True)
    packed = jnp.where(lane == 0, one, jnp.where(lane == 1, two, 0.0))
    r["sum_send"][0] = turned(packed)[:8]
    sums_row.start()
    r["sums"][:, 0:q] = jnp.sum(d_hidden * normed, axis=0, keepdims=True)
    r["sums"][:, q : 2 * q] = jnp.sum(d_hidden, axis=0, keepdims=True)
    r["sums"][:, 2 * q + z.qkv + z.hidden :] = jnp.sum(r["cotq"][0, row].astype(f32), axis=0, keepdims=True)
    small_side = Message(r["sums"], r["sums_got"].at[0], to_side)
    small_side.start()

    stream(tiles, row_tiles("down", z.down_chunk), down_out)
    stream(1, row_tiles("dense", z.features), dense_out)
    out_first, out_second, out_third, out_messages = scatter("out", total, dh_messages)
    out_first()
    sums_row.wait()
    r["sum_send"][1] = r["sum_send"][0] + r["sum_got"][0]
    sums_col.start()
    up.steps(cuts[2], cuts[3])
    out_second()
    sums_col.wait()
    both = r["sum_send"][1] + r["sum_got"][1]
    spread = turned(jnp.concatenate([both, jnp.zeros((120, rows), f32)], axis=0))
    part_one, part_two = spread[:, 0:1] / z.width, spread[:, 1:2] / z.width
    normed = (own_in[...].astype(f32) - r["stat"][0]) * r["stat"][1]
    d_normed = r["grad_inputs"][...] * gain
    r["grad_inputs"][...] = cot[...].astype(f32) + r["stat"][1] * (d_normed - part_one - normed * part_two)

    small_send, small_recv = take("send", 2), take("recv", 2)

    def small(way, device):
        return remote(r["sums_send"].at[way], r["sums_got"].at[1 + way], small_send + way, small_recv + way, device)

    def hop(number):
        for way, rank, device, last in ((0, place, right, has_right), (1, line - 1 - place, left, has_left)):

            @pl.when((rank == number) & last)
            def _():
                @pl.when(rank == 0)
                def _():
                    r["sums_send"][way] = r["sums"][...]

                @pl.when(rank > 0)
                def _():
                    small(way, device).wait_recv()
                    r["sums_send"][way] = r["sums"][...] + r["sums_got"][1 + way]

                small(way, device).start()

    def hops(first, last):
        if last - first == 1:
            hop(first)
        elif last > first:
            loop(first, last, hop)

    loop(0, pairs, pass_on(dp_side, dp_on))
    loop(0, half_line, pass_on(att_side, att_on))
    loop(0, half_line, waits(att_col, att_on))
    end_att.start(False, 0, line - 1)
    end_att.start(True, 0, line - 1)
    loop(0, pairs, waits(dp_col, dp_on))
    qkv.steps(cuts[0], cuts[1])
    branch = out_third()
    bias = as_row(r["out_bias"][...])
    valid = (r["seg_col"][...] < z.seqs).astype(f32)
    r["outputs"][...] = (r["inq"][0, row].astype(f32) + valid * (branch + bias)).astype(bf16)
    small_side.wait()
    small_side.copy().wait_send()
    pending.remove(small_side)
    r["sums"][...] = r["sums"][...] + r["sums_got"][0]
    hops(cuts[0], cuts[1])
    down.own()
    dense.steps(cuts[1], cuts[2])
    qkv.steps(cuts[1], cuts[2])
    hops(cuts[1], cuts[2])
    up.own()
    dense.steps(cuts[2], cuts[3])
    qkv.steps(cuts[2], cuts[3])
    hops(cuts[2], cuts[3])
    dense.own()
    qkv.own()

    r["small"][...] = r["sums"][...]

    @pl.when(place == line - 1)
    def _():
        small(0, left).wait_recv()

    @pl.when(place == 0)
    def _():
        small(1, right).wait_recv()

    @pl.when(has_left)
    def _():
        r["small"][...] = r["small"][...] + r["sums_got"][1]

    @pl.when(has_right)
    def _():
        r["small"][...] = r["small"][...] + r["sums_got"][2]

    @pl.when(has_right)
    def _():
        small(0, right).wait_send()

    @pl.when(has_left)
    def _():
        small(1, left).wait_send()

    for flow in (down, up, dense, qkv):
        flow.finish()
    end_act.finish()
    end_att.finish()

    @pl.when(at_end)
    def _():
        for pair in range(2):
            for part in range(2):
                end_cot(pair, part, inward).wait_send()

    for message in pending:
        message.copy().wait_send()

    def sent(*copies):
        def work(k):
            for copy in copies:
                copy(k).wait_send()

        return work

    loop(0, half_line, sent(act_side, act_col, act_on, att_side, att_col, att_on))
    loop(0, tiles, sent(db_side, db_col, db_on))
    loop(0, pairs, sent(dp_side, dp_col, dp_on))
    assert marks["send"] <= SENDS * line and marks["recv"] <= SENDS * line and marks["local"] <= 16


def on_device(
    dp_size,
    inputs,
    norm_gain,
    norm_shift,
    qkv_weight,
    qkv_bias,
    up_weight,
    up_bias,
    dense_weight,
    down_weight,
    out_bias,
    cotangent,
    seq_lengths,
    seq_owner,
):
    z = Sizes(dp_size, inputs, qkv_weight, up_weight, dense_weight, down_weight, seq_lengths)
    if not fits(z):
        return on_device_plain(
            dp_size,
            inputs,
            norm_gain,
            norm_shift,
            qkv_weight,
            qkv_bias,
            up_weight,
            up_bias,
            dense_weight,
            down_weight,
            out_bias,
            cotangent,
            seq_lengths,
            seq_owner,
        )
    rows, q, line = z.rows, z.quarter, z.line
    lane_rate = np.zeros((1, HEAD_DIM), np.float32)
    lane_rate[0, :ROT] = rope_base ** (-2.0 * (np.arange(ROT) % HALF_ROT) / ROT)
    operands = dict(
        inputs=(inputs, pl.ANY),
        cot=(cotangent, pltpu.VMEM),
        norm_gain=(norm_gain, pltpu.VMEM),
        norm_shift=(norm_shift, pltpu.VMEM),
        qkv_bias=(qkv_bias, pltpu.VMEM),
        up_bias=(up_bias, pltpu.VMEM),
        out_bias=(out_bias, pltpu.VMEM),
        frequency=(jnp.asarray(lane_rate), pltpu.VMEM),
        seq_lengths=(seq_lengths, pltpu.SMEM),
        seq_owner=(seq_owner, pltpu.SMEM),
        up_w=(up_weight, pl.ANY),
        down_w=(down_weight, pl.ANY),
        qkv_w=(qkv_weight, pl.ANY),
        dense_w=(dense_weight, pl.ANY),
    )
    results = dict(
        outputs=((rows, q), bf16, pltpu.VMEM),
        grad_inputs=((rows, q), f32, pltpu.VMEM),
        small=((1, 3 * q + z.qkv + z.hidden), f32, pltpu.VMEM),
        up_o=((z.half, z.hidden), bf16, pl.ANY),
        down_o=((z.hidden, z.half), bf16, pl.ANY),
        qkv_o=((z.half, z.qkv), bf16, pl.ANY),
        dense_o=((z.features, z.half), bf16, pl.ANY),
        end_cot=((2, 2, rows, q), bf16, pl.ANY),
        end_act=((line, 2, rows, z.down_chunk), bf16, pl.ANY),
        end_att=((line, 2, rows, z.dense_chunk), bf16, pl.ANY),
    )
    for name, shape in flows_of(z).items():
        results["land_" + name] = ((line + 2, 2) + shape, bf16, pl.ANY)
        results["own_" + name] = ((2,) + shape, bf16, pl.ANY)
    scratch = scratch_of(z)
    names = list(operands) + list(results) + list(scratch) + ["send_sem", "recv_sem", "local_sem"]
    found = pl.pallas_call(
        partial(layer_kernel, z, names),
        in_specs=[pl.BlockSpec(memory_space=space) for value, space in operands.values()],
        out_specs=[pl.BlockSpec(memory_space=space) for shape, kind, space in results.values()],
        out_shape=[jax.ShapeDtypeStruct(shape, kind) for shape, kind, space in results.values()],
        scratch_shapes=[pltpu.VMEM(shape, kind) for shape, kind in scratch.values()]
        + [pltpu.SemaphoreType.DMA((SENDS * line,)), pltpu.SemaphoreType.DMA((SENDS * line,)), pltpu.SemaphoreType.DMA((16,))],
        compiler_params=pltpu.CompilerParams(
            collective_id=0, has_side_effects=True, vmem_limit_bytes=VMEM_LIMIT
        ),
        name="layer",
    )(*[value for value, space in operands.values()])
    got = dict(zip(results, found))
    big, small = finish(z, got)
    return (
        big["outputs"],
        big["grad_inputs"],
        small["gain"],
        small["shift"],
        big["qkv"],
        small["qkv"],
        big["up"],
        small["up"],
        big["dense"],
        big["down"],
        small["out"],
    )


def finish(z, got):
    line, steps = z.line, 8
    flows = flows_of(z)
    names = list(flows)
    pieces = dict(gain=z.quarter, shift=z.quarter, qkv=z.qkv, up=z.hidden, out=z.quarter)

    def kernel(*refs):
        place = lax.axis_index("dp") // 2
        fed = refs[: 3 * len(names) + 3]
        made = refs[3 * len(names) + 3 :]
        for index in range(len(names)):
            own, from_left, from_right = (ref[...].astype(f32) for ref in fed[3 * index : 3 * index + 3])
            far = 1 if names[index] in ("down", "dense") else 0
            total = own + jnp.where(place > far, from_left, 0.0) + jnp.where(place < line - 1 - far, from_right, 0.0)
            made[index][...] = total.reshape(made[index].shape)
        outputs, grad_inputs, small = fed[3 * len(names) :]
        made[len(names)][...] = outputs[...]
        made[len(names) + 1][...] = grad_inputs[...]

        @pl.when(pl.program_id(0) == 0)
        def _():
            start = 0
            for index, width in enumerate(pieces.values()):
                made[len(names) + 2 + index][...] = small[:, start : start + width].reshape(width)
                start += width

    in_specs, out_specs, out_shape, fed = [], [], [], []
    for name in names:
        count, depth, each = flows[name]
        group = count // (steps // 2) or 1

        def tile_index(step, name=name):
            half, tile = step // (steps // 2), lax.rem(step, steps // 2)
            return half, tile if flows[name][0] >= steps // 2 else 0

        block = (None, group, depth, each)
        land_block = (None, None, group, depth, each)
        in_specs.append(pl.BlockSpec(block, lambda i, f=tile_index: (*f(i), 0, 0)))
        in_specs.append(pl.BlockSpec(land_block, lambda i, f=tile_index: (line, *f(i), 0, 0)))
        in_specs.append(pl.BlockSpec(land_block, lambda i, f=tile_index: (line + 1, *f(i), 0, 0)))
        fed += [got["own_" + name], got["land_" + name], got["land_" + name]]
        if name == "down":
            out_shape.append(jax.ShapeDtypeStruct((count * depth, 2 * each), f32))
            out_specs.append(pl.BlockSpec((group * depth, each), lambda i, f=tile_index: f(i)[::-1]))
        else:
            assert group == 1
            out_shape.append(jax.ShapeDtypeStruct((depth, 2 * count * each), f32))
            out_specs.append(
                pl.BlockSpec((depth, each), lambda i, f=tile_index, count=count: (0, f(i)[0] * count + f(i)[1]))
            )
    for name in ("outputs", "grad_inputs"):
        rows, columns = got[name].shape
        spec = pl.BlockSpec((rows // steps, columns), lambda i: (i, 0))
        in_specs.append(spec)
        out_specs.append(spec)
        out_shape.append(jax.ShapeDtypeStruct((rows, columns), got[name].dtype))
        fed.append(got[name])
    in_specs.append(pl.BlockSpec(memory_space=pltpu.VMEM))
    fed.append(got["small"])
    for width in pieces.values():
        out_specs.append(pl.BlockSpec(memory_space=pltpu.VMEM))
        out_shape.append(jax.ShapeDtypeStruct((width,), f32))
    made = pl.pallas_call(
        kernel, grid=(steps,), in_specs=in_specs, out_specs=out_specs, out_shape=out_shape, name="finish"
    )(*fed)
    big = dict(zip(names + ["outputs", "grad_inputs"], made))
    return big, dict(zip(pieces, made[len(names) + 2 :]))


def attention_kernel(proj_ref, mixed_ref, tables_ref, seg_col_ref, seg_row_ref, attended_ref, grad_ref):
    attended_ref[...], grad_ref[...] = attention_pair(
        proj_ref[...], mixed_ref[...], tables_ref, seg_col_ref[...], seg_row_ref[...]
    )


def attention(projected, mixed, tables, segment):
    rows, width = projected.shape
    pairs = width // PAIR_QKV
    return pl.pallas_call(
        attention_kernel,
        grid=(pairs,),
        in_specs=[
            pl.BlockSpec((rows, PAIR_QKV), lambda i: (0, i)),
            pl.BlockSpec((rows, PAIR), lambda i: (0, i)),
            pl.BlockSpec((3, rows, HEAD_DIM), lambda i: (0, 0, 0)),
            pl.BlockSpec((rows, 1), lambda i: (0, 0)),
            pl.BlockSpec((1, rows), lambda i: (0, 0)),
        ],
        out_specs=[
            pl.BlockSpec((rows, PAIR), lambda i: (0, i)),
            pl.BlockSpec((rows, PAIR_QKV), lambda i: (0, i)),
        ],
        out_shape=[
            jax.ShapeDtypeStruct((rows, pairs * PAIR), bf16),
            jax.ShapeDtypeStruct((rows, width), bf16),
        ],
        compiler_params=pltpu.CompilerParams(vmem_limit_bytes=48 * 1024 * 1024),
        cost_estimate=pl.CostEstimate(
            flops=14 * 2 * pairs * rows * rows * HEAD_DIM * 2,
            bytes_accessed=rows * width * 7,
            transcendentals=2 * pairs * rows * rows,
        ),
        name="attention",
    )(projected, mixed, tables, segment[:, None], segment[None, :])


def dot_plain(left, right):
    return jnp.dot(left, right, preferred_element_type=f32)


def contract_rows(left, right):
    return lax.dot_general(left, right, (((0,), (0,)), ((), ())), preferred_element_type=f32)


def contract_cols(left, right):
    return lax.dot_general(left, right, (((1,), (1,)), ((), ())), preferred_element_type=f32)


def on_device_plain(
    dp_size,
    inputs,
    norm_gain,
    norm_shift,
    qkv_weight,
    qkv_bias,
    up_weight,
    up_bias,
    dense_weight,
    down_weight,
    out_bias,
    cotangent,
    seq_lengths,
    seq_owner,
):
    row_count = inputs.shape[0]
    line = dp_size // 2
    device = lax.axis_index("dp")
    place = device // 2
    side = device % 2
    row = lax.axis_index("row")
    col = lax.axis_index("col")

    over_row = partial(lax.ppermute, axis_name="row", perm=[(0, 1), (1, 0)])
    over_col = partial(lax.ppermute, axis_name="col", perm=[(0, 1), (1, 0)])
    over_side = partial(lax.ppermute, axis_name="dp", perm=[(e, e ^ 1) for e in range(dp_size)])

    def in_order(index, mine, other, axis):
        first = jnp.where(index == 0, mine, other)
        second = jnp.where(index == 0, other, mine)
        return jnp.concatenate([first, second], axis=axis)

    def half_at(array, index, axis):
        width = array.shape[axis] // 2
        return lax.dynamic_slice_in_dim(array, index * width, width, axis)

    segment, position, is_valid = layout(seq_lengths, seq_owner, device, row_count)
    tables = rotation_tables(position)

    gains = jnp.stack([norm_gain, norm_shift])
    grad_branch = cotangent * is_valid.astype(bf16)[:, None]
    inputs_half = in_order(row, inputs, over_row(inputs), 1)
    gains_half = in_order(row, gains, over_row(gains), 1)
    inputs_other = over_col(inputs_half)
    gains_other = over_col(gains_half)
    branch_half = in_order(row, grad_branch, over_row(grad_branch), 1)
    branch_other = over_col(branch_half)

    up_mine, up_other = half_at(up_weight, col, 1), over_col(half_at(up_weight, 1 - col, 1))
    down_mine, down_other = half_at(down_weight, col, 0), over_col(half_at(down_weight, 1 - col, 0))
    qkv_mine, qkv_other = half_at(qkv_weight, col, 1), over_col(half_at(qkv_weight, 1 - col, 1))
    dense_mine, dense_other = half_at(dense_weight, col, 0), over_col(half_at(dense_weight, 1 - col, 0))

    width = 4 * inputs.shape[1]
    source, source_other = inputs_half.astype(f32), inputs_other.astype(f32)
    average = (jnp.sum(source, axis=1) + jnp.sum(source_other, axis=1)) / width
    square = (jnp.sum(source * source, axis=1) + jnp.sum(source_other * source_other, axis=1)) / width
    scale_inv = lax.rsqrt(square - average * average + epsilon)[:, None]

    def hidden_of(rows_in, gain_pair):
        normed = (rows_in - average[:, None]) * scale_inv
        pair = gain_pair.astype(f32)
        return (normed * pair[0] + pair[1]).astype(bf16)

    hidden, hidden_other = hidden_of(source, gains_half), hidden_of(source_other, gains_other)

    before = dot_plain(hidden, up_mine) + dot_plain(hidden_other, up_other) + up_bias.astype(f32)
    activated = jax.nn.gelu(before, approximate=True).astype(bf16)
    d_activated = contract_cols(branch_half, down_mine) + contract_cols(branch_other, down_other)
    unused_value, gelu_back = jax.vjp(partial(jax.nn.gelu, approximate=True), before)
    d_before = gelu_back(d_activated)[0].astype(bf16)

    projected = dot_plain(hidden, qkv_mine) + dot_plain(hidden_other, qkv_other) + qkv_bias.astype(f32)
    d_mixed = (contract_cols(branch_half, dense_mine) + contract_cols(branch_other, dense_other)).astype(bf16)
    attended, d_projected = attention(projected, d_mixed, tables, segment)

    def chunks_of(array, index):
        rows, columns = array.shape
        grouped = array.reshape(rows, columns // (2 * chunk), 2, chunk)
        return lax.dynamic_index_in_dim(grouped, index, 2, keepdims=False).reshape(rows, columns // 2)

    branch_pair = over_side(branch_half)

    def feature_sums(array):
        kept = chunks_of(array, side)
        got = over_side(chunks_of(array, 1 - side))
        own = in_order(col, kept, over_col(kept), 1)
        pair = in_order(col, got, over_col(got), 1)
        return (contract_rows(own, branch_half) + contract_rows(pair, branch_pair)).astype(bf16)

    def along_line(sums):
        depth = sums.shape[0] // line
        parts = sums.reshape(line, depth, sums.shape[1])

        def part(index):
            return lax.dynamic_index_in_dim(parts, jnp.clip(index, 0, line - 1), 0, keepdims=False).astype(f32)

        rightward, leftward = None, None
        for step in range(line - 1):
            right_part = part(line - 1 - step + place)
            left_part = part(place - (line - 1) + step)
            if step:
                right_part = right_part + rightward.astype(f32)
                left_part = left_part + leftward.astype(f32)
            to_right = [(2 * z + x, 2 * z + 2 + x) for z in range(min(step + 1, line - 1)) for x in range(2)]
            to_left = [(dp_size - 1 - p, dp_size - 1 - q) for p, q in to_right]
            rightward = lax.ppermute(right_part.astype(bf16), "dp", to_right)
            leftward = lax.ppermute(left_part.astype(bf16), "dp", to_left)
        return part(place) + rightward.astype(f32) + leftward.astype(f32)

    chunk = down_weight.shape[0] // dp_size
    grad_down = along_line(feature_sums(activated))

    chunk = up_weight.shape[0] // dp_size
    hidden_own = chunks_of(hidden, side)
    hidden_pair = over_side(chunks_of(hidden, 1 - side))

    def hidden_sums(array):
        pair = over_side(array)
        mine = (contract_rows(hidden_own, array) + contract_rows(hidden_pair, pair)).astype(bf16)
        theirs = (contract_rows(hidden_own, over_col(array)) + contract_rows(hidden_pair, over_col(pair))).astype(bf16)
        return in_order(col, along_line(mine), along_line(theirs), 1)

    grad_up = hidden_sums(d_before)
    chunk = dense_weight.shape[0] // dp_size
    grad_dense = along_line(feature_sums(attended))
    grad_qkv = hidden_sums(d_projected)

    def scatter(mine, other):
        half = mine + over_col(other.astype(bf16)).astype(f32)
        return half_at(half, row, 1) + over_row(half_at(half, 1 - row, 1).astype(bf16)).astype(f32)

    branch = scatter(
        dot_plain(attended, dense_mine) + dot_plain(activated, down_mine),
        dot_plain(attended, dense_other) + dot_plain(activated, down_other),
    )
    valid_col = is_valid.astype(f32)[:, None]
    outputs = (inputs.astype(f32) + valid_col * (branch + out_bias.astype(f32))).astype(bf16)

    d_hidden = scatter(
        contract_cols(d_projected, qkv_mine) + contract_cols(d_before, up_mine),
        contract_cols(d_projected, qkv_other) + contract_cols(d_before, up_other),
    )
    normed = (inputs.astype(f32) - average[:, None]) * scale_inv
    d_normed = d_hidden * norm_gain.astype(f32)
    row_sums = jnp.stack([jnp.sum(d_normed, axis=1), jnp.sum(d_normed * normed, axis=1)])
    row_sums = row_sums + over_row(row_sums)
    row_sums = row_sums + over_col(row_sums)
    grad_inputs = cotangent.astype(f32) + scale_inv * (
        d_normed - row_sums[0][:, None] / width - normed * row_sums[1][:, None] / width
    )

    small = [
        jnp.sum(d_hidden * normed, axis=0),
        jnp.sum(d_hidden, axis=0),
        jnp.sum(d_projected.astype(f32), axis=0),
        jnp.sum(d_before.astype(f32), axis=0),
        jnp.sum(grad_branch.astype(f32), axis=0),
    ]
    together = jnp.concatenate(small)
    bit = 1
    while bit < dp_size:
        together = together + lax.ppermute(together, "dp", [(e, e ^ bit) for e in range(dp_size)])
        bit *= 2
    ends = []
    for piece in small:
        ends.append((ends[-1] if ends else 0) + piece.shape[0])
    grad_gain, grad_shift, grad_qkv_bias, grad_up_bias, grad_out_bias = jnp.split(together, ends[:-1])
    return (
        outputs,
        grad_inputs,
        grad_gain,
        grad_shift,
        grad_qkv,
        grad_qkv_bias,
        grad_up,
        grad_up_bias,
        grad_dense,
        grad_down,
        grad_out_bias,
    )


def solution(mesh):
    in_specs = (
        P("dp", ("col", "row")),
        P(("col", "row")),
        P(("col", "row")),
        P("col", "row"),
        P(("row", "col")),
        P("col", "row"),
        P(("row", "col")),
        P("row", "col"),
        P("row", "col"),
        P(("col", "row")),
        P("dp", ("col", "row")),
        P(),
        P(),
    )
    out_specs = (
        P("dp", ("col", "row")),
        P("dp", ("col", "row")),
        P(("col", "row")),
        P(("col", "row")),
        P(("col", "dp"), "row"),
        P(("row", "col")),
        P(("col", "dp"), "row"),
        P(("row", "col")),
        P(("row", "dp"), "col"),
        P(("row", "dp"), "col"),
        P(("col", "row")),
    )
    return jax.shard_map(
        partial(on_device, mesh.shape["dp"]), mesh=mesh, in_specs=in_specs, out_specs=out_specs, check_vma=False
    )
```

```python
from functools import partial
import math

import jax
import jax.numpy as jnp
import numpy as np
from jax import lax
from jax.experimental import pallas as pl
from jax.experimental.pallas import tpu as pltpu
from jax.sharding import PartitionSpec as P

HEAD_DIM = 64
ROT = 32
HALF_ROT = ROT // 2
PAIR = 2 * HEAD_DIM
PAIR_QKV = 3 * PAIR

epsilon = 1e-05
masked_score = -1e30
rope_base = 10000.0
VMEM_LIMIT = 67_000_000
SCRATCH_LIMIT = 58 * 1024 * 1024
SENDS = 48
LOCALS = 20
score_scale = HEAD_DIM ** (-0.5)
bf16 = jnp.bfloat16
f32 = jnp.float32


def layout(seq_lengths, seq_owner, device, row_count):
    owned = seq_owner == device
    lengths_owned = jnp.where(owned, seq_lengths, 0)
    seq_ends = jnp.cumsum(lengths_owned, dtype=jnp.int32)
    seq_starts = seq_ends - lengths_owned
    slot_index = jnp.arange(row_count, dtype=jnp.int32)
    segment = jnp.sum((seq_ends[None, :] <= slot_index[:, None]).astype(jnp.int32), axis=1)
    picked = jnp.arange(seq_lengths.shape[0], dtype=jnp.int32)[None, :] == segment[:, None]
    seq_begin = jnp.sum(jnp.where(picked, seq_starts[None, :], 0), axis=1)
    position = slot_index - seq_begin
    is_valid = slot_index < seq_ends[-1]
    return (segment, position, is_valid)


def rotation_tables(position):
    index_range = jnp.arange(HALF_ROT, dtype=f32)
    frequency = rope_base ** (-2.0 * index_range / ROT)
    phase = position.astype(f32)[:, None] * frequency[None, :]
    cosines, sines = jnp.cos(phase), jnp.sin(phase)
    rows = position.shape[0]
    ones = jnp.ones((rows, HEAD_DIM - ROT), f32)
    none = jnp.zeros((rows, HALF_ROT), f32)
    rest = jnp.zeros((rows, HEAD_DIM - ROT), f32)
    same = jnp.concatenate([cosines, cosines, ones], axis=1)
    from_right = jnp.concatenate([sines, none, rest], axis=1)
    from_left = jnp.concatenate([none, sines, rest], axis=1)
    return jnp.stack([same, from_right, from_left])


def turned(array):
    return jnp.swapaxes(array, 0, 1)


def contract(left, right, left_dim, right_dim):
    dims = (((left_dim,), (right_dim,)), ((), ()))
    return lax.dot_general(left, right, dims, preferred_element_type=f32)


gelu_rate = math.sqrt(2.0 / math.pi)
gelu_cube = 0.044715


def gelu(x):
    return 0.5 * x * (1.0 + jnp.tanh(gelu_rate * (x + gelu_cube * x * x * x)))


def gelu_slope(x):
    square = x * x
    bent = jnp.tanh(gelu_rate * (x + gelu_cube * x * square))
    return 0.5 * (1.0 + bent) + 0.5 * x * (1.0 - bent * bent) * (gelu_rate * (1.0 + 3.0 * gelu_cube * square))


def attention_pair(proj, mixed, tables, seg_col, seg_row):
    rows = proj.shape[0]
    block = min(256, rows)
    same, from_right, from_left = tables[0], tables[1], tables[2]

    def rotate(part, sign):
        right = jnp.concatenate([part[:, HALF_ROT:], part[:, :HALF_ROT]], axis=1)
        left = jnp.concatenate([part[:, HEAD_DIM - HALF_ROT :], part[:, : HEAD_DIM - HALF_ROT]], axis=1)
        return part * same - sign * (right * from_right) + sign * (left * from_left)

    attended_heads, grads = [], []
    for head in range(2):
        base = head * 3 * HEAD_DIM
        queries = rotate(proj[:, base : base + HEAD_DIM], 1.0).astype(bf16)
        keys = rotate(proj[:, base + HEAD_DIM : base + 2 * HEAD_DIM], 1.0).astype(bf16)
        values = proj[:, base + 2 * HEAD_DIM : base + 3 * HEAD_DIM].astype(bf16)
        d_outs = mixed[:, head * HEAD_DIM : (head + 1) * HEAD_DIM]
        outs, d_queries, d_keys, d_values = [], [], None, None
        for first in range(0, rows, block):
            last = first + block
            q, d_out = queries[first:last], d_outs[first:last]
            k, v = keys[:last], values[:last]
            row_index = first + lax.broadcasted_iota(jnp.int32, (block, last), 0)
            key_index = lax.broadcasted_iota(jnp.int32, (block, last), 1)
            allowed = (seg_col[first:last, :] == seg_row[:, :last]) & (key_index <= row_index)
            scores = jnp.where(allowed, contract(q, k, 1, 1) * score_scale, masked_score)
            weights = jnp.exp(scores - jnp.max(scores, axis=1, keepdims=True))
            probs = weights * (1.0 / jnp.sum(weights, axis=1, keepdims=True))
            probs_low = probs.astype(bf16)
            outs.append(contract(probs_low, v, 1, 0))
            d_probs = contract(d_out, v, 1, 1)
            row_dot = jnp.sum(probs * d_probs, axis=1, keepdims=True)
            d_scores = (probs * (d_probs - row_dot)).astype(bf16)
            d_queries.append(contract(d_scores, k, 1, 0))
            key_part = contract(d_scores, q, 0, 0)
            value_part = contract(probs_low, d_out, 0, 0)
            if d_keys is None:
                d_keys, d_values = key_part, value_part
            else:
                d_keys = jnp.concatenate([key_part[:first] + d_keys, key_part[first:]], axis=0)
                d_values = jnp.concatenate([value_part[:first] + d_values, value_part[first:]], axis=0)
        attended_heads.append(jnp.concatenate(outs, axis=0))
        grads.append(rotate(jnp.concatenate(d_queries, axis=0) * score_scale, -1.0))
        grads.append(rotate(d_keys * score_scale, -1.0))
        grads.append(d_values)
    attended = jnp.concatenate(attended_heads, axis=1).astype(bf16)
    return attended, jnp.concatenate(grads, axis=1).astype(bf16)


class Sizes:
    def __init__(self, dp_size, inputs, qkv_weight, up_weight, dense_weight, down_weight, seq_lengths):
        self.dp = dp_size
        self.seqs = seq_lengths.shape[0]
        self.line = dp_size // 2
        self.rows, self.quarter = inputs.shape
        self.half = up_weight.shape[0]
        self.width = 2 * self.half
        self.up_chunk = self.half // dp_size
        self.down_chunk = down_weight.shape[0] // dp_size
        self.dense_chunk = dense_weight.shape[0] // dp_size
        self.hidden = up_weight.shape[1] // 2
        self.tiles = self.hidden // self.down_chunk
        self.qkv = qkv_weight.shape[1] // 2
        self.pairs = self.qkv // PAIR_QKV
        self.features = dense_weight.shape[0] // 2


def flows_of(z):
    return dict(
        down=(z.down_chunk // z.up_chunk, z.up_chunk, z.quarter),
        up=(z.tiles, z.up_chunk, z.down_chunk),
        dense=(1, z.dense_chunk, z.quarter),
        qkv=(z.pairs, z.up_chunk, PAIR_QKV),
    )


def scratch_of(z):
    rows, q, line, tiles, pairs = z.rows, z.quarter, z.line, z.tiles, z.pairs
    up, down, dense = z.up_chunk, z.down_chunk, z.dense_chunk
    shapes = dict(
        inq=((2, 2, rows, q), bf16),
        cotq=((2, 2, rows, q), bf16),
        cotp=((2, rows, q), bf16),
        gainq=((2, 2, 16, q), f32),
        seg_col=((rows, 1), f32),
        seg_row=((1, rows), f32),
        tables=((3, rows, HEAD_DIM), f32),
        up_b=((tiles, 1, down), f32),
        qkv_b=((pairs, 1, PAIR_QKV), f32),
        sums=((1, 3 * q + z.qkv + z.hidden), f32),
        sums_got=((3, 1, 3 * q + z.qkv + z.hidden), f32),
        sums_send=((2, 1, 3 * q + z.qkv + z.hidden), f32),
        hid=((2, rows, z.half), bf16),
        hid_own=((rows, line * up), bf16),
        hid_send=((rows, line * up), bf16),
        hid_pair=((rows, line * up), bf16),
        stat=((2, rows, 1), f32),
        before=((tiles, rows, down), f32),
        act=((tiles, rows, down), bf16),
        act_own=((line, rows, down), bf16),
        act_pair=((line, rows, down), bf16),
        db_mine=((tiles, rows, down), bf16),
        db_theirs=((tiles, rows, down), bf16),
        db_mine_pair=((tiles, rows, down), bf16),
        db_theirs_pair=((tiles, rows, down), bf16),
        mixed=((pairs, rows, PAIR), bf16),
        att=((rows, z.features), bf16),
        att_part=((line, rows, dense), bf16),
        att_own=((line, rows, dense), bf16),
        att_pair=((line, rows, dense), bf16),
        dp_mine=((pairs, rows, PAIR_QKV), bf16),
        dp_theirs=((pairs, rows, PAIR_QKV), bf16),
        dp_mine_pair=((pairs, rows, PAIR_QKV), bf16),
        dp_theirs_pair=((pairs, rows, PAIR_QKV), bf16),
        weight=((2, 2, z.half, 512), bf16),
        st_down=((line, 2) + flows_of(z)["down"], bf16),
        st_up=((line, 2) + flows_of(z)["up"], bf16),
        st_dense=((line, 2) + flows_of(z)["dense"], bf16),
        got_down=(flows_of(z)["down"], bf16),
        got_dense=(flows_of(z)["dense"], bf16),
        part_send=((2, rows, q), bf16),
        part_row=((rows, q), bf16),
        out_row=((rows, q), bf16),
        dh_row=((rows, q), bf16),
        sum_send=((2, 8, rows), f32),
        sum_got=((2, 8, rows), f32),
    )
    return shapes


def fits(z):
    total = 0
    for shape, kind in scratch_of(z).values():
        total += math.prod(shape[:-1]) * -(-shape[-1] // 128) * 128 * jnp.dtype(kind).itemsize
    flows = flows_of(z)
    alike = flows["down"] == flows["up"] and flows["qkv"][:2] == flows["up"][:2] and flows["qkv"][2] <= flows["up"][2]
    square = z.rows == z.quarter and (z.tiles, z.rows, z.down_chunk) == (4, z.rows, z.quarter)
    return z.line == 4 and alike and square and total <= SCRATCH_LIMIT


def layer_kernel(z, names, *refs):
    r = dict(zip(names, refs))
    rows, q, line, tiles, pairs = z.rows, z.quarter, z.line, z.tiles, z.pairs
    half_line = line // 2
    r["total"] = r["before"]
    r["dh_got"], r["out_got"] = r["inq"].at[1], r["cotq"].at[1]
    r["got_up"] = r["got_qkv"] = r["got_down"]
    r["st_qkv"] = r["st_down"]
    dp = lax.axis_index("dp")
    row = lax.axis_index("row")
    col = lax.axis_index("col")
    place, side = dp // 2, lax.rem(dp, 2)
    other_row, other_col, other_side = 1 - row, 1 - col, 1 - side
    to_row = {"row": other_row}
    to_col = {"col": other_col}
    to_side = {"dp": dp + 1 - 2 * side}
    MESH = pl.DeviceIdType.MESH

    marks = dict(send=0, recv=0, local=0)

    def take(kind, count):
        first = marks[kind]
        marks[kind] += count
        return first

    def remote(src, dst, send, recv, device):
        return pltpu.make_async_remote_copy(
            src_ref=src,
            dst_ref=dst,
            send_sem=r["send_sem"].at[send],
            recv_sem=r["recv_sem"].at[recv],
            device_id=device,
            device_id_type=MESH,
        )

    pending = []

    class Message:
        def __init__(self, src, dst, device, got=None):
            index = (take("send", 1), take("recv", 1))
            self.copy = lambda: remote(src, dst, *index, device)
            self.got = lambda: remote(src if got is None else got, dst if got is None else got, *index, device)

        def start(self):
            self.copy().start()
            pending.append(self)

        def wait(self):
            self.got().wait_recv()

    right, left = {"dp": dp + 2}, {"dp": dp - 2}
    has_right, has_left = place < line - 1, place > 0
    at_end, near_end = (place == 0) | (place == line - 1), (place == 1) | (place == line - 2)
    inward, outward = {"dp": dp + 2 - 4 * (place > 0)}, {"dp": dp + 2 - 4 * (place == 1)}
    mate = {"dp": dp - 2 + 4 * (place == 1)}
    first_half = place < line // 2

    def counted(chunk):
        return jnp.where(first_half, chunk, line - 1 - chunk)

    barrier = pltpu.get_barrier_semaphore()
    for device in (to_row, to_col, to_side):
        pl.semaphore_signal(barrier, inc=1, device_id=device, device_id_type=MESH)

    @pl.when(has_right)
    def _():
        pl.semaphore_signal(barrier, inc=1, device_id=right, device_id_type=MESH)

    @pl.when(has_left)
    def _():
        pl.semaphore_signal(barrier, inc=1, device_id=left, device_id_type=MESH)

    slots = lax.broadcasted_iota(jnp.int32, (8, rows), 1)

    def add_sequence(number, carry):
        end, segments, begins = carry
        start = end
        end = start + jnp.where(r["seq_owner"][number] == dp, r["seq_lengths"][number], 0)
        segments = segments + (end <= slots).astype(jnp.int32)
        begins = jnp.where((start <= slots) & (slots < end), start, begins)
        return end, segments, begins

    nothing = jnp.zeros((8, rows), jnp.int32)
    segments, begins = lax.fori_loop(0, z.seqs, add_sequence, (jnp.int32(0), nothing, nothing))[1:]
    segments = segments.astype(f32)
    r["seg_row"][...] = segments[:1]
    r["seg_col"][...] = turned(segments)[:, :1]
    cot = r["cot"]
    valid = (r["seg_col"][...] < z.seqs).astype(f32)
    r["cotq"][0, row] = cot[...] * valid.astype(bf16)

    def as_row(vector):
        return vector.astype(f32).reshape(1, vector.shape[0])

    r["gainq"][0, row] = jnp.concatenate(
        [
            jnp.broadcast_to(as_row(r["norm_gain"][...]), (8, q)),
            jnp.broadcast_to(as_row(r["norm_shift"][...]), (8, q)),
        ]
    )
    pl.semaphore_wait(barrier, 3 + has_right.astype(jnp.int32) + has_left.astype(jnp.int32))

    def gather(src, held):
        over = Message(src, held.at[0, row], to_row, held.at[0, other_row])
        across = Message(src, held.at[1, row], to_col, held.at[1, row])
        onward = Message(held.at[0, other_row], held.at[1, other_row], to_col, held.at[1, other_row])
        return over, across, onward

    in_over, in_across, in_onward = gather(r["inputs"], r["inq"])
    gain_over, gain_across, gain_onward = gather(r["gainq"].at[0, row], r["gainq"])
    cot_over, cot_across, cot_onward = gather(r["cotq"].at[0, row], r["cotq"])
    cot_side = Message(r["cotq"].at[0, row], r["cotp"].at[row], to_side)
    cot_side_onward = Message(r["cotq"].at[0, other_row], r["cotp"].at[other_row], to_side)
    hid_side = Message(r["hid_send"], r["hid_pair"], to_side)

    end_cot_send, end_cot_recv = take("send", 4), take("recv", 4)

    def end_cot(pair, part, device):
        src = r["cotp"].at[part] if pair else r["cotq"].at[0, part]
        index = 2 * pair + part
        return remote(src, r["end_cot"].at[pair, part], end_cot_send + index, end_cot_recv + index, device)

    def send_end_cot(pair, part):
        @pl.when(at_end)
        def _():
            end_cot(pair, part, inward).start()

    def loop(first, last, work):
        def one(k, carry):
            work(k)
            return carry

        lax.fori_loop(first, last, one, 0)

    def pass_on(got, onward):
        def work(k):
            got(k).wait_recv()
            onward(k).start()

        return work

    def waits(*copies):
        def work(k):
            for copy in copies:
                copy(k).wait_recv()

        return work

    class EndRows:
        def __init__(self, own, pair, land):
            self.own, self.pair, self.land = own, pair, land
            self.send, self.recv = take("send", line), take("recv", line)
            self.on_send, self.on_recv = take("send", line), take("recv", line)

        def copy(self, chunk, device, pair):
            src = (self.pair if pair else self.own).at[chunk]
            return remote(src, self.land.at[chunk, int(pair)], self.send + chunk, self.recv + chunk, device)

        def onward(self, chunk):
            part = self.land.at[chunk, col]
            return remote(part, part, self.on_send + chunk, self.on_recv + chunk, to_col)

        def start(self, pair, first, last):
            kind = 1 if pair else 0

            @pl.when(at_end & (col == kind))
            def _():
                def one(number):
                    chunk = jnp.where(place == 0, line - 1 - number, number)
                    self.copy(chunk, inward, pair).start()

                loop(first, last, one)

        def hand_over(self, *numbers):
            @pl.when(near_end)
            def _():
                for number in numbers:
                    chunk = counted(line - 1 - number)
                    self.copy(chunk, outward, False).wait_recv()
                    self.onward(chunk).start()

        def finish(self):
            def one(chunk):
                @pl.when(at_end & (chunk != place))
                def _():
                    self.copy(chunk, inward, False).wait_send()

                @pl.when(near_end)
                def _():
                    gone = jnp.where(place == 1, 0, line - 1)

                    @pl.when(chunk != gone)
                    def _():
                        self.onward(chunk).wait_send()

            loop(0, line, one)

    end_act = EndRows(r["act_own"], r["act_pair"], r["end_act"])
    end_att = EndRows(r["att_own"], r["att_pair"], r["end_att"])
    swaps = {
        "up": Message(r["up_w"].at[:, pl.ds(pl.multiple_of(other_col * z.hidden, 128), z.hidden)], r["up_o"], to_col, r["up_o"]),
        "qkv": Message(r["qkv_w"].at[:, pl.ds(pl.multiple_of(other_col * z.qkv, 128), z.qkv)], r["qkv_o"], to_col, r["qkv_o"]),
        "down": Message(r["down_w"].at[pl.ds(pl.multiple_of(other_col * z.hidden, 16), z.hidden), :], r["down_o"], to_col, r["down_o"]),
        "dense": Message(r["dense_w"].at[pl.ds(pl.multiple_of(other_col * z.features, 16), z.features), :], r["dense_o"], to_col, r["dense_o"]),
    }

    def local(src, dst, index):
        return pltpu.make_async_copy(src, dst, r["local_sem"].at[index])

    stream_base = take("local", 8)
    once = take("local", 4)

    in_over.start()
    gain_over.start()
    in_across.start()
    gain_across.start()
    keep_in = local(r["inputs"], r["inq"].at[0, row], once)
    keep_in.start()
    cot_side.start()
    send_end_cot(0, row)
    swaps["up"].start()
    up_bias, qkv_bias = as_row(r["up_bias"][...]), as_row(r["qkv_bias"][...])
    for tile in range(tiles):
        r["up_b"][tile] = up_bias[:, tile * z.down_chunk : (tile + 1) * z.down_chunk]
    for pair in range(pairs):
        r["qkv_b"][pair] = qkv_bias[:, pair * PAIR_QKV : (pair + 1) * PAIR_QKV]
    position = turned((slots - begins).astype(f32))[:, :1]
    phase = position * r["frequency"][...]
    lane = lax.broadcasted_iota(jnp.int32, (1, HEAD_DIM), 1)
    sines = jnp.sin(phase)
    r["tables"][0] = jnp.where(lane < ROT, jnp.cos(phase), 1.0)
    r["tables"][1] = jnp.where(lane < HALF_ROT, sines, 0.0)
    r["tables"][2] = jnp.where((lane >= HALF_ROT) & (lane < ROT), sines, 0.0)
    gain_over.wait()
    gain_onward.start()
    in_over.wait()
    in_onward.start()
    cot_over.start()
    cot_across.start()
    cot_side.wait()
    send_end_cot(1, row)
    keep_in.wait()
    gain_across.wait()
    gain_onward.wait()
    in_across.wait()
    in_onward.wait()

    block = min(64, rows)

    def norm_rows(step, carry):
        at = pl.ds(pl.multiple_of(step * block, block), block)
        parts = [r["inq"][h, p, at].astype(f32) for h in range(2) for p in range(2)]
        total = parts[0] + parts[1] + parts[2] + parts[3]
        squares = parts[0] * parts[0] + parts[1] * parts[1] + parts[2] * parts[2] + parts[3] * parts[3]
        average = jnp.sum(total, axis=1, keepdims=True) / z.width
        variance = jnp.sum(squares, axis=1, keepdims=True) / z.width - average * average
        scale_inv = lax.rsqrt(variance + epsilon)
        r["stat"][0, at] = average
        r["stat"][1, at] = scale_inv
        for h in range(2):
            for p in range(2):
                normed = (parts[2 * h + p] - average) * scale_inv
                gain, shift = r["gainq"][h, p, 0:1, :], r["gainq"][h, p, 8:9, :]
                r["hid"][h, at, p * q : (p + 1) * q] = (normed * gain + shift).astype(bf16)
        return carry

    lax.fori_loop(0, rows // block, norm_rows, 0)
    for c in range(line):
        even = r["hid"][0, :, 2 * c * z.up_chunk : (2 * c + 1) * z.up_chunk]
        odd = r["hid"][0, :, (2 * c + 1) * z.up_chunk : (2 * c + 2) * z.up_chunk]
        at = slice(c * z.up_chunk, (c + 1) * z.up_chunk)
        r["hid_own"][:, at] = jnp.where(side == 0, even, odd)
        r["hid_send"][:, at] = jnp.where(side == 0, odd, even)

    def stream(count, copies, work):
        for copy in copies(jnp.int32(0), jnp.int32(0)):
            copy.start()

        def one(step, carry):
            slot = lax.rem(step, 2)

            @pl.when(step + 1 < count)
            def _():
                for copy in copies(step + 1, 1 - slot):
                    copy.start()

            for copy in copies(step, slot):
                copy.wait()
            work(step, slot)
            return carry

        lax.fori_loop(0, count, one, 0)

    def column_tiles(name, each, tile_of=lambda step: step):
        def copies(step, slot):
            tile = tile_of(step)
            mine = r[name + "_w"].at[:, pl.ds(pl.multiple_of((col * r[name + "_o"].shape[1]) + tile * each, 128), each)]
            theirs = r[name + "_o"].at[:, pl.ds(pl.multiple_of(tile * each, 128), each)]
            return [
                local(mine, r["weight"].at[slot, 0, :, :each], stream_base + slot * 4),
                local(theirs, r["weight"].at[slot, 1, :, :each], stream_base + slot * 4 + 1),
            ]

        return copies

    def row_tiles(name, each, tile_of=lambda step: step):
        def copies(step, slot):
            tile = tile_of(step)
            found = []
            for h in range(2):
                start = tile * each + (col * r[name + "_o"].shape[0] if h == 0 else 0)
                src = r[name + ("_w" if h == 0 else "_o")]
                for p in range(2):
                    found.append(
                        local(
                            src.at[pl.ds(pl.multiple_of(start, 16), each), p * q : (p + 1) * q],
                            r["weight"].at[slot, h, p * q : p * q + each, :],
                            stream_base + slot * 4 + 2 * h + p,
                        )
                    )
            return found

        return copies

    def rank_of(j):
        return jnp.where(col == 1, half_line - 1 - j, j)

    def tile_at(step):
        later = (step >= half_line).astype(jnp.int32)
        return 2 * rank_of(step - later * half_line) + jnp.where(later == 1, side, other_side)

    act_side_send, act_side_recv = take("send", half_line), take("recv", half_line)
    act_col_send, act_col_recv = take("send", half_line), take("recv", half_line)
    act_on_send, act_on_recv = take("send", half_line), take("recv", half_line)

    def act_side(j):
        tile, slot = 2 * rank_of(j) + other_side, col * half_line + rank_of(j)
        return remote(r["act"].at[tile], r["act_pair"].at[slot], act_side_send + j, act_side_recv + j, to_side)

    def act_col(j):
        slot = col * half_line + rank_of(j)
        return remote(r["act_own"].at[slot], r["act_own"].at[slot], act_col_send + j, act_col_recv + j, to_col)

    def act_on(j):
        slot = col * half_line + rank_of(j)
        return remote(r["act_pair"].at[slot], r["act_pair"].at[slot], act_on_send + j, act_on_recv + j, to_col)

    def up_work(step, slot):
        tile = tile_at(step)
        before = contract(r["hid"][0], r["weight"][slot, 0, :, : z.down_chunk], 1, 0)
        before = before + contract(r["hid"][1], r["weight"][slot, 1, :, : z.down_chunk], 1, 0)
        before = before + r["up_b"][tile]
        r["before"][tile] = before
        activated = gelu(before).astype(bf16)
        r["act"][tile] = activated

        @pl.when(step == 0)
        def _():
            act_side(0).start()

        @pl.when(step >= half_line)
        def _():
            j = step - half_line
            r["act_own"][col * half_line + rank_of(j)] = activated
            act_col(j).start()

    hid_side.start()
    swaps["down"].start()
    swaps["up"].wait()
    stream(tiles, column_tiles("up", z.down_chunk, tile_at), up_work)

    cot_over.wait()
    cot_onward.start()
    cot_side_onward.start()
    send_end_cot(0, other_row)

    def start_side(j):
        act_side(j).start()

    loop(1, half_line, start_side)
    loop(0, half_line, waits(act_col))
    end_act.start(False, 0, line - 1)
    swaps["qkv"].start()
    swaps["dense"].start()
    cot_across.wait()
    cot_onward.wait()
    swaps["down"].wait()

    def each_side(name, count):
        side_send, side_recv = take("send", count), take("recv", count)
        col_send, col_recv = take("send", count), take("recv", count)
        on_send, on_recv = take("send", count), take("recv", count)
        mine, theirs = r[name + "_mine"], r[name + "_theirs"]
        mine_pair, theirs_pair = r[name + "_mine_pair"], r[name + "_theirs_pair"]

        def to_side_peer(k):
            return remote(mine.at[k], mine_pair.at[k], side_send + k, side_recv + k, to_side)

        def to_col_peer(k):
            return remote(mine.at[k], theirs.at[k], col_send + k, col_recv + k, to_col)

        def onward(k):
            return remote(mine_pair.at[k], theirs_pair.at[k], on_send + k, on_recv + k, to_col)

        return to_side_peer, to_col_peer, onward

    db_side, db_col, db_on = each_side("db", tiles)
    dp_side, dp_col, dp_on = each_side("dp", pairs)

    def over_weight_rows(slot, each, lefts):
        total = None
        for h in range(2):
            for p in range(2):
                part = contract(lefts(h, p), r["weight"][slot, h, p * q : p * q + each, :], 1, 1)
                total = part if total is None else total + part
        return total

    def down_work(step, slot):
        tile = step
        d_activated = over_weight_rows(slot, z.down_chunk, lambda h, p: r["cotq"][h, p])
        d_before = (d_activated * gelu_slope(r["before"][tile])).astype(bf16)
        r["db_mine"][tile] = d_before
        sums = jnp.sum(d_before.astype(f32), axis=0, keepdims=True)
        r["sums"][:, pl.ds(pl.multiple_of(2 * q + z.qkv + tile * z.down_chunk, 128), z.down_chunk)] = sums
        db_col(tile).start()
        db_side(tile).start()

    stream(tiles, row_tiles("down", z.down_chunk), down_work)

    class Flow:
        def __init__(self, name, by_col=False, ends=None):
            self.name, self.by_col, self.ends = name, by_col, ends
            self.stage, self.land, self.got = r["st_" + name], r["land_" + name], r["got_" + name]
            self.count, self.depth, self.each = flows_of(z)[name]
            self.send = take("send", 2 * line)
            self.recv = take("recv", 2 * (line + 2))
            self.local = take("local", 2)
            self.done = False

        def half(self, group):
            return jnp.where(col == 0, group, 1 - group) if self.by_col else group

        def staged(self, chunk, half, tiles=slice(None)):
            return self.stage.at[chunk, half, tiles, :, : self.each]

        def copy(self, chunk, group, slot, device):
            half = self.half(group)
            return remote(
                self.staged(chunk, half),
                self.land.at[slot, half],
                self.send + 2 * chunk + group,
                self.recv + 2 * slot + group,
                device,
            )

        def keep(self, chunk, group, tile, value):
            self.stage[chunk, self.half(group), tile, :, : self.each] = value.astype(bf16)

        def add(self, chunk, group, slot, device):
            half = self.half(group)
            self.copy(chunk, group, slot, device).wait_recv()
            got = self.got.at[:, :, : self.each]
            bring = local(self.land.at[slot, half], got, self.local)
            bring.start()
            bring.wait()
            for tile in range(self.count):
                whole = self.stage[chunk, half, tile, :, : self.each].astype(f32) + got[tile].astype(f32)
                self.keep(chunk, group, tile, whole)

        def out_from_end(self, number, tile=None):
            @pl.when(at_end)
            def _():
                chunk = counted(line - 1 - number)
                slot = chunk if number < line - 2 else jnp.where(first_half, line, line + 1)
                for group in range(2):
                    half = self.half(group)
                    if tile is None:
                        self.copy(chunk, group, slot, inward).start()
                    else:
                        remote(
                            self.staged(chunk, half, tile),
                            self.land.at[slot, half, tile],
                            self.send + 2 * chunk + group,
                            self.recv + 2 * slot + group,
                            inward,
                        ).start()

        def to_mate(self, number):
            @pl.when(near_end)
            def _():
                chunk = counted(line - 1 - number)
                slot = chunk if number == 0 else jnp.where(first_half, line, line + 1)
                if self.ends is not None:
                    self.product(chunk, True)
                for group in range(2):
                    if self.ends is None:
                        self.add(chunk, group, chunk, outward)
                    self.copy(chunk, group, slot, mate).start()

        def to_end(self):
            @pl.when(near_end)
            def _():
                chunk = counted(0)
                slot = jnp.where(first_half, line + 1, line)
                if self.ends is not None:
                    self.product(chunk, False)
                for group in range(2):
                    self.add(chunk, group, chunk, mate)
                    self.copy(chunk, group, slot, outward).start()

        def own(self):
            if self.ends is not None:

                @pl.when(at_end)
                def _():
                    self.product(place, False)

                @pl.when(near_end)
                def _():
                    self.product(place, True)

            self.out = local(self.staged(place, slice(None)), r["own_" + self.name], self.local + 1)
            self.out.start()

        def sent(self):
            self.done = True
            self.out.wait()

            def one(chunk):
                for group in range(2):
                    self.copy(chunk, group, chunk, inward).wait_send()

            if self.ends is None:

                @pl.when(at_end)
                def _():
                    for number in range(line - 1):
                        one(counted(line - 1 - number))

            @pl.when(near_end)
            def _():
                for chunk in (line - 1, line - 2, 0):
                    one(counted(chunk))

        def finish(self):
            if not self.done:
                self.sent()
            far = 0 if self.ends is None else 1
            for group in range(2):

                @pl.when(place > far)
                def _():
                    self.copy(place, group, line, left).wait_recv()

                @pl.when(place < line - 1 - far)
                def _():
                    self.copy(place, group, line + 1, right).wait_recv()

    class ColumnFlow(Flow):
        def __init__(self, name, own, pair):
            super().__init__(name, by_col=True)
            self.own_columns, self.pair_columns = own, pair

        def products(self, tile):
            for group in range(2):
                full = contract(r["hid_own"][...], r[self.own_columns[group]][tile], 0, 0)
                full = full + contract(r["hid_pair"][...], r[self.pair_columns[group]][tile], 0, 0)
                for chunk in range(line):
                    self.keep(chunk, group, tile, full[chunk * self.depth : (chunk + 1) * self.depth])

    class RowFlow(Flow):
        def __init__(self, name, own, pair, ends):
            super().__init__(name, ends=ends)
            self.own_rows, self.pair_rows = own, pair

        def product(self, chunk, with_end):
            copies = self.bring_end(chunk) if with_end else []
            for copy in copies:
                copy.start()
            for group in range(2):
                full = contract(self.own_rows[chunk], r["cotq"][0, group], 0, 0)
                full = full + contract(self.pair_rows[chunk], r["cotp"][group], 0, 0)
                for copy in copies:
                    copy.wait()
                copies = []
                if with_end:
                    for pair in range(2):
                        rows_in = r["weight"][1, pair, :rows, : self.count * self.depth]
                        cot_in = r["weight"][0, pair, group * rows : (group + 1) * rows, :q]
                        full = full + contract(rows_in, cot_in, 0, 0)
                for tile in range(self.count):
                    self.keep(chunk, group, tile, full[tile * self.depth : (tile + 1) * self.depth])

        def bring_end(self, chunk):
            copies = []
            self.ends.onward(chunk).wait_recv()
            for pair in range(2):
                rows_in = self.ends.land.at[chunk, pair]
                copies.append(local(rows_in, r["weight"].at[1, pair, :rows, : rows_in.shape[1]], stream_base + pair))
                for part in range(2):
                    at = r["weight"].at[0, pair, part * rows : (part + 1) * rows, :q]
                    copies.append(local(r["end_cot"].at[pair, part], at, stream_base + 2 + 2 * pair + part))
            return copies

    down = RowFlow("down", r["act_own"], r["act_pair"], end_act)
    up = ColumnFlow("up", ("db_mine", "db_theirs"), ("db_mine_pair", "db_theirs_pair"))
    dense = RowFlow("dense", r["att_own"], r["att_pair"], end_att)
    qkv = ColumnFlow("qkv", ("dp_mine", "dp_theirs"), ("dp_mine_pair", "dp_theirs_pair"))
    swaps["qkv"].wait()

    def qkv_work(step, slot):
        part = contract(r["hid"][0], r["weight"][slot, 0, :, :PAIR_QKV], 1, 0)
        part = part + contract(r["hid"][1], r["weight"][slot, 1, :, :PAIR_QKV], 1, 0)
        r["total"][step, :, :PAIR_QKV] = part + r["qkv_b"][step]

    stream(pairs, column_tiles("qkv", PAIR_QKV), qkv_work)
    swaps["dense"].wait()

    def dense_work(step, slot):
        d_mixed = over_weight_rows(slot, z.features, lambda h, p: r["cotq"][h, p]).astype(bf16)
        for pair in range(pairs):
            r["mixed"][pair] = d_mixed[:, pair * PAIR : (pair + 1) * PAIR]

    stream(1, row_tiles("dense", z.features), dense_work)
    loop(0, 1, pass_on(act_side, act_on))
    loop(0, 1, waits(act_on))
    end_act.start(True, 0, 1)
    cot_side_onward.wait()
    send_end_cot(1, other_row)

    att_side_send, att_side_recv = take("send", half_line), take("recv", half_line)
    att_col_send, att_col_recv = take("send", half_line), take("recv", half_line)
    att_on_send, att_on_recv = take("send", half_line), take("recv", half_line)

    def att_side(k):
        slot = col * half_line + k
        return remote(
            r["att_part"].at[2 * k + other_side], r["att_pair"].at[slot], att_side_send + k, att_side_recv + k, to_side
        )

    def att_col(k):
        slot = col * half_line + k
        return remote(r["att_own"].at[slot], r["att_own"].at[slot], att_col_send + k, att_col_recv + k, to_col)

    def att_on(k):
        slot = col * half_line + k
        return remote(r["att_pair"].at[slot], r["att_pair"].at[slot], att_on_send + k, att_on_recv + k, to_col)

    def head_pair(pair):
        attended, d_projected = attention_pair(
            r["total"][pair, :, :PAIR_QKV], r["mixed"][pair], r["tables"], r["seg_col"][...], r["seg_row"][...]
        )
        r["dp_mine"][pair] = d_projected
        dp_side(pair).start()
        dp_col(pair).start()
        sums = jnp.sum(d_projected.astype(f32), axis=0, keepdims=True)
        r["sums"][:, pl.ds(pl.multiple_of(2 * q + pair * PAIR_QKV, 128), PAIR_QKV)] = sums
        r["att"][:, pl.ds(pl.multiple_of(pair * PAIR, PAIR), PAIR)] = attended
        each = PAIR // z.dense_chunk
        for part in range(each):
            chunk = pair * each + part
            k = chunk // 2
            piece = attended[:, part * z.dense_chunk : (part + 1) * z.dense_chunk]

            @pl.when(lax.rem(chunk, 2) == side)
            def _():
                r["att_own"][col * half_line + k] = piece
                att_col(k).start()

            @pl.when(lax.rem(chunk, 2) == other_side)
            def _():
                r["att_part"][chunk] = piece
                att_side(k).start()

    def near_end_cot():
        @pl.when(near_end)
        def _():
            for pair in range(2):
                for part in range(2):
                    end_cot(pair, part, outward).wait_recv()

    def pair_and_more(pair):
        head_pair(pair)

        @pl.when(pair == 0)
        def _():
            loop(1, half_line, pass_on(act_side, act_on))
            loop(1, half_line, waits(act_on))
            end_act.start(True, 1, line - 1)
            end_act.hand_over(0)

        @pl.when(pair == 1)
        def _():
            near_end_cot()
            down.to_mate(0)
            end_act.hand_over(1, 2)

    loop(0, pairs, pair_and_more)
    down.to_mate(1)

    def scatter(name, total, earlier=None):
        across = Message(r["part_send"], r[name + "_got"], to_col)
        over = Message(r["part_row"], r[name + "_row"], to_row)

        def free(message):
            message.copy().wait_send()
            pending.remove(message)

        def first():
            if earlier is not None:
                free(earlier[0])
            for p in range(2):
                r["part_send"][p] = total[2 + p].astype(bf16)
            across.start()

        def second():
            across.wait()
            if earlier is not None:
                free(earlier[1])
            for p in range(2):
                total[p] = total[p] + r[name + "_got"][p].astype(f32)
            r["part_row"][...] = total[other_row].astype(bf16)
            over.start()
            return total[row]

        def third(part):
            over.wait()
            return part + r[name + "_row"][...].astype(f32)

        return first, second, third, (across, over)

    total = r["total"]

    def down_out(step, slot):
        for h in range(2):
            for p in range(2):
                part = contract(r["act"][step], r["weight"][slot, h, p * q : p * q + z.down_chunk, :], 1, 0)

                @pl.when(step == 0)
                def _():
                    total[2 * h + p] = part

                @pl.when(step > 0)
                def _():
                    total[2 * h + p] = total[2 * h + p] + part

    def dense_out(step, slot):
        for h in range(2):
            for p in range(2):
                part = contract(r["att"][...], r["weight"][slot, h, p * q : p * q + z.features, :], 1, 0)
                total[2 * h + p] = total[2 * h + p] + part

    def up_back(step, slot):
        for h in range(2):
            for p in range(2):
                part = contract(r["db_mine"][step], r["weight"][slot, h, p * q : (p + 1) * q, : z.down_chunk], 1, 1)

                @pl.when(step == 0)
                def _():
                    total[2 * h + p] = part

                @pl.when(step > 0)
                def _():
                    total[2 * h + p] = total[2 * h + p] + part

    def qkv_back(step, slot):
        for h in range(2):
            for p in range(2):
                part = contract(r["dp_mine"][step], r["weight"][slot, h, p * q : (p + 1) * q, :PAIR_QKV], 1, 1)
                total[2 * h + p] = total[2 * h + p] + part

    def take_d_before(tile):
        loop(tile, tile + 1, pass_on(db_side, db_on))
        loop(tile, tile + 1, waits(db_col, db_on))
        up.products(tile)
        up.out_from_end(0, tile)
        up.out_from_end(1, tile)

    hid_side.wait()
    take_d_before(0)
    stream(tiles, column_tiles("up", z.down_chunk), up_back)
    take_d_before(1)
    stream(pairs, column_tiles("qkv", PAIR_QKV), qkv_back)
    dh_first, dh_second, dh_third, dh_messages = scatter("dh", total)
    dh_first()
    for tile in range(2, tiles):
        take_d_before(tile)
    up.out_from_end(2)
    down.to_end()
    r["grad_inputs"][...] = dh_second()
    up.to_mate(0)
    up.to_mate(1)
    stream(tiles, row_tiles("down", z.down_chunk), down_out)
    stream(1, row_tiles("dense", z.features), dense_out)
    out_first, out_second, out_third, out_messages = scatter("out", total, dh_messages)
    out_first()

    d_hidden = dh_third(r["grad_inputs"][...])
    r["grad_inputs"][...] = d_hidden
    own_in = r["inq"].at[0, row]
    gain = r["gainq"][0, row, 0:1, :]
    sums_row = Message(r["sum_send"].at[0], r["sum_got"].at[0], to_row)
    sums_col = Message(r["sum_send"].at[1], r["sum_got"].at[1], to_col)
    normed = (own_in[...].astype(f32) - r["stat"][0]) * r["stat"][1]
    d_normed = d_hidden * gain
    lane = lax.broadcasted_iota(jnp.int32, (rows, 128), 1)
    one = jnp.sum(d_normed, axis=1, keepdims=True)
    two = jnp.sum(d_normed * normed, axis=1, keepdims=True)
    packed = jnp.where(lane == 0, one, jnp.where(lane == 1, two, 0.0))
    r["sum_send"][0] = turned(packed)[:8]
    sums_row.start()
    r["sums"][:, 0:q] = jnp.sum(d_hidden * normed, axis=0, keepdims=True)
    r["sums"][:, q : 2 * q] = jnp.sum(d_hidden, axis=0, keepdims=True)
    r["sums"][:, 2 * q + z.qkv + z.hidden :] = jnp.sum(r["cotq"][0, row].astype(f32), axis=0, keepdims=True)
    small_side = Message(r["sums"], r["sums_got"].at[0], to_side)
    small_side.start()

    small_send, small_recv = take("send", 2), take("recv", 2)

    def small(way, device):
        return remote(r["sums_send"].at[way], r["sums_got"].at[1 + way], small_send + way, small_recv + way, device)

    def hop(number):
        for way, rank, device, last in ((0, place, right, has_right), (1, line - 1 - place, left, has_left)):

            @pl.when((rank == number) & last)
            def _():
                @pl.when(rank == 0)
                def _():
                    r["sums_send"][way] = r["sums"][...]

                @pl.when(rank > 0)
                def _():
                    small(way, device).wait_recv()
                    r["sums_send"][way] = r["sums"][...] + r["sums_got"][1 + way]

                small(way, device).start()

    branch = out_second()
    total[0] = branch
    down.own()
    down.sent()
    for pair in range(pairs):
        loop(pair, pair + 1, pass_on(dp_side, dp_on))
        loop(pair, pair + 1, waits(dp_col, dp_on))
        qkv.products(pair)
    loop(0, half_line, pass_on(att_side, att_on))
    loop(0, half_line, waits(att_col, att_on))
    end_att.start(False, 0, line - 1)
    end_att.start(True, 0, line - 1)
    small_side.wait()
    small_side.copy().wait_send()
    pending.remove(small_side)
    r["sums"][...] = r["sums"][...] + r["sums_got"][0]
    hop(0)
    for number in range(line - 1):
        qkv.out_from_end(number)
    up.to_end()
    hop(1)
    sums_row.wait()
    r["sum_send"][1] = r["sum_send"][0] + r["sum_got"][0]
    sums_col.start()
    up.own()
    end_att.hand_over(0, 1, 2)
    dense.to_mate(0)
    dense.to_mate(1)
    hop(2)
    qkv.to_mate(0)
    dense.to_end()
    qkv.to_mate(1)
    qkv.to_end()
    qkv.own()

    dense.own()
    branch = out_third(total[0])
    bias = as_row(r["out_bias"][...])
    valid = (r["seg_col"][...] < z.seqs).astype(f32)
    r["outputs"][...] = (r["inq"][0, row].astype(f32) + valid * (branch + bias)).astype(bf16)
    sums_col.wait()
    both = r["sum_send"][1] + r["sum_got"][1]
    spread = turned(jnp.concatenate([both, jnp.zeros((120, rows), f32)], axis=0))
    part_one, part_two = spread[:, 0:1] / z.width, spread[:, 1:2] / z.width
    normed = (own_in[...].astype(f32) - r["stat"][0]) * r["stat"][1]
    d_normed = r["grad_inputs"][...] * gain
    r["grad_inputs"][...] = cot[...].astype(f32) + r["stat"][1] * (d_normed - part_one - normed * part_two)

    r["small"][...] = r["sums"][...]

    @pl.when(place == line - 1)
    def _():
        small(0, left).wait_recv()

    @pl.when(place == 0)
    def _():
        small(1, right).wait_recv()

    @pl.when(has_left)
    def _():
        r["small"][...] = r["small"][...] + r["sums_got"][1]

    @pl.when(has_right)
    def _():
        r["small"][...] = r["small"][...] + r["sums_got"][2]

    @pl.when(has_right)
    def _():
        small(0, right).wait_send()

    @pl.when(has_left)
    def _():
        small(1, left).wait_send()

    for flow in (down, up, dense, qkv):
        flow.finish()
    end_act.finish()
    end_att.finish()

    @pl.when(at_end)
    def _():
        for pair in range(2):
            for part in range(2):
                end_cot(pair, part, inward).wait_send()

    for message in pending:
        message.copy().wait_send()

    def sent(*copies):
        def work(k):
            for copy in copies:
                copy(k).wait_send()

        return work

    loop(0, half_line, sent(act_side, act_col, act_on, att_side, att_col, att_on))
    loop(0, tiles, sent(db_side, db_col, db_on))
    loop(0, pairs, sent(dp_side, dp_col, dp_on))
    assert marks["send"] <= SENDS * line and marks["recv"] <= SENDS * line and marks["local"] <= LOCALS


def on_device(
    dp_size,
    inputs,
    norm_gain,
    norm_shift,
    qkv_weight,
    qkv_bias,
    up_weight,
    up_bias,
    dense_weight,
    down_weight,
    out_bias,
    cotangent,
    seq_lengths,
    seq_owner,
):
    z = Sizes(dp_size, inputs, qkv_weight, up_weight, dense_weight, down_weight, seq_lengths)
    if not fits(z):
        return on_device_plain(
            dp_size,
            inputs,
            norm_gain,
            norm_shift,
            qkv_weight,
            qkv_bias,
            up_weight,
            up_bias,
            dense_weight,
            down_weight,
            out_bias,
            cotangent,
            seq_lengths,
            seq_owner,
        )
    rows, q, line = z.rows, z.quarter, z.line
    lane_rate = np.zeros((1, HEAD_DIM), np.float32)
    lane_rate[0, :ROT] = rope_base ** (-2.0 * (np.arange(ROT) % HALF_ROT) / ROT)
    operands = dict(
        inputs=(inputs, pl.ANY),
        cot=(cotangent, pltpu.VMEM),
        norm_gain=(norm_gain, pltpu.VMEM),
        norm_shift=(norm_shift, pltpu.VMEM),
        qkv_bias=(qkv_bias, pltpu.VMEM),
        up_bias=(up_bias, pltpu.VMEM),
        out_bias=(out_bias, pltpu.VMEM),
        frequency=(jnp.asarray(lane_rate), pltpu.VMEM),
        seq_lengths=(seq_lengths, pltpu.SMEM),
        seq_owner=(seq_owner, pltpu.SMEM),
        up_w=(up_weight, pl.ANY),
        down_w=(down_weight, pl.ANY),
        qkv_w=(qkv_weight, pl.ANY),
        dense_w=(dense_weight, pl.ANY),
    )
    results = dict(
        outputs=((rows, q), bf16, pltpu.VMEM),
        grad_inputs=((rows, q), f32, pltpu.VMEM),
        small=((1, 3 * q + z.qkv + z.hidden), f32, pltpu.VMEM),
        up_o=((z.half, z.hidden), bf16, pl.ANY),
        down_o=((z.hidden, z.half), bf16, pl.ANY),
        qkv_o=((z.half, z.qkv), bf16, pl.ANY),
        dense_o=((z.features, z.half), bf16, pl.ANY),
        end_cot=((2, 2, rows, q), bf16, pl.ANY),
        end_act=((line, 2, rows, z.down_chunk), bf16, pl.ANY),
        end_att=((line, 2, rows, z.dense_chunk), bf16, pl.ANY),
    )
    for name, shape in flows_of(z).items():
        results["land_" + name] = ((line + 2, 2) + shape, bf16, pl.ANY)
        results["own_" + name] = ((2,) + shape, bf16, pl.ANY)
    scratch = scratch_of(z)
    names = list(operands) + list(results) + list(scratch) + ["send_sem", "recv_sem", "local_sem"]
    found = pl.pallas_call(
        partial(layer_kernel, z, names),
        in_specs=[pl.BlockSpec(memory_space=space) for value, space in operands.values()],
        out_specs=[pl.BlockSpec(memory_space=space) for shape, kind, space in results.values()],
        out_shape=[jax.ShapeDtypeStruct(shape, kind) for shape, kind, space in results.values()],
        scratch_shapes=[pltpu.VMEM(shape, kind) for shape, kind in scratch.values()]
        + [pltpu.SemaphoreType.DMA((SENDS * line,)), pltpu.SemaphoreType.DMA((SENDS * line,)), pltpu.SemaphoreType.DMA((LOCALS,))],
        compiler_params=pltpu.CompilerParams(
            collective_id=0, has_side_effects=True, vmem_limit_bytes=VMEM_LIMIT
        ),
        name="layer",
    )(*[value for value, space in operands.values()])
    got = dict(zip(results, found))
    big, small = finish(z, got)
    return (
        big["outputs"],
        big["grad_inputs"],
        small["gain"],
        small["shift"],
        big["qkv"],
        small["qkv"],
        big["up"],
        small["up"],
        big["dense"],
        big["down"],
        small["out"],
    )


def finish(z, got):
    line, steps = z.line, 8
    flows = flows_of(z)
    names = list(flows)
    pieces = dict(gain=z.quarter, shift=z.quarter, qkv=z.qkv, up=z.hidden, out=z.quarter)

    def kernel(*refs):
        place = lax.axis_index("dp") // 2
        fed = refs[: 3 * len(names) + 3]
        made = refs[3 * len(names) + 3 :]
        for index in range(len(names)):
            own, from_left, from_right = (ref[...].astype(f32) for ref in fed[3 * index : 3 * index + 3])
            far = 1 if names[index] in ("down", "dense") else 0
            total = own + jnp.where(place > far, from_left, 0.0) + jnp.where(place < line - 1 - far, from_right, 0.0)
            made[index][...] = total.reshape(made[index].shape)
        outputs, grad_inputs, small = fed[3 * len(names) :]
        made[len(names)][...] = outputs[...]
        made[len(names) + 1][...] = grad_inputs[...]

        @pl.when(pl.program_id(0) == 0)
        def _():
            start = 0
            for index, width in enumerate(pieces.values()):
                made[len(names) + 2 + index][...] = small[:, start : start + width].reshape(width)
                start += width

    in_specs, out_specs, out_shape, fed = [], [], [], []
    for name in names:
        count, depth, each = flows[name]
        group = count // (steps // 2) or 1

        def tile_index(step, name=name):
            half, tile = step // (steps // 2), lax.rem(step, steps // 2)
            return half, tile if flows[name][0] >= steps // 2 else 0

        block = (None, group, depth, each)
        land_block = (None, None, group, depth, each)
        in_specs.append(pl.BlockSpec(block, lambda i, f=tile_index: (*f(i), 0, 0)))
        in_specs.append(pl.BlockSpec(land_block, lambda i, f=tile_index: (line, *f(i), 0, 0)))
        in_specs.append(pl.BlockSpec(land_block, lambda i, f=tile_index: (line + 1, *f(i), 0, 0)))
        fed += [got["own_" + name], got["land_" + name], got["land_" + name]]
        if name == "down":
            out_shape.append(jax.ShapeDtypeStruct((count * depth, 2 * each), f32))
            out_specs.append(pl.BlockSpec((group * depth, each), lambda i, f=tile_index: f(i)[::-1]))
        else:
            assert group == 1
            out_shape.append(jax.ShapeDtypeStruct((depth, 2 * count * each), f32))
            out_specs.append(
                pl.BlockSpec((depth, each), lambda i, f=tile_index, count=count: (0, f(i)[0] * count + f(i)[1]))
            )
    for name in ("outputs", "grad_inputs"):
        rows, columns = got[name].shape
        spec = pl.BlockSpec((rows // steps, columns), lambda i: (i, 0))
        in_specs.append(spec)
        out_specs.append(spec)
        out_shape.append(jax.ShapeDtypeStruct((rows, columns), got[name].dtype))
        fed.append(got[name])
    in_specs.append(pl.BlockSpec(memory_space=pltpu.VMEM))
    fed.append(got["small"])
    for width in pieces.values():
        out_specs.append(pl.BlockSpec(memory_space=pltpu.VMEM))
        out_shape.append(jax.ShapeDtypeStruct((width,), f32))
    made = pl.pallas_call(
        kernel, grid=(steps,), in_specs=in_specs, out_specs=out_specs, out_shape=out_shape, name="finish"
    )(*fed)
    big = dict(zip(names + ["outputs", "grad_inputs"], made))
    return big, dict(zip(pieces, made[len(names) + 2 :]))


def attention_kernel(proj_ref, mixed_ref, tables_ref, seg_col_ref, seg_row_ref, attended_ref, grad_ref):
    attended_ref[...], grad_ref[...] = attention_pair(
        proj_ref[...], mixed_ref[...], tables_ref, seg_col_ref[...], seg_row_ref[...]
    )


def attention(projected, mixed, tables, segment):
    rows, width = projected.shape
    pairs = width // PAIR_QKV
    return pl.pallas_call(
        attention_kernel,
        grid=(pairs,),
        in_specs=[
            pl.BlockSpec((rows, PAIR_QKV), lambda i: (0, i)),
            pl.BlockSpec((rows, PAIR), lambda i: (0, i)),
            pl.BlockSpec((3, rows, HEAD_DIM), lambda i: (0, 0, 0)),
            pl.BlockSpec((rows, 1), lambda i: (0, 0)),
            pl.BlockSpec((1, rows), lambda i: (0, 0)),
        ],
        out_specs=[
            pl.BlockSpec((rows, PAIR), lambda i: (0, i)),
            pl.BlockSpec((rows, PAIR_QKV), lambda i: (0, i)),
        ],
        out_shape=[
            jax.ShapeDtypeStruct((rows, pairs * PAIR), bf16),
            jax.ShapeDtypeStruct((rows, width), bf16),
        ],
        compiler_params=pltpu.CompilerParams(vmem_limit_bytes=48 * 1024 * 1024),
        cost_estimate=pl.CostEstimate(
            flops=14 * 2 * pairs * rows * rows * HEAD_DIM * 2,
            bytes_accessed=rows * width * 7,
            transcendentals=2 * pairs * rows * rows,
        ),
        name="attention",
    )(projected, mixed, tables, segment[:, None], segment[None, :])


def dot_plain(left, right):
    return jnp.dot(left, right, preferred_element_type=f32)


def contract_rows(left, right):
    return lax.dot_general(left, right, (((0,), (0,)), ((), ())), preferred_element_type=f32)


def contract_cols(left, right):
    return lax.dot_general(left, right, (((1,), (1,)), ((), ())), preferred_element_type=f32)


def on_device_plain(
    dp_size,
    inputs,
    norm_gain,
    norm_shift,
    qkv_weight,
    qkv_bias,
    up_weight,
    up_bias,
    dense_weight,
    down_weight,
    out_bias,
    cotangent,
    seq_lengths,
    seq_owner,
):
    row_count = inputs.shape[0]
    line = dp_size // 2
    device = lax.axis_index("dp")
    place = device // 2
    side = device % 2
    row = lax.axis_index("row")
    col = lax.axis_index("col")

    over_row = partial(lax.ppermute, axis_name="row", perm=[(0, 1), (1, 0)])
    over_col = partial(lax.ppermute, axis_name="col", perm=[(0, 1), (1, 0)])
    over_side = partial(lax.ppermute, axis_name="dp", perm=[(e, e ^ 1) for e in range(dp_size)])

    def in_order(index, mine, other, axis):
        first = jnp.where(index == 0, mine, other)
        second = jnp.where(index == 0, other, mine)
        return jnp.concatenate([first, second], axis=axis)

    def half_at(array, index, axis):
        width = array.shape[axis] // 2
        return lax.dynamic_slice_in_dim(array, index * width, width, axis)

    segment, position, is_valid = layout(seq_lengths, seq_owner, device, row_count)
    tables = rotation_tables(position)

    gains = jnp.stack([norm_gain, norm_shift])
    grad_branch = cotangent * is_valid.astype(bf16)[:, None]
    inputs_half = in_order(row, inputs, over_row(inputs), 1)
    gains_half = in_order(row, gains, over_row(gains), 1)
    inputs_other = over_col(inputs_half)
    gains_other = over_col(gains_half)
    branch_half = in_order(row, grad_branch, over_row(grad_branch), 1)
    branch_other = over_col(branch_half)

    up_mine, up_other = half_at(up_weight, col, 1), over_col(half_at(up_weight, 1 - col, 1))
    down_mine, down_other = half_at(down_weight, col, 0), over_col(half_at(down_weight, 1 - col, 0))
    qkv_mine, qkv_other = half_at(qkv_weight, col, 1), over_col(half_at(qkv_weight, 1 - col, 1))
    dense_mine, dense_other = half_at(dense_weight, col, 0), over_col(half_at(dense_weight, 1 - col, 0))

    width = 4 * inputs.shape[1]
    source, source_other = inputs_half.astype(f32), inputs_other.astype(f32)
    average = (jnp.sum(source, axis=1) + jnp.sum(source_other, axis=1)) / width
    square = (jnp.sum(source * source, axis=1) + jnp.sum(source_other * source_other, axis=1)) / width
    scale_inv = lax.rsqrt(square - average * average + epsilon)[:, None]

    def hidden_of(rows_in, gain_pair):
        normed = (rows_in - average[:, None]) * scale_inv
        pair = gain_pair.astype(f32)
        return (normed * pair[0] + pair[1]).astype(bf16)

    hidden, hidden_other = hidden_of(source, gains_half), hidden_of(source_other, gains_other)

    before = dot_plain(hidden, up_mine) + dot_plain(hidden_other, up_other) + up_bias.astype(f32)
    activated = jax.nn.gelu(before, approximate=True).astype(bf16)
    d_activated = contract_cols(branch_half, down_mine) + contract_cols(branch_other, down_other)
    unused_value, gelu_back = jax.vjp(partial(jax.nn.gelu, approximate=True), before)
    d_before = gelu_back(d_activated)[0].astype(bf16)

    projected = dot_plain(hidden, qkv_mine) + dot_plain(hidden_other, qkv_other) + qkv_bias.astype(f32)
    d_mixed = (contract_cols(branch_half, dense_mine) + contract_cols(branch_other, dense_other)).astype(bf16)
    attended, d_projected = attention(projected, d_mixed, tables, segment)

    def chunks_of(array, index):
        rows, columns = array.shape
        grouped = array.reshape(rows, columns // (2 * chunk), 2, chunk)
        return lax.dynamic_index_in_dim(grouped, index, 2, keepdims=False).reshape(rows, columns // 2)

    branch_pair = over_side(branch_half)

    def feature_sums(array):
        kept = chunks_of(array, side)
        got = over_side(chunks_of(array, 1 - side))
        own = in_order(col, kept, over_col(kept), 1)
        pair = in_order(col, got, over_col(got), 1)
        return (contract_rows(own, branch_half) + contract_rows(pair, branch_pair)).astype(bf16)

    def along_line(sums):
        depth = sums.shape[0] // line
        parts = sums.reshape(line, depth, sums.shape[1])

        def part(index):
            return lax.dynamic_index_in_dim(parts, jnp.clip(index, 0, line - 1), 0, keepdims=False).astype(f32)

        rightward, leftward = None, None
        for step in range(line - 1):
            right_part = part(line - 1 - step + place)
            left_part = part(place - (line - 1) + step)
            if step:
                right_part = right_part + rightward.astype(f32)
                left_part = left_part + leftward.astype(f32)
            to_right = [(2 * z + x, 2 * z + 2 + x) for z in range(min(step + 1, line - 1)) for x in range(2)]
            to_left = [(dp_size - 1 - p, dp_size - 1 - q) for p, q in to_right]
            rightward = lax.ppermute(right_part.astype(bf16), "dp", to_right)
            leftward = lax.ppermute(left_part.astype(bf16), "dp", to_left)
        return part(place) + rightward.astype(f32) + leftward.astype(f32)

    chunk = down_weight.shape[0] // dp_size
    grad_down = along_line(feature_sums(activated))

    chunk = up_weight.shape[0] // dp_size
    hidden_own = chunks_of(hidden, side)
    hidden_pair = over_side(chunks_of(hidden, 1 - side))

    def hidden_sums(array):
        pair = over_side(array)
        mine = (contract_rows(hidden_own, array) + contract_rows(hidden_pair, pair)).astype(bf16)
        theirs = (contract_rows(hidden_own, over_col(array)) + contract_rows(hidden_pair, over_col(pair))).astype(bf16)
        return in_order(col, along_line(mine), along_line(theirs), 1)

    grad_up = hidden_sums(d_before)
    chunk = dense_weight.shape[0] // dp_size
    grad_dense = along_line(feature_sums(attended))
    grad_qkv = hidden_sums(d_projected)

    def scatter(mine, other):
        half = mine + over_col(other.astype(bf16)).astype(f32)
        return half_at(half, row, 1) + over_row(half_at(half, 1 - row, 1).astype(bf16)).astype(f32)

    branch = scatter(
        dot_plain(attended, dense_mine) + dot_plain(activated, down_mine),
        dot_plain(attended, dense_other) + dot_plain(activated, down_other),
    )
    valid_col = is_valid.astype(f32)[:, None]
    outputs = (inputs.astype(f32) + valid_col * (branch + out_bias.astype(f32))).astype(bf16)

    d_hidden = scatter(
        contract_cols(d_projected, qkv_mine) + contract_cols(d_before, up_mine),
        contract_cols(d_projected, qkv_other) + contract_cols(d_before, up_other),
    )
    normed = (inputs.astype(f32) - average[:, None]) * scale_inv
    d_normed = d_hidden * norm_gain.astype(f32)
    row_sums = jnp.stack([jnp.sum(d_normed, axis=1), jnp.sum(d_normed * normed, axis=1)])
    row_sums = row_sums + over_row(row_sums)
    row_sums = row_sums + over_col(row_sums)
    grad_inputs = cotangent.astype(f32) + scale_inv * (
        d_normed - row_sums[0][:, None] / width - normed * row_sums[1][:, None] / width
    )

    small = [
        jnp.sum(d_hidden * normed, axis=0),
        jnp.sum(d_hidden, axis=0),
        jnp.sum(d_projected.astype(f32), axis=0),
        jnp.sum(d_before.astype(f32), axis=0),
        jnp.sum(grad_branch.astype(f32), axis=0),
    ]
    together = jnp.concatenate(small)
    bit = 1
    while bit < dp_size:
        together = together + lax.ppermute(together, "dp", [(e, e ^ bit) for e in range(dp_size)])
        bit *= 2
    ends = []
    for piece in small:
        ends.append((ends[-1] if ends else 0) + piece.shape[0])
    grad_gain, grad_shift, grad_qkv_bias, grad_up_bias, grad_out_bias = jnp.split(together, ends[:-1])
    return (
        outputs,
        grad_inputs,
        grad_gain,
        grad_shift,
        grad_qkv,
        grad_qkv_bias,
        grad_up,
        grad_up_bias,
        grad_dense,
        grad_down,
        grad_out_bias,
    )


def solution(mesh):
    in_specs = (
        P("dp", ("col", "row")),
        P(("col", "row")),
        P(("col", "row")),
        P("col", "row"),
        P(("row", "col")),
        P("col", "row"),
        P(("row", "col")),
        P("row", "col"),
        P("row", "col"),
        P(("col", "row")),
        P("dp", ("col", "row")),
        P(),
        P(),
    )
    out_specs = (
        P("dp", ("col", "row")),
        P("dp", ("col", "row")),
        P(("col", "row")),
        P(("col", "row")),
        P(("col", "dp"), "row"),
        P(("row", "col")),
        P(("col", "dp"), "row"),
        P(("row", "col")),
        P(("row", "dp"), "col"),
        P(("row", "dp"), "col"),
        P(("col", "row")),
    )
    return jax.shard_map(
        partial(on_device, mesh.shape["dp"]), mesh=mesh, in_specs=in_specs, out_specs=out_specs, check_vma=False
    )
```

```python
from functools import partial
import math

import jax
import jax.numpy as jnp
import numpy as np
from jax import lax
from jax.experimental import pallas as pl
from jax.experimental.pallas import tpu as pltpu
from jax.sharding import PartitionSpec as P

HEAD_DIM = 64
ROT = 32
HALF_ROT = ROT // 2
PAIR = 2 * HEAD_DIM
PAIR_QKV = 3 * PAIR

epsilon = 1e-05
masked_score = -1e30
rope_base = 10000.0
VMEM_LIMIT = 67_000_000
SCRATCH_LIMIT = 58 * 1024 * 1024
SENDS = 48
LOCALS = 20
score_scale = HEAD_DIM ** (-0.5)
bf16 = jnp.bfloat16
f32 = jnp.float32


def layout(seq_lengths, seq_owner, device, row_count):
    owned = seq_owner == device
    lengths_owned = jnp.where(owned, seq_lengths, 0)
    seq_ends = jnp.cumsum(lengths_owned, dtype=jnp.int32)
    seq_starts = seq_ends - lengths_owned
    slot_index = jnp.arange(row_count, dtype=jnp.int32)
    segment = jnp.sum((seq_ends[None, :] <= slot_index[:, None]).astype(jnp.int32), axis=1)
    picked = jnp.arange(seq_lengths.shape[0], dtype=jnp.int32)[None, :] == segment[:, None]
    seq_begin = jnp.sum(jnp.where(picked, seq_starts[None, :], 0), axis=1)
    position = slot_index - seq_begin
    is_valid = slot_index < seq_ends[-1]
    return (segment, position, is_valid)


def rotation_tables(position):
    index_range = jnp.arange(HALF_ROT, dtype=f32)
    frequency = rope_base ** (-2.0 * index_range / ROT)
    phase = position.astype(f32)[:, None] * frequency[None, :]
    cosines, sines = jnp.cos(phase), jnp.sin(phase)
    rows = position.shape[0]
    ones = jnp.ones((rows, HEAD_DIM - ROT), f32)
    none = jnp.zeros((rows, HALF_ROT), f32)
    rest = jnp.zeros((rows, HEAD_DIM - ROT), f32)
    same = jnp.concatenate([cosines, cosines, ones], axis=1)
    from_right = jnp.concatenate([sines, none, rest], axis=1)
    from_left = jnp.concatenate([none, sines, rest], axis=1)
    return jnp.stack([same, from_right, from_left])


def turned(array):
    return jnp.swapaxes(array, 0, 1)


def contract(left, right, left_dim, right_dim):
    dims = (((left_dim,), (right_dim,)), ((), ()))
    return lax.dot_general(left, right, dims, preferred_element_type=f32)


gelu_rate = math.sqrt(2.0 / math.pi)
gelu_cube = 0.044715


def gelu(x):
    return 0.5 * x * (1.0 + jnp.tanh(gelu_rate * (x + gelu_cube * x * x * x)))


def gelu_slope(x):
    square = x * x
    bent = jnp.tanh(gelu_rate * (x + gelu_cube * x * square))
    return 0.5 * (1.0 + bent) + 0.5 * x * (1.0 - bent * bent) * (gelu_rate * (1.0 + 3.0 * gelu_cube * square))


def attention_pair(proj, mixed, tables, seg_col, seg_row):
    rows = proj.shape[0]
    block = min(256, rows)
    same, from_right, from_left = tables[0], tables[1], tables[2]
    upper = lax.broadcasted_iota(jnp.int32, (1, PAIR), 1) >= HEAD_DIM
    turn_all, turn_upper, turn_lower = True, upper, jnp.logical_not(upper)

    def rotate(group, which, sign):
        ahead, behind = pltpu.roll(group, PAIR - HALF_ROT, 1), pltpu.roll(group, HALF_ROT, 1)
        spun = group * same - sign * (ahead * from_right) + sign * (behind * from_left)
        return spun if which is True else jnp.where(which, spun, group)

    groups = [
        rotate(proj[:, number * PAIR : (number + 1) * PAIR], which, 1.0)
        for number, which in enumerate((turn_all, turn_upper, turn_lower))
    ]
    low = [group.astype(bf16) for group in groups]
    fields = [low[number // 2][:, (number % 2) * HEAD_DIM : (number % 2 + 1) * HEAD_DIM] for number in range(6)]
    ones = jnp.ones((rows, HEAD_DIM), bf16)
    attended_heads, grads = [], []
    for head in range(2):
        queries, keys, values = fields[3 * head : 3 * head + 3]
        queries = queries * jnp.asarray(score_scale, bf16)
        values_ones = jnp.concatenate([values, ones], axis=1)
        d_outs = mixed[:, head * HEAD_DIM : (head + 1) * HEAD_DIM].astype(f32)
        outs, d_queries, d_keys, d_values = [], [], None, None
        for first in range(0, rows, block):
            last = first + block
            q, k, v = queries[first:last], keys[:last], values[:last]
            row_index = first + lax.broadcasted_iota(jnp.int32, (block, last), 0)
            key_index = lax.broadcasted_iota(jnp.int32, (block, last), 1)
            allowed = (seg_col[first:last, :] == seg_row[:, :last]) & (key_index <= row_index)
            scores = jnp.where(allowed, contract(q, k, 1, 1), masked_score)
            weights = jnp.exp(scores - jnp.max(scores, axis=1, keepdims=True))
            weights_low = weights.astype(bf16)
            sums = contract(weights_low, values_ones[:last], 1, 0)
            inverse = 1.0 / sums[:, HEAD_DIM : HEAD_DIM + 1]
            out = sums[:, :HEAD_DIM] * inverse
            outs.append(out)
            d_out = (d_outs[first:last] * inverse).astype(bf16)
            row_dot = jnp.sum(out * d_out.astype(f32), axis=1, keepdims=True)
            d_scores = (weights * (contract(d_out, v, 1, 1) - row_dot)).astype(bf16)
            d_queries.append(contract(d_scores, k, 1, 0))
            key_part = contract(d_scores, q, 0, 0)
            value_part = contract(weights_low, d_out, 0, 0)
            if d_keys is None:
                d_keys, d_values = key_part, value_part
            else:
                d_keys = jnp.concatenate([key_part[:first] + d_keys, key_part[first:]], axis=0)
                d_values = jnp.concatenate([value_part[:first] + d_values, value_part[first:]], axis=0)
        attended_heads.append(jnp.concatenate(outs, axis=0))
        grads += [jnp.concatenate(d_queries, axis=0) * score_scale, d_keys, d_values]
    attended = jnp.concatenate(attended_heads, axis=1).astype(bf16)
    turned_back = [
        rotate(jnp.concatenate(grads[2 * number : 2 * number + 2], axis=1), which, -1.0)
        for number, which in enumerate((turn_all, turn_upper, turn_lower))
    ]
    return attended, jnp.concatenate(turned_back, axis=1).astype(bf16)


class Sizes:
    def __init__(self, dp_size, inputs, qkv_weight, up_weight, dense_weight, down_weight, seq_lengths):
        self.dp = dp_size
        self.seqs = seq_lengths.shape[0]
        self.line = dp_size // 2
        self.rows, self.quarter = inputs.shape
        self.half = up_weight.shape[0]
        self.width = 2 * self.half
        self.up_chunk = self.half // dp_size
        self.down_chunk = down_weight.shape[0] // dp_size
        self.dense_chunk = dense_weight.shape[0] // dp_size
        self.hidden = up_weight.shape[1] // 2
        self.tiles = self.hidden // self.down_chunk
        self.qkv = qkv_weight.shape[1] // 2
        self.pairs = self.qkv // PAIR_QKV
        self.features = dense_weight.shape[0] // 2


def flows_of(z):
    return dict(
        down=(z.down_chunk // z.up_chunk, z.up_chunk, z.quarter),
        up=(z.tiles, z.up_chunk, z.down_chunk),
        dense=(1, z.dense_chunk, z.quarter),
        qkv=(z.pairs, z.up_chunk, PAIR_QKV),
    )


def scratch_of(z):
    rows, q, line, tiles, pairs = z.rows, z.quarter, z.line, z.tiles, z.pairs
    up, down, dense = z.up_chunk, z.down_chunk, z.dense_chunk
    shapes = dict(
        inq=((2, 2, rows, q), bf16),
        cotq=((2, 2, rows, q), bf16),
        cotp=((2, rows, q), bf16),
        gainq=((2, 2, 16, q), f32),
        seg_col=((rows, 1), f32),
        seg_row=((1, rows), f32),
        tables=((3, rows, PAIR), f32),
        up_b=((tiles, 1, down), f32),
        qkv_b=((pairs, 1, PAIR_QKV), f32),
        sums=((1, 3 * q + z.qkv + z.hidden), f32),
        sums_got=((3, 1, 3 * q + z.qkv + z.hidden), f32),
        sums_send=((2, 1, 3 * q + z.qkv + z.hidden), f32),
        hid=((2, rows, z.half), bf16),
        hid_own=((rows, line * up), bf16),
        hid_send=((rows, line * up), bf16),
        hid_pair=((rows, line * up), bf16),
        stat=((2, rows, 1), f32),
        before=((tiles, rows, down), f32),
        act=((tiles, rows, down), bf16),
        act_own=((line, rows, down), bf16),
        act_pair=((line, rows, down), bf16),
        db_mine=((tiles, rows, down), bf16),
        db_theirs=((tiles, rows, down), bf16),
        db_mine_pair=((tiles, rows, down), bf16),
        db_theirs_pair=((tiles, rows, down), bf16),
        mixed=((pairs, rows, PAIR), bf16),
        att=((rows, z.features), bf16),
        att_part=((line, rows, dense), bf16),
        att_own=((line, rows, dense), bf16),
        att_pair=((line, rows, dense), bf16),
        dp_mine=((pairs, rows, PAIR_QKV), bf16),
        dp_theirs=((pairs, rows, PAIR_QKV), bf16),
        dp_mine_pair=((pairs, rows, PAIR_QKV), bf16),
        dp_theirs_pair=((pairs, rows, PAIR_QKV), bf16),
        weight=((2, 2, z.half, 512), bf16),
        st_down=((line, 2) + flows_of(z)["down"], bf16),
        st_up=((line, 2) + flows_of(z)["up"], bf16),
        st_dense=((line, 2) + flows_of(z)["dense"], bf16),
        got_down=(flows_of(z)["down"], bf16),
        got_dense=(flows_of(z)["dense"], bf16),
        part_send=((2, rows, q), bf16),
        part_row=((rows, q), bf16),
        out_row=((rows, q), bf16),
        dh_row=((rows, q), bf16),
        sum_send=((2, 8, rows), f32),
        sum_got=((2, 8, rows), f32),
    )
    return shapes


def fits(z):
    total = 0
    for shape, kind in scratch_of(z).values():
        total += math.prod(shape[:-1]) * -(-shape[-1] // 128) * 128 * jnp.dtype(kind).itemsize
    flows = flows_of(z)
    alike = flows["down"] == flows["up"] and flows["qkv"][:2] == flows["up"][:2] and flows["qkv"][2] <= flows["up"][2]
    square = z.rows == z.quarter and (z.tiles, z.rows, z.down_chunk) == (4, z.rows, z.quarter)
    return z.line == 4 and alike and square and total <= SCRATCH_LIMIT


def layer_kernel(z, names, *refs):
    r = dict(zip(names, refs))
    rows, q, line, tiles, pairs = z.rows, z.quarter, z.line, z.tiles, z.pairs
    half_line = line // 2
    r["total"] = r["before"]
    r["dh_got"], r["out_got"] = r["inq"].at[1], r["cotq"].at[1]
    r["got_up"] = r["got_qkv"] = r["got_down"]
    r["st_qkv"] = r["st_down"]
    dp = lax.axis_index("dp")
    row = lax.axis_index("row")
    col = lax.axis_index("col")
    place, side = dp // 2, lax.rem(dp, 2)
    other_row, other_col, other_side = 1 - row, 1 - col, 1 - side
    to_row = {"row": other_row}
    to_col = {"col": other_col}
    to_side = {"dp": dp + 1 - 2 * side}
    MESH = pl.DeviceIdType.MESH

    marks = dict(send=0, recv=0, local=0)

    def take(kind, count):
        first = marks[kind]
        marks[kind] += count
        return first

    def remote(src, dst, send, recv, device):
        return pltpu.make_async_remote_copy(
            src_ref=src,
            dst_ref=dst,
            send_sem=r["send_sem"].at[send],
            recv_sem=r["recv_sem"].at[recv],
            device_id=device,
            device_id_type=MESH,
        )

    pending = []

    class Message:
        def __init__(self, src, dst, device, got=None):
            index = (take("send", 1), take("recv", 1))
            self.copy = lambda: remote(src, dst, *index, device)
            self.got = lambda: remote(src if got is None else got, dst if got is None else got, *index, device)

        def start(self):
            self.copy().start()
            pending.append(self)

        def wait(self):
            self.got().wait_recv()

    right, left = {"dp": dp + 2}, {"dp": dp - 2}
    has_right, has_left = place < line - 1, place > 0
    at_end, near_end = (place == 0) | (place == line - 1), (place == 1) | (place == line - 2)
    inward, outward = {"dp": dp + 2 - 4 * (place > 0)}, {"dp": dp + 2 - 4 * (place == 1)}
    mate = {"dp": dp - 2 + 4 * (place == 1)}
    first_half = place < line // 2

    def counted(chunk):
        return jnp.where(first_half, chunk, line - 1 - chunk)

    barrier = pltpu.get_barrier_semaphore()
    for device in (to_row, to_col, to_side):
        pl.semaphore_signal(barrier, inc=1, device_id=device, device_id_type=MESH)

    @pl.when(has_right)
    def _():
        pl.semaphore_signal(barrier, inc=1, device_id=right, device_id_type=MESH)

    @pl.when(has_left)
    def _():
        pl.semaphore_signal(barrier, inc=1, device_id=left, device_id_type=MESH)

    slots = lax.broadcasted_iota(jnp.int32, (8, rows), 1)

    def add_sequence(number, carry):
        end, segments, begins = carry
        start = end
        end = start + jnp.where(r["seq_owner"][number] == dp, r["seq_lengths"][number], 0)
        segments = segments + (end <= slots).astype(jnp.int32)
        begins = jnp.where((start <= slots) & (slots < end), start, begins)
        return end, segments, begins

    nothing = jnp.zeros((8, rows), jnp.int32)
    segments, begins = lax.fori_loop(0, z.seqs, add_sequence, (jnp.int32(0), nothing, nothing))[1:]
    segments = segments.astype(f32)
    r["seg_row"][...] = segments[:1]
    r["seg_col"][...] = turned(segments)[:, :1]
    cot = r["cot"]
    valid = (r["seg_col"][...] < z.seqs).astype(f32)
    r["cotq"][0, row] = cot[...] * valid.astype(bf16)

    def as_row(vector):
        return vector.astype(f32).reshape(1, vector.shape[0])

    r["gainq"][0, row] = jnp.concatenate(
        [
            jnp.broadcast_to(as_row(r["norm_gain"][...]), (8, q)),
            jnp.broadcast_to(as_row(r["norm_shift"][...]), (8, q)),
        ]
    )
    pl.semaphore_wait(barrier, 3 + has_right.astype(jnp.int32) + has_left.astype(jnp.int32))

    def gather(src, held):
        over = Message(src, held.at[0, row], to_row, held.at[0, other_row])
        across = Message(src, held.at[1, row], to_col, held.at[1, row])
        onward = Message(held.at[0, other_row], held.at[1, other_row], to_col, held.at[1, other_row])
        return over, across, onward

    in_over, in_across, in_onward = gather(r["inputs"], r["inq"])
    gain_over, gain_across, gain_onward = gather(r["gainq"].at[0, row], r["gainq"])
    cot_over, cot_across, cot_onward = gather(r["cotq"].at[0, row], r["cotq"])
    cot_side = Message(r["cotq"].at[0, row], r["cotp"].at[row], to_side)
    cot_side_onward = Message(r["cotq"].at[0, other_row], r["cotp"].at[other_row], to_side)
    hid_side = Message(r["hid_send"], r["hid_pair"], to_side)

    end_cot_send, end_cot_recv = take("send", 4), take("recv", 4)

    def end_cot(pair, part, device):
        src = r["cotp"].at[part] if pair else r["cotq"].at[0, part]
        index = 2 * pair + part
        return remote(src, r["end_cot"].at[pair, part], end_cot_send + index, end_cot_recv + index, device)

    end_cot_on_send, end_cot_on_recv = take("send", 2), take("recv", 2)

    def end_cot_on(pair):
        part = r["end_cot"].at[pair, row]
        return remote(part, part, end_cot_on_send + pair, end_cot_on_recv + pair, to_row)

    def send_end_cot(pair, part):
        @pl.when(at_end)
        def _():
            end_cot(pair, part, inward).start()

    def loop(first, last, work):
        def one(k, carry):
            work(k)
            return carry

        lax.fori_loop(first, last, one, 0)

    def pass_on(got, onward):
        def work(k):
            got(k).wait_recv()
            onward(k).start()

        return work

    def waits(*copies):
        def work(k):
            for copy in copies:
                copy(k).wait_recv()

        return work

    class EndRows:
        def __init__(self, own, pair, land):
            self.own, self.pair, self.land = own, pair, land
            self.send, self.recv = take("send", line), take("recv", line)
            self.on_send, self.on_recv = take("send", line), take("recv", line)

        def copy(self, chunk, device, pair):
            src = (self.pair if pair else self.own).at[chunk]
            return remote(src, self.land.at[chunk, int(pair)], self.send + chunk, self.recv + chunk, device)

        def onward(self, chunk):
            part = self.land.at[chunk, col]
            return remote(part, part, self.on_send + chunk, self.on_recv + chunk, to_col)

        def start(self, pair, first, last):
            kind = 1 if pair else 0

            @pl.when(at_end & (col == kind))
            def _():
                def one(number):
                    chunk = jnp.where(place == 0, line - 1 - number, number)
                    self.copy(chunk, inward, pair).start()

                loop(first, last, one)

        def hand_over(self, *numbers):
            @pl.when(near_end)
            def _():
                for number in numbers:
                    chunk = counted(line - 1 - number)
                    self.copy(chunk, outward, False).wait_recv()
                    self.onward(chunk).start()

        def finish(self):
            def one(chunk):
                @pl.when(at_end & (chunk != place))
                def _():
                    self.copy(chunk, inward, False).wait_send()

                @pl.when(near_end)
                def _():
                    gone = jnp.where(place == 1, 0, line - 1)

                    @pl.when(chunk != gone)
                    def _():
                        self.onward(chunk).wait_send()

            loop(0, line, one)

    end_act = EndRows(r["act_own"], r["act_pair"], r["end_act"])
    end_att = EndRows(r["att_own"], r["att_pair"], r["end_att"])
    swaps = {
        "up": Message(r["up_w"].at[:, pl.ds(pl.multiple_of(other_col * z.hidden, 128), z.hidden)], r["up_o"], to_col, r["up_o"]),
        "qkv": Message(r["qkv_w"].at[:, pl.ds(pl.multiple_of(other_col * z.qkv, 128), z.qkv)], r["qkv_o"], to_col, r["qkv_o"]),
        "down": Message(r["down_w"].at[pl.ds(pl.multiple_of(other_col * z.hidden, 16), z.hidden), :], r["down_o"], to_col, r["down_o"]),
        "dense": Message(r["dense_w"].at[pl.ds(pl.multiple_of(other_col * z.features, 16), z.features), :], r["dense_o"], to_col, r["dense_o"]),
    }

    def local(src, dst, index):
        return pltpu.make_async_copy(src, dst, r["local_sem"].at[index])

    stream_base = take("local", 8)
    once = take("local", 4)

    in_over.start()
    gain_over.start()
    in_across.start()
    gain_across.start()
    keep_in = local(r["inputs"], r["inq"].at[0, row], once)
    keep_in.start()
    cot_side.start()
    send_end_cot(0, row)
    swaps["up"].start()
    up_bias, qkv_bias = as_row(r["up_bias"][...]), as_row(r["qkv_bias"][...])
    for tile in range(tiles):
        r["up_b"][tile] = up_bias[:, tile * z.down_chunk : (tile + 1) * z.down_chunk]
    for pair in range(pairs):
        r["qkv_b"][pair] = qkv_bias[:, pair * PAIR_QKV : (pair + 1) * PAIR_QKV]
    position = turned((slots - begins).astype(f32))[:, :1]
    phase = position * r["frequency"][...]
    lane = lax.rem(lax.broadcasted_iota(jnp.int32, (1, PAIR), 1), HEAD_DIM)
    sines = jnp.sin(phase)
    r["tables"][0] = jnp.where(lane < ROT, jnp.cos(phase), 1.0)
    r["tables"][1] = jnp.where(lane < HALF_ROT, sines, 0.0)
    r["tables"][2] = jnp.where((lane >= HALF_ROT) & (lane < ROT), sines, 0.0)
    gain_over.wait()
    gain_onward.start()
    in_over.wait()
    in_onward.start()
    cot_over.start()
    cot_across.start()
    cot_side.wait()
    send_end_cot(1, row)
    keep_in.wait()
    gain_across.wait()
    gain_onward.wait()
    in_across.wait()
    in_onward.wait()

    block = min(64, rows)

    def norm_rows(step, carry):
        at = pl.ds(pl.multiple_of(step * block, block), block)
        parts = [r["inq"][h, p, at].astype(f32) for h in range(2) for p in range(2)]
        total = parts[0] + parts[1] + parts[2] + parts[3]
        squares = parts[0] * parts[0] + parts[1] * parts[1] + parts[2] * parts[2] + parts[3] * parts[3]
        average = jnp.sum(total, axis=1, keepdims=True) / z.width
        variance = jnp.sum(squares, axis=1, keepdims=True) / z.width - average * average
        scale_inv = lax.rsqrt(variance + epsilon)
        r["stat"][0, at] = average
        r["stat"][1, at] = scale_inv
        for h in range(2):
            for p in range(2):
                normed = (parts[2 * h + p] - average) * scale_inv
                gain, shift = r["gainq"][h, p, 0:1, :], r["gainq"][h, p, 8:9, :]
                r["hid"][h, at, p * q : (p + 1) * q] = (normed * gain + shift).astype(bf16)
        return carry

    lax.fori_loop(0, rows // block, norm_rows, 0)
    for c in range(line):
        even = r["hid"][0, :, 2 * c * z.up_chunk : (2 * c + 1) * z.up_chunk]
        odd = r["hid"][0, :, (2 * c + 1) * z.up_chunk : (2 * c + 2) * z.up_chunk]
        at = slice(c * z.up_chunk, (c + 1) * z.up_chunk)
        r["hid_own"][:, at] = jnp.where(side == 0, even, odd)
        r["hid_send"][:, at] = jnp.where(side == 0, odd, even)

    def stream(count, copies, work):
        for copy in copies(jnp.int32(0), jnp.int32(0)):
            copy.start()

        def one(step, carry):
            slot = lax.rem(step, 2)

            @pl.when(step + 1 < count)
            def _():
                for copy in copies(step + 1, 1 - slot):
                    copy.start()

            for copy in copies(step, slot):
                copy.wait()
            work(step, slot)
            return carry

        lax.fori_loop(0, count, one, 0)

    def column_tiles(name, each, tile_of=lambda step: step):
        def copies(step, slot):
            tile = tile_of(step)
            mine = r[name + "_w"].at[:, pl.ds(pl.multiple_of((col * r[name + "_o"].shape[1]) + tile * each, 128), each)]
            theirs = r[name + "_o"].at[:, pl.ds(pl.multiple_of(tile * each, 128), each)]
            return [
                local(mine, r["weight"].at[slot, 0, :, :each], stream_base + slot * 4),
                local(theirs, r["weight"].at[slot, 1, :, :each], stream_base + slot * 4 + 1),
            ]

        return copies

    def row_tiles(name, each, tile_of=lambda step: step):
        def copies(step, slot):
            tile = tile_of(step)
            found = []
            for h in range(2):
                start = tile * each + (col * r[name + "_o"].shape[0] if h == 0 else 0)
                src = r[name + ("_w" if h == 0 else "_o")]
                for p in range(2):
                    found.append(
                        local(
                            src.at[pl.ds(pl.multiple_of(start, 16), each), p * q : (p + 1) * q],
                            r["weight"].at[slot, h, p * q : p * q + each, :],
                            stream_base + slot * 4 + 2 * h + p,
                        )
                    )
            return found

        return copies

    def rank_of(j):
        return jnp.where(col == 1, half_line - 1 - j, j)

    def tile_at(step):
        later = (step >= half_line).astype(jnp.int32)
        return 2 * rank_of(step - later * half_line) + jnp.where(later == 1, side, other_side)

    act_side_send, act_side_recv = take("send", half_line), take("recv", half_line)
    act_col_send, act_col_recv = take("send", half_line), take("recv", half_line)
    act_on_send, act_on_recv = take("send", half_line), take("recv", half_line)

    def act_side(j):
        tile, slot = 2 * rank_of(j) + other_side, col * half_line + rank_of(j)
        return remote(r["act"].at[tile], r["act_pair"].at[slot], act_side_send + j, act_side_recv + j, to_side)

    def act_col(j):
        slot = col * half_line + rank_of(j)
        return remote(r["act_own"].at[slot], r["act_own"].at[slot], act_col_send + j, act_col_recv + j, to_col)

    def act_on(j):
        slot = col * half_line + rank_of(j)
        return remote(r["act_pair"].at[slot], r["act_pair"].at[slot], act_on_send + j, act_on_recv + j, to_col)

    def up_work(step, slot):
        tile = tile_at(step)
        before = contract(r["hid"][0], r["weight"][slot, 0, :, : z.down_chunk], 1, 0)
        before = before + contract(r["hid"][1], r["weight"][slot, 1, :, : z.down_chunk], 1, 0)
        before = before + r["up_b"][tile]
        r["before"][tile] = before
        activated = gelu(before).astype(bf16)
        r["act"][tile] = activated

        @pl.when(step == 0)
        def _():
            act_side(0).start()

        @pl.when(step >= half_line)
        def _():
            j = step - half_line
            r["act_own"][col * half_line + rank_of(j)] = activated
            act_col(j).start()

    hid_side.start()
    swaps["down"].start()
    swaps["up"].wait()
    stream(tiles, column_tiles("up", z.down_chunk, tile_at), up_work)

    cot_over.wait()
    cot_onward.start()

    def start_side(j):
        act_side(j).start()

    loop(1, half_line, start_side)
    pending.append(cot_side_onward)

    @pl.when(near_end)
    def _():
        cot_side_onward.copy().start()

    loop(0, half_line, waits(act_col))
    end_act.start(False, 0, line - 1)

    @pl.when(near_end)
    def _():
        for pair in range(2):
            end_cot(pair, row, outward).wait_recv()
            end_cot_on(pair).start()

    swaps["qkv"].start()
    swaps["dense"].start()
    cot_across.wait()
    cot_onward.wait()
    swaps["down"].wait()

    def each_side(name, count):
        side_send, side_recv = take("send", count), take("recv", count)
        col_send, col_recv = take("send", count), take("recv", count)
        on_send, on_recv = take("send", count), take("recv", count)
        mine, theirs = r[name + "_mine"], r[name + "_theirs"]
        mine_pair, theirs_pair = r[name + "_mine_pair"], r[name + "_theirs_pair"]

        def to_side_peer(k):
            return remote(mine.at[k], mine_pair.at[k], side_send + k, side_recv + k, to_side)

        def to_col_peer(k):
            return remote(mine.at[k], theirs.at[k], col_send + k, col_recv + k, to_col)

        def onward(k):
            return remote(mine_pair.at[k], theirs_pair.at[k], on_send + k, on_recv + k, to_col)

        return to_side_peer, to_col_peer, onward

    db_side, db_col, db_on = each_side("db", tiles)
    dp_side, dp_col, dp_on = each_side("dp", pairs)

    def over_weight_rows(slot, each, lefts):
        total = None
        for h in range(2):
            for p in range(2):
                part = contract(lefts(h, p), r["weight"][slot, h, p * q : p * q + each, :], 1, 1)
                total = part if total is None else total + part
        return total

    def down_work(step, slot):
        tile = step
        d_activated = over_weight_rows(slot, z.down_chunk, lambda h, p: r["cotq"][h, p])
        d_before = (d_activated * gelu_slope(r["before"][tile])).astype(bf16)
        r["db_mine"][tile] = d_before
        sums = jnp.sum(d_before.astype(f32), axis=0, keepdims=True)
        r["sums"][:, pl.ds(pl.multiple_of(2 * q + z.qkv + tile * z.down_chunk, 128), z.down_chunk)] = sums
        db_col(tile).start()
        db_side(tile).start()

    stream(tiles, row_tiles("down", z.down_chunk), down_work)

    class Flow:
        def __init__(self, name, by_col=False, ends=None):
            self.name, self.by_col, self.ends = name, by_col, ends
            self.stage, self.land, self.got = r["st_" + name], r["land_" + name], r["got_" + name]
            self.count, self.depth, self.each = flows_of(z)[name]
            self.send = take("send", 2 * line)
            self.recv = take("recv", 2 * (line + 2))
            self.local = take("local", 2)
            self.done = False

        def half(self, group):
            return jnp.where(col == 0, group, 1 - group) if self.by_col else group

        def staged(self, chunk, half, tiles=slice(None)):
            return self.stage.at[chunk, half, tiles, :, : self.each]

        def copy(self, chunk, group, slot, device):
            half = self.half(group)
            return remote(
                self.staged(chunk, half),
                self.land.at[slot, half],
                self.send + 2 * chunk + group,
                self.recv + 2 * slot + group,
                device,
            )

        def keep(self, chunk, group, tile, value):
            self.stage[chunk, self.half(group), tile, :, : self.each] = value.astype(bf16)

        def add(self, chunk, group, slot, device):
            half = self.half(group)
            self.copy(chunk, group, slot, device).wait_recv()
            got = self.got.at[:, :, : self.each]
            bring = local(self.land.at[slot, half], got, self.local)
            bring.start()
            bring.wait()
            for tile in range(self.count):
                whole = self.stage[chunk, half, tile, :, : self.each].astype(f32) + got[tile].astype(f32)
                self.keep(chunk, group, tile, whole)

        def out_from_end(self, number, tile=None):
            @pl.when(at_end)
            def _():
                chunk = counted(line - 1 - number)
                slot = chunk if number < line - 2 else jnp.where(first_half, line, line + 1)
                for group in range(2):
                    half = self.half(group)
                    if tile is None:
                        self.copy(chunk, group, slot, inward).start()
                    else:
                        remote(
                            self.staged(chunk, half, tile),
                            self.land.at[slot, half, tile],
                            self.send + 2 * chunk + group,
                            self.recv + 2 * slot + group,
                            inward,
                        ).start()

        def to_mate(self, number):
            @pl.when(near_end)
            def _():
                chunk = counted(line - 1 - number)
                slot = chunk if number == 0 else jnp.where(first_half, line, line + 1)
                if self.ends is not None:
                    self.product(chunk, True)
                for group in range(2):
                    if self.ends is None:
                        self.add(chunk, group, chunk, outward)
                    self.copy(chunk, group, slot, mate).start()

        def to_end(self):
            @pl.when(near_end)
            def _():
                chunk = counted(0)
                slot = jnp.where(first_half, line + 1, line)
                if self.ends is not None:
                    self.product(chunk, False)
                for group in range(2):
                    self.add(chunk, group, chunk, mate)
                    self.copy(chunk, group, slot, outward).start()

        def own(self):
            if self.ends is not None:

                @pl.when(at_end)
                def _():
                    self.product(place, False)

                @pl.when(near_end)
                def _():
                    self.product(place, True)

            self.copy_out().start()

        def copy_out(self):
            return local(self.staged(place, slice(None)), r["own_" + self.name], self.local + 1)

        def sent(self, wait_out=True):
            self.done = True
            if wait_out:
                self.copy_out().wait()

            def one(chunk):
                for group in range(2):
                    self.copy(chunk, group, chunk, inward).wait_send()

            if self.ends is None:

                @pl.when(at_end)
                def _():
                    for number in range(line - 1):
                        one(counted(line - 1 - number))

            @pl.when(near_end)
            def _():
                for chunk in (line - 1, line - 2, 0):
                    one(counted(chunk))

        def finish(self):
            far = 0 if self.ends is None else 1
            for group in range(2):

                @pl.when(place > far)
                def _():
                    self.copy(place, group, line, left).wait_recv()

                @pl.when(place < line - 1 - far)
                def _():
                    self.copy(place, group, line + 1, right).wait_recv()

    class ColumnFlow(Flow):
        def __init__(self, name, own, pair):
            super().__init__(name, by_col=True)
            self.own_columns, self.pair_columns = own, pair

        def products(self, tile):
            for group in range(2):
                full = contract(r["hid_own"][...], r[self.own_columns[group]][tile], 0, 0)
                full = full + contract(r["hid_pair"][...], r[self.pair_columns[group]][tile], 0, 0)
                for chunk in range(line):
                    self.keep(chunk, group, tile, full[chunk * self.depth : (chunk + 1) * self.depth])

    class RowFlow(Flow):
        def __init__(self, name, own, pair, ends):
            super().__init__(name, ends=ends)
            self.own_rows, self.pair_rows = own, pair

        def product(self, chunk, with_end):
            copies = self.bring_end(chunk) if with_end else []
            for copy in copies:
                copy.start()
            for group in range(2):
                full = contract(self.own_rows[chunk], r["cotq"][0, group], 0, 0)
                full = full + contract(self.pair_rows[chunk], r["cotp"][group], 0, 0)
                for copy in copies:
                    copy.wait()
                copies = []
                if with_end:
                    for pair in range(2):
                        rows_in = r["weight"][1, pair, :rows, : self.count * self.depth]
                        cot_in = r["weight"][0, pair, group * rows : (group + 1) * rows, :q]
                        full = full + contract(rows_in, cot_in, 0, 0)
                for tile in range(self.count):
                    self.keep(chunk, group, tile, full[tile * self.depth : (tile + 1) * self.depth])

        def bring_end(self, chunk):
            copies = []
            self.ends.onward(chunk).wait_recv()
            for pair in range(2):
                rows_in = self.ends.land.at[chunk, pair]
                copies.append(local(rows_in, r["weight"].at[1, pair, :rows, : rows_in.shape[1]], stream_base + pair))
                for part in range(2):
                    at = r["weight"].at[0, pair, part * rows : (part + 1) * rows, :q]
                    copies.append(local(r["end_cot"].at[pair, part], at, stream_base + 2 + 2 * pair + part))
            return copies

    down = RowFlow("down", r["act_own"], r["act_pair"], end_act)
    up = ColumnFlow("up", ("db_mine", "db_theirs"), ("db_mine_pair", "db_theirs_pair"))
    dense = RowFlow("dense", r["att_own"], r["att_pair"], end_att)
    qkv = ColumnFlow("qkv", ("dp_mine", "dp_theirs"), ("dp_mine_pair", "dp_theirs_pair"))
    swaps["qkv"].wait()

    def qkv_work(step, slot):
        part = contract(r["hid"][0], r["weight"][slot, 0, :, :PAIR_QKV], 1, 0)
        part = part + contract(r["hid"][1], r["weight"][slot, 1, :, :PAIR_QKV], 1, 0)
        r["total"][step, :, :PAIR_QKV] = part + r["qkv_b"][step]

    stream(pairs, column_tiles("qkv", PAIR_QKV), qkv_work)
    swaps["dense"].wait()

    def dense_work(step, slot):
        d_mixed = over_weight_rows(slot, z.features, lambda h, p: r["cotq"][h, p]).astype(bf16)
        for pair in range(pairs):
            r["mixed"][pair] = d_mixed[:, pair * PAIR : (pair + 1) * PAIR]

    stream(1, row_tiles("dense", z.features), dense_work)
    loop(0, 1, pass_on(act_side, act_on))
    loop(0, 1, waits(act_on))
    end_act.start(True, 0, 1)
    att_side_send, att_side_recv = take("send", half_line), take("recv", half_line)
    att_col_send, att_col_recv = take("send", half_line), take("recv", half_line)
    att_on_send, att_on_recv = take("send", half_line), take("recv", half_line)

    def att_side(k):
        slot = col * half_line + k
        return remote(
            r["att_part"].at[2 * k + other_side], r["att_pair"].at[slot], att_side_send + k, att_side_recv + k, to_side
        )

    def att_col(k):
        slot = col * half_line + k
        return remote(r["att_own"].at[slot], r["att_own"].at[slot], att_col_send + k, att_col_recv + k, to_col)

    def att_on(k):
        slot = col * half_line + k
        return remote(r["att_pair"].at[slot], r["att_pair"].at[slot], att_on_send + k, att_on_recv + k, to_col)

    def head_pair(pair):
        attended, d_projected = attention_pair(
            r["total"][pair, :, :PAIR_QKV], r["mixed"][pair], r["tables"], r["seg_col"][...], r["seg_row"][...]
        )
        r["dp_mine"][pair] = d_projected
        dp_side(pair).start()
        dp_col(pair).start()
        sums = jnp.sum(d_projected.astype(f32), axis=0, keepdims=True)
        r["sums"][:, pl.ds(pl.multiple_of(2 * q + pair * PAIR_QKV, 128), PAIR_QKV)] = sums
        r["att"][:, pl.ds(pl.multiple_of(pair * PAIR, PAIR), PAIR)] = attended
        each = PAIR // z.dense_chunk
        for part in range(each):
            chunk = pair * each + part
            k = chunk // 2
            piece = attended[:, part * z.dense_chunk : (part + 1) * z.dense_chunk]

            @pl.when(lax.rem(chunk, 2) == side)
            def _():
                r["att_own"][col * half_line + k] = piece
                att_col(k).start()

            @pl.when(lax.rem(chunk, 2) == other_side)
            def _():
                r["att_part"][chunk] = piece
                att_side(k).start()

    def near_end_cot():
        @pl.when(near_end)
        def _():
            cot_side_onward.wait()
            for pair in range(2):
                end_cot_on(pair).wait_recv()

    def pair_and_more(pair):
        head_pair(pair)

        @pl.when(pair == 0)
        def _():
            loop(1, half_line, pass_on(act_side, act_on))
            loop(1, half_line, waits(act_on))
            end_act.start(True, 1, line - 1)
            end_act.hand_over(0)

        @pl.when(pair == 1)
        def _():
            near_end_cot()
            down.to_mate(0)
            end_act.hand_over(1, 2)

    loop(0, pairs, pair_and_more)
    down.to_mate(1)

    @pl.when(at_end)
    def _():
        cot_side_onward.copy().start()


    def scatter(name, total, earlier=None):
        across = Message(r["part_send"], r[name + "_got"], to_col)
        over = Message(r["part_row"], r[name + "_row"], to_row)

        def free(message):
            message.copy().wait_send()
            pending.remove(message)

        def first():
            if earlier is not None:
                free(earlier[0])
            for p in range(2):
                r["part_send"][p] = total[2 + p].astype(bf16)
            across.start()

        def second():
            across.wait()
            if earlier is not None:
                free(earlier[1])
            for p in range(2):
                total[p] = total[p] + r[name + "_got"][p].astype(f32)
            r["part_row"][...] = total[other_row].astype(bf16)
            over.start()
            return total[row]

        def third(part):
            over.wait()
            return part + r[name + "_row"][...].astype(f32)

        return first, second, third, (across, over)

    total = r["total"]

    def down_out(step, slot):
        for h in range(2):
            for p in range(2):
                part = contract(r["act"][step], r["weight"][slot, h, p * q : p * q + z.down_chunk, :], 1, 0)

                @pl.when(step == 0)
                def _():
                    total[2 * h + p] = part

                @pl.when(step > 0)
                def _():
                    total[2 * h + p] = total[2 * h + p] + part

    def dense_out(step, slot):
        for h in range(2):
            for p in range(2):
                part = contract(r["att"][...], r["weight"][slot, h, p * q : p * q + z.features, :], 1, 0)
                total[2 * h + p] = total[2 * h + p] + part

    def up_back(step, slot):
        for h in range(2):
            for p in range(2):
                part = contract(r["db_mine"][step], r["weight"][slot, h, p * q : (p + 1) * q, : z.down_chunk], 1, 1)

                @pl.when(step == 0)
                def _():
                    total[2 * h + p] = part

                @pl.when(step > 0)
                def _():
                    total[2 * h + p] = total[2 * h + p] + part

    def qkv_back(step, slot):
        for h in range(2):
            for p in range(2):
                part = contract(r["dp_mine"][step], r["weight"][slot, h, p * q : (p + 1) * q, :PAIR_QKV], 1, 1)
                total[2 * h + p] = total[2 * h + p] + part

    def take_d_before(tile):
        loop(tile, tile + 1, pass_on(db_side, db_on))
        loop(tile, tile + 1, waits(db_col, db_on))
        up.products(tile)
        up.out_from_end(0, tile)
        up.out_from_end(1, tile)

    hid_side.wait()
    take_d_before(0)
    stream(tiles, column_tiles("up", z.down_chunk), up_back)
    take_d_before(1)
    stream(pairs, column_tiles("qkv", PAIR_QKV), qkv_back)
    dh_first, dh_second, dh_third, dh_messages = scatter("dh", total)
    dh_first()
    for tile in range(2, tiles):
        take_d_before(tile)
    up.out_from_end(2)
    down.to_end()
    r["grad_inputs"][...] = dh_second()
    up.to_mate(0)
    up.to_mate(1)
    stream(tiles, row_tiles("down", z.down_chunk), down_out)
    stream(1, row_tiles("dense", z.features), dense_out)
    out_first, out_second, out_third, out_messages = scatter("out", total, dh_messages)
    out_first()

    d_hidden = dh_third(r["grad_inputs"][...])
    r["grad_inputs"][...] = d_hidden
    own_in = r["inq"].at[0, row]
    gain = r["gainq"][0, row, 0:1, :]
    sums_row = Message(r["sum_send"].at[0], r["sum_got"].at[0], to_row)
    sums_col = Message(r["sum_send"].at[1], r["sum_got"].at[1], to_col)
    normed = (own_in[...].astype(f32) - r["stat"][0]) * r["stat"][1]
    d_normed = d_hidden * gain
    lane = lax.broadcasted_iota(jnp.int32, (rows, 128), 1)
    one = jnp.sum(d_normed, axis=1, keepdims=True)
    two = jnp.sum(d_normed * normed, axis=1, keepdims=True)
    packed = jnp.where(lane == 0, one, jnp.where(lane == 1, two, 0.0))
    r["sum_send"][0] = turned(packed)[:8]
    sums_row.start()
    r["sums"][:, 0:q] = jnp.sum(d_hidden * normed, axis=0, keepdims=True)
    r["sums"][:, q : 2 * q] = jnp.sum(d_hidden, axis=0, keepdims=True)
    r["sums"][:, 2 * q + z.qkv + z.hidden :] = jnp.sum(r["cotq"][0, row].astype(f32), axis=0, keepdims=True)
    small_side = Message(r["sums"], r["sums_got"].at[0], to_side)
    small_side.start()

    small_send, small_recv = take("send", 2), take("recv", 2)

    def small(way, device):
        return remote(r["sums_send"].at[way], r["sums_got"].at[1 + way], small_send + way, small_recv + way, device)

    def hop(number):
        for way, rank, device, last in ((0, place, right, has_right), (1, line - 1 - place, left, has_left)):

            @pl.when((rank == number) & last)
            def _():
                @pl.when(rank == 0)
                def _():
                    r["sums_send"][way] = r["sums"][...]

                @pl.when(rank > 0)
                def _():
                    small(way, device).wait_recv()
                    r["sums_send"][way] = r["sums"][...] + r["sums_got"][1 + way]

                small(way, device).start()

    branch = out_second()
    total[0] = branch

    @pl.when(near_end)
    def _():
        down.product(place, True)
        down.copy_out().start()
        down.copy_out().wait()

    down.sent(wait_out=False)
    for pair in range(pairs):
        loop(pair, pair + 1, pass_on(dp_side, dp_on))
        loop(pair, pair + 1, waits(dp_col, dp_on))
        qkv.products(pair)
    loop(0, half_line, pass_on(att_side, att_on))
    loop(0, half_line, waits(att_col, att_on))
    end_att.start(False, 0, line - 1)
    end_att.start(True, 0, line - 1)
    small_side.wait()
    small_side.copy().wait_send()
    pending.remove(small_side)
    r["sums"][...] = r["sums"][...] + r["sums_got"][0]
    hop(0)
    for number in range(line - 1):
        qkv.out_from_end(number)
    up.to_end()
    hop(1)
    sums_row.wait()
    r["sum_send"][1] = r["sum_send"][0] + r["sum_got"][0]
    sums_col.start()
    up.own()
    end_att.hand_over(0, 1, 2)
    dense.to_mate(0)
    dense.to_mate(1)
    hop(2)
    qkv.to_mate(0)
    dense.to_end()
    qkv.to_mate(1)
    qkv.to_end()
    qkv.own()

    qkv.copy_out().wait()

    @pl.when(at_end)
    def _():
        cot_side_onward.wait()
        down.product(place, False)
        down.copy_out().start()

    dense.own()

    @pl.when(at_end)
    def _():
        down.copy_out().wait()

    branch = out_third(total[0])
    bias = as_row(r["out_bias"][...])
    valid = (r["seg_col"][...] < z.seqs).astype(f32)
    r["outputs"][...] = (r["inq"][0, row].astype(f32) + valid * (branch + bias)).astype(bf16)
    sums_col.wait()
    both = r["sum_send"][1] + r["sum_got"][1]
    spread = turned(jnp.concatenate([both, jnp.zeros((120, rows), f32)], axis=0))
    part_one, part_two = spread[:, 0:1] / z.width, spread[:, 1:2] / z.width
    normed = (own_in[...].astype(f32) - r["stat"][0]) * r["stat"][1]
    d_normed = r["grad_inputs"][...] * gain
    r["grad_inputs"][...] = cot[...].astype(f32) + r["stat"][1] * (d_normed - part_one - normed * part_two)

    r["small"][...] = r["sums"][...]

    @pl.when(place == line - 1)
    def _():
        small(0, left).wait_recv()

    @pl.when(place == 0)
    def _():
        small(1, right).wait_recv()

    @pl.when(has_left)
    def _():
        r["small"][...] = r["small"][...] + r["sums_got"][1]

    @pl.when(has_right)
    def _():
        r["small"][...] = r["small"][...] + r["sums_got"][2]

    @pl.when(has_right)
    def _():
        small(0, right).wait_send()

    @pl.when(has_left)
    def _():
        small(1, left).wait_send()

    up.sent()
    dense.sent()
    qkv.sent(wait_out=False)
    for flow in (down, up, dense, qkv):
        flow.finish()
    end_act.finish()
    end_att.finish()

    @pl.when(at_end)
    def _():
        for pair in range(2):
            end_cot(pair, row, inward).wait_send()

    @pl.when(near_end)
    def _():
        for pair in range(2):
            end_cot_on(pair).wait_send()

    for message in pending:
        message.copy().wait_send()

    def sent(*copies):
        def work(k):
            for copy in copies:
                copy(k).wait_send()

        return work

    loop(0, half_line, sent(act_side, act_col, act_on, att_side, att_col, att_on))
    loop(0, tiles, sent(db_side, db_col, db_on))
    loop(0, pairs, sent(dp_side, dp_col, dp_on))
    assert marks["send"] <= SENDS * line and marks["recv"] <= SENDS * line and marks["local"] <= LOCALS


def on_device(
    dp_size,
    inputs,
    norm_gain,
    norm_shift,
    qkv_weight,
    qkv_bias,
    up_weight,
    up_bias,
    dense_weight,
    down_weight,
    out_bias,
    cotangent,
    seq_lengths,
    seq_owner,
):
    z = Sizes(dp_size, inputs, qkv_weight, up_weight, dense_weight, down_weight, seq_lengths)
    if not fits(z):
        return on_device_plain(
            dp_size,
            inputs,
            norm_gain,
            norm_shift,
            qkv_weight,
            qkv_bias,
            up_weight,
            up_bias,
            dense_weight,
            down_weight,
            out_bias,
            cotangent,
            seq_lengths,
            seq_owner,
        )
    rows, q, line = z.rows, z.quarter, z.line
    lane_rate = np.zeros((1, HEAD_DIM), np.float32)
    lane_rate[0, :ROT] = rope_base ** (-2.0 * (np.arange(ROT) % HALF_ROT) / ROT)
    lane_rate = np.tile(lane_rate, (1, 2))
    operands = dict(
        inputs=(inputs, pl.ANY),
        cot=(cotangent, pltpu.VMEM),
        norm_gain=(norm_gain, pltpu.VMEM),
        norm_shift=(norm_shift, pltpu.VMEM),
        qkv_bias=(qkv_bias, pltpu.VMEM),
        up_bias=(up_bias, pltpu.VMEM),
        out_bias=(out_bias, pltpu.VMEM),
        frequency=(jnp.asarray(lane_rate), pltpu.VMEM),
        seq_lengths=(seq_lengths, pltpu.SMEM),
        seq_owner=(seq_owner, pltpu.SMEM),
        up_w=(up_weight, pl.ANY),
        down_w=(down_weight, pl.ANY),
        qkv_w=(qkv_weight, pl.ANY),
        dense_w=(dense_weight, pl.ANY),
    )
    results = dict(
        outputs=((rows, q), bf16, pltpu.VMEM),
        grad_inputs=((rows, q), f32, pltpu.VMEM),
        small=((1, 3 * q + z.qkv + z.hidden), f32, pltpu.VMEM),
        up_o=((z.half, z.hidden), bf16, pl.ANY),
        down_o=((z.hidden, z.half), bf16, pl.ANY),
        qkv_o=((z.half, z.qkv), bf16, pl.ANY),
        dense_o=((z.features, z.half), bf16, pl.ANY),
        end_cot=((2, 2, rows, q), bf16, pl.ANY),
        end_act=((line, 2, rows, z.down_chunk), bf16, pl.ANY),
        end_att=((line, 2, rows, z.dense_chunk), bf16, pl.ANY),
    )
    for name, shape in flows_of(z).items():
        results["land_" + name] = ((line + 2, 2) + shape, bf16, pl.ANY)
        results["own_" + name] = ((2,) + shape, bf16, pl.ANY)
    scratch = scratch_of(z)
    names = list(operands) + list(results) + list(scratch) + ["send_sem", "recv_sem", "local_sem"]
    found = pl.pallas_call(
        partial(layer_kernel, z, names),
        in_specs=[pl.BlockSpec(memory_space=space) for value, space in operands.values()],
        out_specs=[pl.BlockSpec(memory_space=space) for shape, kind, space in results.values()],
        out_shape=[jax.ShapeDtypeStruct(shape, kind) for shape, kind, space in results.values()],
        scratch_shapes=[pltpu.VMEM(shape, kind) for shape, kind in scratch.values()]
        + [pltpu.SemaphoreType.DMA((SENDS * line,)), pltpu.SemaphoreType.DMA((SENDS * line,)), pltpu.SemaphoreType.DMA((LOCALS,))],
        compiler_params=pltpu.CompilerParams(
            collective_id=0, has_side_effects=True, vmem_limit_bytes=VMEM_LIMIT
        ),
        name="layer",
    )(*[value for value, space in operands.values()])
    got = dict(zip(results, found))
    big, small = finish(z, got)
    return (
        big["outputs"],
        big["grad_inputs"],
        small["gain"],
        small["shift"],
        big["qkv"],
        small["qkv"],
        big["up"],
        small["up"],
        big["dense"],
        big["down"],
        small["out"],
    )


def finish(z, got):
    line, steps = z.line, 8
    flows = flows_of(z)
    names = list(flows)
    pieces = dict(gain=z.quarter, shift=z.quarter, qkv=z.qkv, up=z.hidden, out=z.quarter)

    def kernel(*refs):
        place = lax.axis_index("dp") // 2
        fed = refs[: 3 * len(names) + 3]
        made = refs[3 * len(names) + 3 :]
        for index in range(len(names)):
            own, from_left, from_right = (ref[...].astype(f32) for ref in fed[3 * index : 3 * index + 3])
            far = 1 if names[index] in ("down", "dense") else 0
            total = own + jnp.where(place > far, from_left, 0.0) + jnp.where(place < line - 1 - far, from_right, 0.0)
            made[index][...] = total.reshape(made[index].shape)
        outputs, grad_inputs, small = fed[3 * len(names) :]
        made[len(names)][...] = outputs[...]
        made[len(names) + 1][...] = grad_inputs[...]

        @pl.when(pl.program_id(0) == 0)
        def _():
            start = 0
            for index, width in enumerate(pieces.values()):
                made[len(names) + 2 + index][...] = small[:, start : start + width].reshape(width)
                start += width

    in_specs, out_specs, out_shape, fed = [], [], [], []
    for name in names:
        count, depth, each = flows[name]
        group = count // (steps // 2) or 1

        def tile_index(step, name=name):
            half, tile = step // (steps // 2), lax.rem(step, steps // 2)
            return half, tile if flows[name][0] >= steps // 2 else 0

        block = (None, group, depth, each)
        land_block = (None, None, group, depth, each)
        in_specs.append(pl.BlockSpec(block, lambda i, f=tile_index: (*f(i), 0, 0)))
        in_specs.append(pl.BlockSpec(land_block, lambda i, f=tile_index: (line, *f(i), 0, 0)))
        in_specs.append(pl.BlockSpec(land_block, lambda i, f=tile_index: (line + 1, *f(i), 0, 0)))
        fed += [got["own_" + name], got["land_" + name], got["land_" + name]]
        if name == "down":
            out_shape.append(jax.ShapeDtypeStruct((count * depth, 2 * each), f32))
            out_specs.append(pl.BlockSpec((group * depth, each), lambda i, f=tile_index: f(i)[::-1]))
        else:
            assert group == 1
            out_shape.append(jax.ShapeDtypeStruct((depth, 2 * count * each), f32))
            out_specs.append(
                pl.BlockSpec((depth, each), lambda i, f=tile_index, count=count: (0, f(i)[0] * count + f(i)[1]))
            )
    for name in ("outputs", "grad_inputs"):
        rows, columns = got[name].shape
        spec = pl.BlockSpec((rows // steps, columns), lambda i: (i, 0))
        in_specs.append(spec)
        out_specs.append(spec)
        out_shape.append(jax.ShapeDtypeStruct((rows, columns), got[name].dtype))
        fed.append(got[name])
    in_specs.append(pl.BlockSpec(memory_space=pltpu.VMEM))
    fed.append(got["small"])
    for width in pieces.values():
        out_specs.append(pl.BlockSpec(memory_space=pltpu.VMEM))
        out_shape.append(jax.ShapeDtypeStruct((width,), f32))
    made = pl.pallas_call(
        kernel, grid=(steps,), in_specs=in_specs, out_specs=out_specs, out_shape=out_shape, name="finish"
    )(*fed)
    big = dict(zip(names + ["outputs", "grad_inputs"], made))
    return big, dict(zip(pieces, made[len(names) + 2 :]))


def attention_kernel(proj_ref, mixed_ref, tables_ref, seg_col_ref, seg_row_ref, attended_ref, grad_ref):
    attended_ref[...], grad_ref[...] = attention_pair(
        proj_ref[...], mixed_ref[...], tables_ref, seg_col_ref[...], seg_row_ref[...]
    )


def attention(projected, mixed, tables, segment):
    rows, width = projected.shape
    pairs = width // PAIR_QKV
    return pl.pallas_call(
        attention_kernel,
        grid=(pairs,),
        in_specs=[
            pl.BlockSpec((rows, PAIR_QKV), lambda i: (0, i)),
            pl.BlockSpec((rows, PAIR), lambda i: (0, i)),
            pl.BlockSpec((3, rows, PAIR), lambda i: (0, 0, 0)),
            pl.BlockSpec((rows, 1), lambda i: (0, 0)),
            pl.BlockSpec((1, rows), lambda i: (0, 0)),
        ],
        out_specs=[
            pl.BlockSpec((rows, PAIR), lambda i: (0, i)),
            pl.BlockSpec((rows, PAIR_QKV), lambda i: (0, i)),
        ],
        out_shape=[
            jax.ShapeDtypeStruct((rows, pairs * PAIR), bf16),
            jax.ShapeDtypeStruct((rows, width), bf16),
        ],
        compiler_params=pltpu.CompilerParams(vmem_limit_bytes=48 * 1024 * 1024),
        cost_estimate=pl.CostEstimate(
            flops=14 * 2 * pairs * rows * rows * HEAD_DIM * 2,
            bytes_accessed=rows * width * 7,
            transcendentals=2 * pairs * rows * rows,
        ),
        name="attention",
    )(projected, mixed, tables, segment[:, None], segment[None, :])


def dot_plain(left, right):
    return jnp.dot(left, right, preferred_element_type=f32)


def contract_rows(left, right):
    return lax.dot_general(left, right, (((0,), (0,)), ((), ())), preferred_element_type=f32)


def contract_cols(left, right):
    return lax.dot_general(left, right, (((1,), (1,)), ((), ())), preferred_element_type=f32)


def on_device_plain(
    dp_size,
    inputs,
    norm_gain,
    norm_shift,
    qkv_weight,
    qkv_bias,
    up_weight,
    up_bias,
    dense_weight,
    down_weight,
    out_bias,
    cotangent,
    seq_lengths,
    seq_owner,
):
    row_count = inputs.shape[0]
    line = dp_size // 2
    device = lax.axis_index("dp")
    place = device // 2
    side = device % 2
    row = lax.axis_index("row")
    col = lax.axis_index("col")

    over_row = partial(lax.ppermute, axis_name="row", perm=[(0, 1), (1, 0)])
    over_col = partial(lax.ppermute, axis_name="col", perm=[(0, 1), (1, 0)])
    over_side = partial(lax.ppermute, axis_name="dp", perm=[(e, e ^ 1) for e in range(dp_size)])

    def in_order(index, mine, other, axis):
        first = jnp.where(index == 0, mine, other)
        second = jnp.where(index == 0, other, mine)
        return jnp.concatenate([first, second], axis=axis)

    def half_at(array, index, axis):
        width = array.shape[axis] // 2
        return lax.dynamic_slice_in_dim(array, index * width, width, axis)

    segment, position, is_valid = layout(seq_lengths, seq_owner, device, row_count)
    tables = jnp.tile(rotation_tables(position), (1, 1, 2))

    gains = jnp.stack([norm_gain, norm_shift])
    grad_branch = cotangent * is_valid.astype(bf16)[:, None]
    inputs_half = in_order(row, inputs, over_row(inputs), 1)
    gains_half = in_order(row, gains, over_row(gains), 1)
    inputs_other = over_col(inputs_half)
    gains_other = over_col(gains_half)
    branch_half = in_order(row, grad_branch, over_row(grad_branch), 1)
    branch_other = over_col(branch_half)

    up_mine, up_other = half_at(up_weight, col, 1), over_col(half_at(up_weight, 1 - col, 1))
    down_mine, down_other = half_at(down_weight, col, 0), over_col(half_at(down_weight, 1 - col, 0))
    qkv_mine, qkv_other = half_at(qkv_weight, col, 1), over_col(half_at(qkv_weight, 1 - col, 1))
    dense_mine, dense_other = half_at(dense_weight, col, 0), over_col(half_at(dense_weight, 1 - col, 0))

    width = 4 * inputs.shape[1]
    source, source_other = inputs_half.astype(f32), inputs_other.astype(f32)
    average = (jnp.sum(source, axis=1) + jnp.sum(source_other, axis=1)) / width
    square = (jnp.sum(source * source, axis=1) + jnp.sum(source_other * source_other, axis=1)) / width
    scale_inv = lax.rsqrt(square - average * average + epsilon)[:, None]

    def hidden_of(rows_in, gain_pair):
        normed = (rows_in - average[:, None]) * scale_inv
        pair = gain_pair.astype(f32)
        return (normed * pair[0] + pair[1]).astype(bf16)

    hidden, hidden_other = hidden_of(source, gains_half), hidden_of(source_other, gains_other)

    before = dot_plain(hidden, up_mine) + dot_plain(hidden_other, up_other) + up_bias.astype(f32)
    activated = jax.nn.gelu(before, approximate=True).astype(bf16)
    d_activated = contract_cols(branch_half, down_mine) + contract_cols(branch_other, down_other)
    unused_value, gelu_back = jax.vjp(partial(jax.nn.gelu, approximate=True), before)
    d_before = gelu_back(d_activated)[0].astype(bf16)

    projected = dot_plain(hidden, qkv_mine) + dot_plain(hidden_other, qkv_other) + qkv_bias.astype(f32)
    d_mixed = (contract_cols(branch_half, dense_mine) + contract_cols(branch_other, dense_other)).astype(bf16)
    attended, d_projected = attention(projected, d_mixed, tables, segment)

    def chunks_of(array, index):
        rows, columns = array.shape
        grouped = array.reshape(rows, columns // (2 * chunk), 2, chunk)
        return lax.dynamic_index_in_dim(grouped, index, 2, keepdims=False).reshape(rows, columns // 2)

    branch_pair = over_side(branch_half)

    def feature_sums(array):
        kept = chunks_of(array, side)
        got = over_side(chunks_of(array, 1 - side))
        own = in_order(col, kept, over_col(kept), 1)
        pair = in_order(col, got, over_col(got), 1)
        return (contract_rows(own, branch_half) + contract_rows(pair, branch_pair)).astype(bf16)

    def along_line(sums):
        depth = sums.shape[0] // line
        parts = sums.reshape(line, depth, sums.shape[1])

        def part(index):
            return lax.dynamic_index_in_dim(parts, jnp.clip(index, 0, line - 1), 0, keepdims=False).astype(f32)

        rightward, leftward = None, None
        for step in range(line - 1):
            right_part = part(line - 1 - step + place)
            left_part = part(place - (line - 1) + step)
            if step:
                right_part = right_part + rightward.astype(f32)
                left_part = left_part + leftward.astype(f32)
            to_right = [(2 * z + x, 2 * z + 2 + x) for z in range(min(step + 1, line - 1)) for x in range(2)]
            to_left = [(dp_size - 1 - p, dp_size - 1 - q) for p, q in to_right]
            rightward = lax.ppermute(right_part.astype(bf16), "dp", to_right)
            leftward = lax.ppermute(left_part.astype(bf16), "dp", to_left)
        return part(place) + rightward.astype(f32) + leftward.astype(f32)

    chunk = down_weight.shape[0] // dp_size
    grad_down = along_line(feature_sums(activated))

    chunk = up_weight.shape[0] // dp_size
    hidden_own = chunks_of(hidden, side)
    hidden_pair = over_side(chunks_of(hidden, 1 - side))

    def hidden_sums(array):
        pair = over_side(array)
        mine = (contract_rows(hidden_own, array) + contract_rows(hidden_pair, pair)).astype(bf16)
        theirs = (contract_rows(hidden_own, over_col(array)) + contract_rows(hidden_pair, over_col(pair))).astype(bf16)
        return in_order(col, along_line(mine), along_line(theirs), 1)

    grad_up = hidden_sums(d_before)
    chunk = dense_weight.shape[0] // dp_size
    grad_dense = along_line(feature_sums(attended))
    grad_qkv = hidden_sums(d_projected)

    def scatter(mine, other):
        half = mine + over_col(other.astype(bf16)).astype(f32)
        return half_at(half, row, 1) + over_row(half_at(half, 1 - row, 1).astype(bf16)).astype(f32)

    branch = scatter(
        dot_plain(attended, dense_mine) + dot_plain(activated, down_mine),
        dot_plain(attended, dense_other) + dot_plain(activated, down_other),
    )
    valid_col = is_valid.astype(f32)[:, None]
    outputs = (inputs.astype(f32) + valid_col * (branch + out_bias.astype(f32))).astype(bf16)

    d_hidden = scatter(
        contract_cols(d_projected, qkv_mine) + contract_cols(d_before, up_mine),
        contract_cols(d_projected, qkv_other) + contract_cols(d_before, up_other),
    )
    normed = (inputs.astype(f32) - average[:, None]) * scale_inv
    d_normed = d_hidden * norm_gain.astype(f32)
    row_sums = jnp.stack([jnp.sum(d_normed, axis=1), jnp.sum(d_normed * normed, axis=1)])
    row_sums = row_sums + over_row(row_sums)
    row_sums = row_sums + over_col(row_sums)
    grad_inputs = cotangent.astype(f32) + scale_inv * (
        d_normed - row_sums[0][:, None] / width - normed * row_sums[1][:, None] / width
    )

    small = [
        jnp.sum(d_hidden * normed, axis=0),
        jnp.sum(d_hidden, axis=0),
        jnp.sum(d_projected.astype(f32), axis=0),
        jnp.sum(d_before.astype(f32), axis=0),
        jnp.sum(grad_branch.astype(f32), axis=0),
    ]
    together = jnp.concatenate(small)
    bit = 1
    while bit < dp_size:
        together = together + lax.ppermute(together, "dp", [(e, e ^ bit) for e in range(dp_size)])
        bit *= 2
    ends = []
    for piece in small:
        ends.append((ends[-1] if ends else 0) + piece.shape[0])
    grad_gain, grad_shift, grad_qkv_bias, grad_up_bias, grad_out_bias = jnp.split(together, ends[:-1])
    return (
        outputs,
        grad_inputs,
        grad_gain,
        grad_shift,
        grad_qkv,
        grad_qkv_bias,
        grad_up,
        grad_up_bias,
        grad_dense,
        grad_down,
        grad_out_bias,
    )


def solution(mesh):
    in_specs = (
        P("dp", ("col", "row")),
        P(("col", "row")),
        P(("col", "row")),
        P("col", "row"),
        P(("row", "col")),
        P("col", "row"),
        P(("row", "col")),
        P("row", "col"),
        P("row", "col"),
        P(("col", "row")),
        P("dp", ("col", "row")),
        P(),
        P(),
    )
    out_specs = (
        P("dp", ("col", "row")),
        P("dp", ("col", "row")),
        P(("col", "row")),
        P(("col", "row")),
        P(("col", "dp"), "row"),
        P(("row", "col")),
        P(("col", "dp"), "row"),
        P(("row", "col")),
        P(("row", "dp"), "col"),
        P(("row", "dp"), "col"),
        P(("col", "row")),
    )
    return jax.shard_map(
        partial(on_device, mesh.shape["dp"]), mesh=mesh, in_specs=in_specs, out_specs=out_specs, check_vma=False
    )
```
